32 devices in a mesh: lemma: 8 (over y, x, core), grp: 4 (over z).
Axes of the slice: x: 2, y: 2, z: 4, core: 2. Of those that a mesh axis runs over, the one named last changes fastest.
Arguments:
- hidden: bfloat16 [64, 64, 1536], P(('lemma', 'grp')), may hold values from -6 to 6
- gain: float32 [1536], replicated, may hold values from 0.3 to 2.1
- weight: bfloat16 [1536, 128], P('grp'), may hold values from -0.15625 to 0.15625
- lemma_emb: bfloat16 [128, 32, 128], P('lemma'), may hold values from -6 to 6
- lemma_len: int32 [128], replicated, may hold values from 8 to 32
- query_len: int32 [64], replicated, may hold values from 16 to 64
- positive: int32 [64], replicated, may hold values from 0 to 127
Outputs:
- loss: float32 [64], P(('lemma', 'grp'))
- hidden_grad: bfloat16 [64, 64, 1536], P(('lemma', 'grp'))
- weight_grad: float32 [1536, 128], P('grp')
- gain_grad: float32 [1536], P('grp')
The draws below stay inside these ranges and needn't reach their ends.
All inputs are finite; a program needn't handle non-finite values.
Results may differ from the reference program's by a relative error of at most 0.03.
Values may be sent and summed in bfloat16 or wider, within the bound.
A program may use at most 64 MiB of HBM per device.

```python
import math
import jax
import jax.numpy as jnp
from jax import lax

D = 1536
P_SIZE = 128
QTOK = 64
LTOK = 32
SDEV = 2
STATES = 64
LEMMAS = 128


def draw_gain(key, part):
    ramp = 0.5 + jnp.arange(D, dtype=jnp.float32) / D
    noise = jax.random.uniform(key, (D,), jnp.float32, 0.8, 1.2)
    return ramp * noise


def draw_lemma_len(key, part):
    values = jax.random.randint(jax.random.fold_in(key, 11), (LEMMAS,), LTOK // 4, LTOK + 1)
    return values.at[0].set(LTOK)


def draw_query_len(key, part):
    values = jax.random.randint(jax.random.fold_in(key, 23), (STATES,), QTOK // 4, QTOK + 1)
    return values.at[0].set(QTOK)


def plant(array, stream_key, smallest, top_value):
    longest = array.shape.index(max(array.shape))
    spots = []
    for shift in (0, 1):
        where = [jax.random.randint(jax.random.fold_in(stream_key, axis), (), 0, length) for axis, length in enumerate(array.shape)]
        where[longest] = (where[longest] + shift) % array.shape[longest]
        spots.append(tuple(where))
    return array.at[spots[0]].set(smallest).at[spots[1]].set(top_value)


def levels(rng, extent, pieces, smallest, top_value):
    def one(dim, blocks):
        steps = jax.random.uniform(jax.random.fold_in(jax.random.fold_in(rng, 6), dim), (blocks,), jnp.float32, smallest / len(pieces), top_value / len(pieces))
        return jnp.repeat(jnp.exp(steps), extent[dim] // blocks).reshape((-1,) + (1,) * (len(extent) - dim - 1))

    level = one(*pieces[0])
    for cut in pieces[1:]:
        level = level * one(*cut)
    return level


def normal_values(key, extent, width, reach, cuts=(), kind=jnp.bfloat16):
    level = levels(key, extent, cuts, -0.22, 0.18) if cuts else 1.0
    entries = jax.random.normal(key, extent, jnp.float32) * width * level
    return jnp.minimum(jnp.maximum(entries, -reach), reach).astype(kind)


def setup_inputs(seed: int = 0) -> dict:
    arg_keys = jax.random.split(jax.random.key(seed), 8)
    return {
        "hidden": normal_values(arg_keys[0], (STATES, QTOK, D), 1.0, 6.0, ((0, 32),)),
        "gain": draw_gain(jax.random.fold_in(arg_keys[7], 71), 0),
        "weight": normal_values(arg_keys[2], (D, P_SIZE), D ** -0.5, 0.15625, ((0, 4),)),
        "lemma_emb": normal_values(arg_keys[3], (LEMMAS, LTOK, P_SIZE), 1.0, 6.0, ((0, 8),)),
        "lemma_len": draw_lemma_len(jax.random.fold_in(arg_keys[7], 71), 0),
        "query_len": draw_query_len(jax.random.fold_in(arg_keys[7], 71), 0),
        "positive": plant(jax.random.randint(arg_keys[6], (STATES,), 0, LEMMAS), jax.random.fold_in(arg_keys[6], 1), 0, LEMMAS - 1).astype(jnp.int32),
    }


token_temp = 0.05
state_temp = 0.05
loss_scale = 1024.0
grad_limit = 400.0
norm_eps = 1e-06

def contract_last(left, right):
    return lax.dot_general(left, right, (((1,), (1,)), ((), ())), preferred_element_type=jnp.float32)

def unit_rows(values):
    scale_rows = lax.rsqrt(lax.optimization_barrier(jnp.mean(values * values, axis=-1, keepdims=True)) + norm_eps)
    return values * scale_rows / math.sqrt(values.shape[-1])

def reference(hidden, gain, weight, lemma_emb, lemma_len, query_len, positive):
    in_float = hidden.reshape(-1, D).astype(jnp.float32)
    inv_rms = lax.rsqrt(lax.optimization_barrier(jnp.mean(in_float * in_float, axis=1, keepdims=True)) + norm_eps)
    normed = in_float * inv_rms
    scaled = (normed * gain[None, :]).astype(jnp.bfloat16)
    projected = jnp.dot(scaled, weight, preferred_element_type=jnp.float32)
    proj_scale = lax.rsqrt(lax.optimization_barrier(jnp.mean(projected * projected, axis=1, keepdims=True)) + norm_eps) / math.sqrt(P_SIZE)
    query_unit = (projected * proj_scale).astype(jnp.bfloat16)
    lemma_unit = unit_rows(lemma_emb.astype(jnp.float32).reshape(-1, P_SIZE)).astype(jnp.bfloat16)
    lemma_live = (jnp.arange(LTOK)[None, :] < lemma_len[:, None]).astype(jnp.float32).reshape(-1)
    query_live = (jnp.arange(QTOK)[None, :] < query_len[:, None]).astype(jnp.float32)
    lemma_ids = jnp.arange(LEMMAS)
    row_count = SDEV * QTOK

    def one_block(items):
        queries, live_rows, lengths, targets = items
        lengths_f = lengths.astype(jnp.float32)
        scores = contract_last(queries, lemma_unit)
        exp_terms = jnp.exp(scores / token_temp) * lemma_live[None, :]
        per_lemma = lax.optimization_barrier(jnp.sum(exp_terms.reshape(row_count, LEMMAS, LTOK), axis=2))
        tok_lse = token_temp * jnp.log(per_lemma)
        similarity = lax.optimization_barrier(jnp.sum(tok_lse.reshape(SDEV, QTOK, LEMMAS) * live_rows[:, :, None], axis=1)) / lengths_f[:, None]
        powers = jnp.exp(similarity / state_temp)
        partition = lax.optimization_barrier(jnp.sum(powers, axis=1))
        is_positive = (lemma_ids[None, :] == targets[:, None]).astype(jnp.float32)
        pos_score = lax.optimization_barrier(jnp.sum(similarity * is_positive, axis=1))
        loss = jnp.log(partition) - pos_score / state_temp
        grad_sim = loss_scale * (powers / partition[:, None] - is_positive) / state_temp
        tok_grad = (grad_sim[:, None, :] * live_rows[:, :, None] / lengths_f[:, None, None]).reshape(row_count, LEMMAS)
        weights = exp_terms.reshape(row_count, LEMMAS, LTOK) / per_lemma[:, :, None]
        coef = (weights * tok_grad[:, :, None]).reshape(row_count, LEMMAS * LTOK).astype(jnp.bfloat16)
        unit_grad = jnp.dot(coef, lemma_unit, preferred_element_type=jnp.float32)
        return (loss, unit_grad)
    blocks = STATES // SDEV
    loss, unit_grad = lax.map(one_block, (query_unit.reshape(blocks, row_count, P_SIZE), query_live.reshape(blocks, SDEV, QTOK), query_len.reshape(blocks, SDEV), positive.reshape(blocks, SDEV)))
    loss = loss.reshape(STATES)
    unit_grad = unit_grad.reshape(-1, P_SIZE)
    proj_grad = proj_scale * unit_grad - projected * proj_scale ** 3 * lax.optimization_barrier(jnp.sum(projected * unit_grad, axis=1, keepdims=True))
    proj_grad_b = proj_grad.astype(jnp.bfloat16)
    scaled_grad = contract_last(proj_grad_b, weight)
    normed_grad = scaled_grad * gain[None, :]
    input_grad = inv_rms * normed_grad - in_float * inv_rms ** 3 * lax.optimization_barrier(jnp.sum(in_float * normed_grad, axis=1, keepdims=True)) / D
    hidden_grad = input_grad.astype(jnp.bfloat16).reshape(STATES, QTOK, D)
    weight_raw = lax.dot_general(scaled, proj_grad_b, (((0,), (0,)), ((), ())), preferred_element_type=jnp.float32)
    gain_raw = lax.optimization_barrier(jnp.sum(scaled_grad * normed, axis=0))
    grad_norm = jnp.sqrt(jnp.sum(weight_raw * weight_raw) + jnp.sum(gain_raw * gain_raw) + norm_eps)
    factor = jnp.minimum(1.0, grad_limit / grad_norm)
    return (loss, hidden_grad, weight_raw * factor, gain_raw * factor)
```

```python
import functools
import math

import jax
import jax.numpy as jnp
from jax import lax
from jax.experimental import pallas as pl
from jax.experimental.pallas import tpu as pltpu
from jax.sharding import PartitionSpec as P

token_temp = 0.05
state_temp = 0.05
loss_scale = 1024.0
grad_limit = 400.0
norm_eps = 1e-06


def contract_last(left, right):
    return lax.dot_general(
        left, right, (((1,), (1,)), ((), ())), preferred_element_type=jnp.float32
    )


def unit_rows(values):
    scale_rows = lax.rsqrt(jnp.mean(values * values, axis=-1, keepdims=True) + norm_eps)
    return values * scale_rows / math.sqrt(values.shape[-1])


def lemma_terms(queries, keys, key_live, lemma_count, lemma_tok):
    scores = contract_last(queries, keys)
    exp_terms = jnp.exp(scores / token_temp) * key_live[None, :]
    per_lemma = jnp.sum(exp_terms.reshape(queries.shape[0], lemma_count, lemma_tok), axis=2)
    return (exp_terms, per_lemma)


def token_grads(queries, grads, keys, key_live, lemma_count, lemma_tok):
    exp_terms, per_lemma = lemma_terms(queries, keys, key_live, lemma_count, lemma_tok)
    rows = queries.shape[0]
    weights = exp_terms.reshape(rows, lemma_count, lemma_tok) / per_lemma[:, :, None]
    coef = (weights * grads[:, :, None]).reshape(rows, lemma_count * lemma_tok).astype(jnp.bfloat16)
    return jnp.dot(coef, keys, preferred_element_type=jnp.float32)


def state_loss(tok_lse, live_rows, lengths_f, targets, lemma_ids):
    states = live_rows.shape[0]
    similarity = (
        jnp.sum(tok_lse.reshape(states, live_rows.shape[1], -1) * live_rows[:, :, None], axis=1)
        / lengths_f[:, None]
    )
    powers = jnp.exp(similarity / state_temp)
    is_positive = (lemma_ids[None, :] == targets[:, None]).astype(jnp.float32)
    return (similarity, powers, is_positive)


def body(hidden, gain, weight, lemma_emb, lemma_len, query_len, positive):
    states_dev, query_tok, width = hidden.shape
    proj_width = weight.shape[1]
    lemma_dev, lemma_tok = (lemma_emb.shape[0], lemma_emb.shape[1])
    lemma_axis = lax.axis_size("lemma")
    group_axis = lax.axis_size("grp")
    lemma_idx = lax.axis_index("lemma")
    group_idx = lax.axis_index("grp")
    own_rows = states_dev * query_tok
    lemmas_all = lemma_dev * lemma_axis
    in_float = hidden.reshape(own_rows, width).astype(jnp.float32)
    inv_rms = lax.rsqrt(jnp.mean(in_float * in_float, axis=1, keepdims=True) + norm_eps)
    normed = in_float * inv_rms
    scaled = (normed * gain[None, :]).astype(jnp.bfloat16)
    projected = jnp.dot(
        scaled,
        lax.all_gather(weight, "grp", axis=0, tiled=True),
        preferred_element_type=jnp.float32,
    )
    proj_scale = lax.rsqrt(
        jnp.mean(projected * projected, axis=1, keepdims=True) + norm_eps
    ) / math.sqrt(proj_width)
    query_unit = (projected * proj_scale).astype(jnp.bfloat16)
    lemma_unit = unit_rows(lemma_emb.astype(jnp.float32).reshape(-1, proj_width)).astype(
        jnp.bfloat16
    )
    all_live = (jnp.arange(lemma_tok)[None, :] < lemma_len[:, None]).astype(jnp.float32)
    block_start = (lemma_idx * group_axis + group_idx) * states_dev
    all_keys = lax.all_gather(lemma_unit, "lemma", axis=0, tiled=True)
    block_count = 8
    block_lemmas = lemmas_all // block_count
    key_blocks = all_keys.reshape(block_count, block_lemmas * lemma_tok, proj_width)
    live_blocks = all_live.reshape(block_count, block_lemmas * lemma_tok)
    own_len = lax.dynamic_slice_in_dim(query_len, block_start, states_dev)
    own_pos = lax.dynamic_slice_in_dim(positive, block_start, states_dev)
    live_rows = (jnp.arange(query_tok)[None, :] < own_len[:, None]).astype(jnp.float32)
    lengths_f = own_len.astype(jnp.float32)

    def block_lse(items):
        keys, key_live = items
        exp_terms, per_lemma = lemma_terms(query_unit, keys, key_live, block_lemmas, lemma_tok)
        return token_temp * jnp.log(per_lemma)

    tok_lse = lax.map(block_lse, (key_blocks, live_blocks))
    tok_lse = jnp.moveaxis(tok_lse, 0, 1).reshape(own_rows, lemmas_all)
    similarity, powers, is_positive = state_loss(
        tok_lse, live_rows, lengths_f, own_pos, jnp.arange(lemmas_all)
    )
    partition = jnp.sum(powers, axis=1)
    pos_score = jnp.sum(similarity * is_positive, axis=1)
    loss = jnp.log(partition) - pos_score / state_temp
    grad_sim = loss_scale * (powers / partition[:, None] - is_positive) / state_temp
    tok_grad = (grad_sim[:, None, :] * live_rows[:, :, None] / lengths_f[:, None, None]).reshape(
        own_rows, block_count, block_lemmas
    )
    grad_blocks = jnp.moveaxis(tok_grad, 1, 0)

    def add_block(acc, items):
        keys, key_live, grads = items
        return (acc + token_grads(query_unit, grads, keys, key_live, block_lemmas, lemma_tok), None)

    unit_grad, unused = lax.scan(
        add_block,
        jnp.zeros((own_rows, proj_width), jnp.float32),
        (key_blocks, live_blocks, grad_blocks),
    )
    proj_grad = proj_scale * unit_grad - projected * proj_scale**3 * jnp.sum(
        projected * unit_grad, axis=1, keepdims=True
    )
    proj_grad_b = proj_grad.astype(jnp.bfloat16)
    scaled_grad = contract_last(proj_grad_b, lax.all_gather(weight, "grp", axis=0, tiled=True))
    normed_grad = scaled_grad * gain[None, :]
    input_grad = (
        inv_rms * normed_grad
        - in_float * inv_rms**3 * jnp.sum(in_float * normed_grad, axis=1, keepdims=True) / width
    )
    hidden_grad = input_grad.astype(jnp.bfloat16).reshape(states_dev, query_tok, width)
    weight_part = lax.dot_general(
        scaled, proj_grad_b, (((0,), (0,)), ((), ())), preferred_element_type=jnp.float32
    )
    gain_part = jnp.sum(scaled_grad * normed, axis=0)
    weight_sum, gain_sum = (
        lax.psum(weight_part.astype(jnp.bfloat16), "lemma").astype(jnp.float32),
        lax.psum(gain_part.astype(jnp.bfloat16), "lemma").astype(jnp.float32),
    )
    weight_sum, gain_sum = (
        lax.psum_scatter(
            weight_sum.astype(jnp.bfloat16), "grp", scatter_dimension=0, tiled=True
        ).astype(jnp.float32),
        lax.psum_scatter(
            gain_sum.astype(jnp.bfloat16), "grp", scatter_dimension=0, tiled=True
        ).astype(jnp.float32),
    )
    squares = jnp.sum(weight_sum * weight_sum) + jnp.sum(gain_sum * gain_sum)
    total_squares = lax.psum(squares, "grp")
    factor = jnp.minimum(1.0, grad_limit / jnp.sqrt(total_squares + norm_eps))
    return (loss, hidden_grad, weight_sum * factor, gain_sum * factor)


NT = (((1,), (1,)), ((), ()))
MESH = pl.DeviceIdType.MESH


def fused_kernel(
    lemma_axis, group_axis, lemma_dev, lemma_tok, states_dev, query_tok,
    hidden_ref, gain_ref, weight_ref, emb_ref, len_ref, qlen_ref, pos_ref,
    loss_ref, hgrad_ref, wgrad_ref, ggrad_ref,
    hid, emb, hout, w_all, keys, live, powers_b, scaled_b, scaled_t,
    part, pair_in, half, chip_in, quarter, grp_in, raw, sq,
    local_sem, w_send, w_recv, wf_send, wf_recv, k_send, k_recv, kf_send, kf_recv,
    p_sem, c_send, c_recv, g_send, g_recv, a_send, a_recv, s_send, s_recv,
):
    chips = lemma_axis // 2
    me, grp = lax.axis_index("lemma"), lax.axis_index("grp")
    chip, core = me // 2, lax.rem(me, 2)
    pair = chip * 2 + (1 - core)
    rows, width = hid.shape
    proj_width = weight_ref.shape[1]
    wrows = weight_ref.shape[0]
    hrows = wrows // 2
    block_tok = lemma_dev * lemma_tok
    lemmas_all = lemma_dev * lemma_axis

    def chip_peer(step):
        return lax.rem(chip + step, chips) * 2 + core

    def chip_from(step):
        return lax.rem(chip + chips - step, chips) * 2 + core

    def grp_peer(step):
        return lax.rem(grp + step, group_axis)

    def grp_from(step):
        return lax.rem(grp + group_axis - step, group_axis)

    def remote(src, dst, send_sem, recv_sem, to_lemma, to_grp):
        return pltpu.make_async_remote_copy(
            src_ref=src, dst_ref=dst, send_sem=send_sem, recv_sem=recv_sem,
            device_id=(to_lemma, to_grp), device_id_type=MESH,
        )

    emb_copy = pltpu.make_async_copy(emb_ref, emb, local_sem.at[0])
    hid_copy = pltpu.make_async_copy(hidden_ref, hid, local_sem.at[1])
    w_copy = pltpu.make_async_copy(weight_ref, w_all.at[grp], local_sem.at[2])
    emb_copy.start()
    w_copy.start()
    hid_copy.start()

    barrier = pltpu.get_barrier_semaphore()
    for step in range(1, lemma_axis):
        pl.semaphore_signal(
            barrier, inc=1, device_id=(lax.rem(me + step, lemma_axis), grp), device_id_type=MESH
        )
    for step in range(1, group_axis):
        pl.semaphore_signal(barrier, inc=1, device_id=(me, grp_peer(step)), device_id_type=MESH)

    emb_copy.wait()
    tokens = emb[...].astype(jnp.float32)
    token_scale = lax.rsqrt(
        jnp.mean(tokens * tokens, axis=1, keepdims=True) + norm_eps
    ) / math.sqrt(proj_width)
    keys[me] = (tokens * token_scale).astype(jnp.bfloat16)
    w_copy.wait()
    pl.semaphore_wait(barrier, lemma_axis - 1 + group_axis - 1)

    my_half = pl.ds(pl.multiple_of(core * hrows, hrows), hrows)
    w_out = []
    for step in range(1, group_axis):
        src = w_all.at[grp, my_half]
        copy = remote(src, src, w_send.at[step], w_recv.at[step], me, grp_peer(step))
        copy.start()
        w_out.append(copy)
    k_out = []
    for step in range(1, chips):
        copy = remote(
            keys.at[me], keys.at[me], k_send.at[step], k_recv.at[step], chip_peer(step), grp
        )
        copy.start()
        k_out.append(copy)
    kf_out = [remote(keys.at[me], keys.at[me], kf_send.at[0], kf_recv.at[0], pair, grp)]
    kf_out[0].start()

    token_row = lax.broadcasted_iota(jnp.int32, (block_tok, lemmas_all), 0)
    lemma_col = lax.broadcasted_iota(jnp.int32, (block_tok, lemmas_all), 1)
    alive = lax.rem(token_row, lemma_tok) < len_ref[...]
    for block in range(lemma_axis):
        member = lemma_col == token_row // lemma_tok + block * lemma_dev
        live[block] = jnp.where(member & alive, 1.0, 0.0).astype(jnp.bfloat16)

    hid_copy.wait()
    in_float = hid[...].astype(jnp.float32)
    inv_rms = lax.rsqrt(jnp.mean(in_float * in_float, axis=1, keepdims=True) + norm_eps)
    scaled = (in_float * inv_rms * gain_ref[...]).astype(jnp.bfloat16)
    scaled_b[...] = scaled
    scaled_t[...] = scaled.T

    wf_out = []
    for step in range(1, group_axis):
        dst = w_all.at[grp_from(step), my_half]
        remote(dst, dst, w_send.at[step], w_recv.at[step], me, grp_peer(step)).wait_recv()
        copy = remote(dst, dst, wf_send.at[step], wf_recv.at[step], pair, grp)
        copy.start()
        wf_out.append(copy)
    for step in range(1, chips):
        dst = keys.at[chip_from(step)]
        remote(dst, dst, k_send.at[step], k_recv.at[step], chip_peer(step), grp).wait_recv()
        copy = remote(dst, dst, kf_send.at[step], kf_recv.at[step], pair, grp)
        copy.start()
        kf_out.append(copy)
    other_half = pl.ds(pl.multiple_of((1 - core) * hrows, hrows), hrows)
    for step in range(1, group_axis):
        dst = w_all.at[grp_from(step), other_half]
        remote(dst, dst, wf_send.at[step], wf_recv.at[step], pair, grp).wait_recv()

    weight = w_all[...].reshape(width, proj_width)
    projected = jnp.dot(scaled_b[...], weight, preferred_element_type=jnp.float32)
    proj_scale = lax.rsqrt(
        jnp.mean(projected * projected, axis=1, keepdims=True) + norm_eps
    ) / math.sqrt(proj_width)
    query_unit = (projected * proj_scale).astype(jnp.bfloat16)

    def first_pass(block, total):
        scores = lax.dot_general(
            query_unit, keys[block], NT, preferred_element_type=jnp.float32
        )
        exp_terms = jnp.exp(scores * (1.0 / token_temp)).astype(jnp.bfloat16)
        powers_b[block] = exp_terms
        return total + jnp.dot(exp_terms, live[block], preferred_element_type=jnp.float32)

    total = first_pass(me, jnp.zeros((rows, lemmas_all), jnp.float32))
    for step in range(1, chips):
        total = first_pass(chip_from(step), total)
    for step in range(chips):
        block = lax.rem(chip + chips - step, chips) * 2 + (1 - core)
        dst = keys.at[block]
        remote(dst, dst, kf_send.at[step], kf_recv.at[step], pair, grp).wait_recv()
        total = first_pass(block, total)

    tok_lse = token_temp * jnp.log(total)
    first_state = (me * group_axis + grp) * states_dev
    ratios = []
    for state in range(states_dev):
        length = qlen_ref[first_state + state]
        target = pos_ref[first_state + state]
        length_f = jnp.full((1, lemmas_all), length, jnp.int32).astype(jnp.float32)
        span = slice(state * query_tok, (state + 1) * query_tok)
        row_ids = lax.broadcasted_iota(jnp.int32, (query_tok, lemmas_all), 0)
        live_rows = jnp.where(row_ids < length, 1.0, 0.0)
        similarity = jnp.sum(tok_lse[span] * live_rows, axis=0, keepdims=True) / length_f
        powers = jnp.exp(similarity / state_temp)
        lemma_ids = lax.broadcasted_iota(jnp.int32, (1, lemmas_all), 1)
        is_positive = jnp.where(lemma_ids == target, 1.0, 0.0)
        partition = jnp.sum(powers, axis=1, keepdims=True)
        pos_score = jnp.sum(similarity * is_positive, axis=1, keepdims=True)
        loss = jnp.log(partition) - pos_score / state_temp
        loss_ref[state] = jnp.sum(loss)
        grad_sim = loss_scale * (powers / partition - is_positive) / state_temp
        ratios.append(live_rows * (grad_sim / length_f) / total[span])
    ratio = jnp.concatenate(ratios, axis=0).astype(jnp.bfloat16)

    unit_grad = jnp.zeros((rows, proj_width), jnp.float32)
    for block in range(lemma_axis):
        spread = lax.dot_general(ratio, live[block], NT, preferred_element_type=jnp.float32)
        coef = (powers_b[block].astype(jnp.float32) * spread).astype(jnp.bfloat16)
        unit_grad += jnp.dot(coef, keys[block], preferred_element_type=jnp.float32)
    proj_grad = proj_scale * unit_grad - projected * (
        proj_scale * proj_scale * proj_scale
    ) * jnp.sum(projected * unit_grad, axis=1, keepdims=True)
    proj_grad_b = proj_grad.astype(jnp.bfloat16)

    weight_part = jnp.dot(scaled_t[...], proj_grad_b, preferred_element_type=jnp.float32)
    piece = wrows // lemma_axis
    for group in range(group_axis):
        for owner in range(lemma_axis):
            start = group * wrows + owner * piece
            part[owner % 2, owner // 2, group] = weight_part[start : start + piece].astype(
                jnp.bfloat16
            )
    pair_copy = remote(part.at[1 - core], pair_in, p_sem.at[0], p_sem.at[1], pair, grp)
    pair_copy.start()
    pair_copy.wait()
    half[...] = (part[core].astype(jnp.float32) + pair_in[...].astype(jnp.float32)).astype(
        jnp.bfloat16
    )
    c_out = []
    for step in range(1, chips):
        copy = remote(
            half.at[lax.rem(chip + step, chips)], chip_in.at[step - 1],
            c_send.at[step], c_recv.at[step], chip_peer(step), grp,
        )
        copy.start()
        c_out.append(copy)

    scaled_grad = lax.dot_general(
        proj_grad_b, w_all[...].reshape(width, proj_width), NT, preferred_element_type=jnp.float32
    )
    row_dot = jnp.sum(projected * proj_grad_b.astype(jnp.float32), axis=1, keepdims=True)
    hout[...] = (
        inv_rms * (scaled_grad * gain_ref[...])
        - hid[...].astype(jnp.float32) * (inv_rms * inv_rms * row_dot / width)
    ).astype(jnp.bfloat16)
    hout_copy = pltpu.make_async_copy(hout, hgrad_ref, local_sem.at[3])
    hout_copy.start()

    for copy in c_out:
        copy.wait()
    chip_sum = half[chip].astype(jnp.float32)
    for step in range(1, chips):
        chip_sum += chip_in[step - 1].astype(jnp.float32)
    quarter[...] = chip_sum.astype(jnp.bfloat16)
    g_out = []
    for step in range(1, group_axis):
        copy = remote(
            quarter.at[grp_peer(step)], grp_in.at[step - 1],
            g_send.at[step], g_recv.at[step], me, grp_peer(step),
        )
        copy.start()
        g_out.append(copy)
    for copy in g_out:
        copy.wait()
    grp_sum = quarter[grp].astype(jnp.float32)
    for step in range(1, group_axis):
        grp_sum += grp_in[step - 1].astype(jnp.float32)
    raw[me] = grp_sum.astype(jnp.bfloat16)
    a_out = []
    for step in range(1, lemma_axis):
        copy = remote(
            raw.at[me], raw.at[me], a_send.at[step], a_recv.at[step],
            lax.rem(me + step, lemma_axis), grp,
        )
        copy.start()
        a_out.append(copy)
    for step in range(1, lemma_axis):
        dst = raw.at[lax.rem(me + lemma_axis - step, lemma_axis)]
        remote(dst, dst, a_send.at[step], a_recv.at[step], me, grp_peer(1)).wait_recv()

    weight_raw = raw[...].reshape(wrows, proj_width).astype(jnp.float32)
    ones = jnp.ones((8, proj_width), jnp.float32)
    own_gain = gain_ref[:, pl.ds(pl.multiple_of(grp * wrows, 128), wrows)]
    gain_raw = lax.dot_general(
        ones, w_all[grp].astype(jnp.float32) * weight_raw, NT,
        preferred_element_type=jnp.float32, precision=lax.Precision.HIGHEST,
    )[:1] / own_gain
    squares = jnp.sum(weight_raw * weight_raw) + jnp.sum(gain_raw * gain_raw)
    sq[grp] = jnp.full((8, 128), squares, jnp.float32)
    s_out = []
    for step in range(1, group_axis):
        copy = remote(
            sq.at[grp], sq.at[grp], s_send.at[step], s_recv.at[step], me, grp_peer(step)
        )
        copy.start()
        s_out.append(copy)
    for step in range(1, group_axis):
        dst = sq.at[grp_from(step)]
        remote(dst, dst, s_send.at[step], s_recv.at[step], me, grp_peer(step)).wait_recv()
    squares_all = sq[0, :1, :]
    for group in range(1, group_axis):
        squares_all += sq[group, :1, :]
    factor = jnp.minimum(1.0, grad_limit / jnp.sqrt(squares_all + norm_eps))
    wgrad_ref[...] = weight_raw * factor
    ggrad_ref[...] = gain_raw * factor[:, :1]

    for copy in w_out + k_out + wf_out + kf_out + a_out + s_out:
        copy.wait_send()
    hout_copy.wait()


def fused_body(hidden, gain, weight, lemma_emb, lemma_len, query_len, positive):
    states_dev, query_tok, width = hidden.shape
    wrows, proj_width = weight.shape
    lemma_dev, lemma_tok = lemma_emb.shape[:2]
    lemma_axis, group_axis = lax.axis_size("lemma"), lax.axis_size("grp")
    chips = lemma_axis // 2
    rows, block_tok = states_dev * query_tok, lemma_dev * lemma_tok
    piece = wrows // lemma_axis
    lemmas_all = lemma_dev * lemma_axis
    vmem = pl.BlockSpec(memory_space=pltpu.VMEM)
    smem = pl.BlockSpec(memory_space=pltpu.SMEM)
    hbm = pl.BlockSpec(memory_space=pl.ANY)
    sem = pltpu.SemaphoreType.DMA
    bf16, f32 = jnp.bfloat16, jnp.float32
    outs = pl.pallas_call(
        functools.partial(
            fused_kernel, lemma_axis, group_axis, lemma_dev, lemma_tok, states_dev, query_tok
        ),
        out_shape=(
            jax.ShapeDtypeStruct((states_dev,), f32),
            jax.ShapeDtypeStruct((rows, width), bf16),
            jax.ShapeDtypeStruct((wrows, proj_width), f32),
            jax.ShapeDtypeStruct((1, wrows), f32),
        ),
        in_specs=[hbm, vmem, hbm, hbm, vmem, smem, smem],
        out_specs=(smem, hbm, vmem, vmem),
        scratch_shapes=[
            pltpu.VMEM((rows, width), bf16),
            pltpu.VMEM((block_tok, proj_width), bf16),
            pltpu.VMEM((rows, width), bf16),
            pltpu.VMEM((group_axis, wrows, proj_width), bf16),
            pltpu.VMEM((lemma_axis, block_tok, proj_width), bf16),
            pltpu.VMEM((lemma_axis, block_tok, lemmas_all), bf16),
            pltpu.VMEM((lemma_axis, rows, block_tok), bf16),
            pltpu.VMEM((rows, width), bf16),
            pltpu.VMEM((width, rows), bf16),
            pltpu.VMEM((2, chips, group_axis, piece, proj_width), bf16),
            pltpu.VMEM((chips, group_axis, piece, proj_width), bf16),
            pltpu.VMEM((chips, group_axis, piece, proj_width), bf16),
            pltpu.VMEM((chips - 1, group_axis, piece, proj_width), bf16),
            pltpu.VMEM((group_axis, piece, proj_width), bf16),
            pltpu.VMEM((group_axis - 1, piece, proj_width), bf16),
            pltpu.VMEM((lemma_axis, piece, proj_width), bf16),
            pltpu.VMEM((group_axis, 8, 128), f32),
            sem((4,)),
            sem((group_axis,)), sem((group_axis,)), sem((group_axis,)), sem((group_axis,)),
            sem((chips,)), sem((chips,)), sem((chips,)), sem((chips,)),
            sem((2,)),
            sem((chips,)), sem((chips,)),
            sem((group_axis,)), sem((group_axis,)),
            sem((lemma_axis,)), sem((lemma_axis,)),
            sem((group_axis,)), sem((group_axis,)),
        ],
        compiler_params=pltpu.CompilerParams(
            collective_id=0, has_side_effects=True, vmem_limit_bytes=48 * 1024 * 1024
        ),
        cost_estimate=pl.CostEstimate(
            flops=2 * rows * proj_width * (3 * width + 4 * block_tok * lemma_axis),
            bytes_accessed=4 * rows * width * 2,
            transcendentals=rows * block_tok * lemma_axis,
        ),
    )(
        hidden.reshape(rows, width), gain.reshape(1, width), weight,
        lemma_emb.reshape(block_tok, proj_width), lemma_len.reshape(1, lemmas_all),
        query_len, positive,
    )
    loss, hidden_grad, weight_grad, gain_grad = outs
    return (loss, hidden_grad.reshape(hidden.shape), weight_grad, gain_grad.reshape(wrows))


def solution(mesh):
    in_specs = (
        P(("lemma", "grp"), None, None),
        P(),
        P("grp", None),
        P("lemma", None, None),
        P(),
        P(),
        P(),
    )
    out_specs = (P(("lemma", "grp")), P(("lemma", "grp"), None, None), P("grp", None), P("grp"))

    def run(hidden, gain, weight, *rest):
        rows = weight.shape[0] // mesh.shape["grp"]
        tiled = rows % (16 * mesh.shape["lemma"]) == 0 and rows % 128 == 0
        chosen = fused_body if tiled else body
        return jax.shard_map(
            chosen, mesh=mesh, in_specs=in_specs, out_specs=out_specs, check_vma=False
        )(hidden, gain, weight, *rest)

    return run
```

```python
import functools
import math

import jax
import jax.numpy as jnp
from jax import lax
from jax.experimental import pallas as pl
from jax.experimental.pallas import tpu as pltpu
from jax.sharding import PartitionSpec as P

token_temp = 0.05
state_temp = 0.05
loss_scale = 1024.0
grad_limit = 400.0
norm_eps = 1e-06


def contract_last(left, right):
    return lax.dot_general(
        left, right, (((1,), (1,)), ((), ())), preferred_element_type=jnp.float32
    )


def unit_rows(values):
    scale_rows = lax.rsqrt(jnp.mean(values * values, axis=-1, keepdims=True) + norm_eps)
    return values * scale_rows / math.sqrt(values.shape[-1])


def lemma_terms(queries, keys, key_live, lemma_count, lemma_tok):
    scores = contract_last(queries, keys)
    exp_terms = jnp.exp(scores / token_temp) * key_live[None, :]
    per_lemma = jnp.sum(exp_terms.reshape(queries.shape[0], lemma_count, lemma_tok), axis=2)
    return (exp_terms, per_lemma)


def token_grads(queries, grads, keys, key_live, lemma_count, lemma_tok):
    exp_terms, per_lemma = lemma_terms(queries, keys, key_live, lemma_count, lemma_tok)
    rows = queries.shape[0]
    weights = exp_terms.reshape(rows, lemma_count, lemma_tok) / per_lemma[:, :, None]
    coef = (weights * grads[:, :, None]).reshape(rows, lemma_count * lemma_tok).astype(jnp.bfloat16)
    return jnp.dot(coef, keys, preferred_element_type=jnp.float32)


def state_loss(tok_lse, live_rows, lengths_f, targets, lemma_ids):
    states = live_rows.shape[0]
    similarity = (
        jnp.sum(tok_lse.reshape(states, live_rows.shape[1], -1) * live_rows[:, :, None], axis=1)
        / lengths_f[:, None]
    )
    powers = jnp.exp(similarity / state_temp)
    is_positive = (lemma_ids[None, :] == targets[:, None]).astype(jnp.float32)
    return (similarity, powers, is_positive)


def body(hidden, gain, weight, lemma_emb, lemma_len, query_len, positive):
    states_dev, query_tok, width = hidden.shape
    proj_width = weight.shape[1]
    lemma_dev, lemma_tok = (lemma_emb.shape[0], lemma_emb.shape[1])
    lemma_axis = lax.axis_size("lemma")
    group_axis = lax.axis_size("grp")
    lemma_idx = lax.axis_index("lemma")
    group_idx = lax.axis_index("grp")
    own_rows = states_dev * query_tok
    lemmas_all = lemma_dev * lemma_axis
    in_float = hidden.reshape(own_rows, width).astype(jnp.float32)
    inv_rms = lax.rsqrt(jnp.mean(in_float * in_float, axis=1, keepdims=True) + norm_eps)
    normed = in_float * inv_rms
    scaled = (normed * gain[None, :]).astype(jnp.bfloat16)
    projected = jnp.dot(
        scaled,
        lax.all_gather(weight, "grp", axis=0, tiled=True),
        preferred_element_type=jnp.float32,
    )
    proj_scale = lax.rsqrt(
        jnp.mean(projected * projected, axis=1, keepdims=True) + norm_eps
    ) / math.sqrt(proj_width)
    query_unit = (projected * proj_scale).astype(jnp.bfloat16)
    lemma_unit = unit_rows(lemma_emb.astype(jnp.float32).reshape(-1, proj_width)).astype(
        jnp.bfloat16
    )
    all_live = (jnp.arange(lemma_tok)[None, :] < lemma_len[:, None]).astype(jnp.float32)
    block_start = (lemma_idx * group_axis + group_idx) * states_dev
    all_keys = lax.all_gather(lemma_unit, "lemma", axis=0, tiled=True)
    block_count = 8
    block_lemmas = lemmas_all // block_count
    key_blocks = all_keys.reshape(block_count, block_lemmas * lemma_tok, proj_width)
    live_blocks = all_live.reshape(block_count, block_lemmas * lemma_tok)
    own_len = lax.dynamic_slice_in_dim(query_len, block_start, states_dev)
    own_pos = lax.dynamic_slice_in_dim(positive, block_start, states_dev)
    live_rows = (jnp.arange(query_tok)[None, :] < own_len[:, None]).astype(jnp.float32)
    lengths_f = own_len.astype(jnp.float32)

    def block_lse(items):
        keys, key_live = items
        exp_terms, per_lemma = lemma_terms(query_unit, keys, key_live, block_lemmas, lemma_tok)
        return token_temp * jnp.log(per_lemma)

    tok_lse = lax.map(block_lse, (key_blocks, live_blocks))
    tok_lse = jnp.moveaxis(tok_lse, 0, 1).reshape(own_rows, lemmas_all)
    similarity, powers, is_positive = state_loss(
        tok_lse, live_rows, lengths_f, own_pos, jnp.arange(lemmas_all)
    )
    partition = jnp.sum(powers, axis=1)
    pos_score = jnp.sum(similarity * is_positive, axis=1)
    loss = jnp.log(partition) - pos_score / state_temp
    grad_sim = loss_scale * (powers / partition[:, None] - is_positive) / state_temp
    tok_grad = (grad_sim[:, None, :] * live_rows[:, :, None] / lengths_f[:, None, None]).reshape(
        own_rows, block_count, block_lemmas
    )
    grad_blocks = jnp.moveaxis(tok_grad, 1, 0)

    def add_block(acc, items):
        keys, key_live, grads = items
        return (acc + token_grads(query_unit, grads, keys, key_live, block_lemmas, lemma_tok), None)

    unit_grad, unused = lax.scan(
        add_block,
        jnp.zeros((own_rows, proj_width), jnp.float32),
        (key_blocks, live_blocks, grad_blocks),
    )
    proj_grad = proj_scale * unit_grad - projected * proj_scale**3 * jnp.sum(
        projected * unit_grad, axis=1, keepdims=True
    )
    proj_grad_b = proj_grad.astype(jnp.bfloat16)
    scaled_grad = contract_last(proj_grad_b, lax.all_gather(weight, "grp", axis=0, tiled=True))
    normed_grad = scaled_grad * gain[None, :]
    input_grad = (
        inv_rms * normed_grad
        - in_float * inv_rms**3 * jnp.sum(in_float * normed_grad, axis=1, keepdims=True) / width
    )
    hidden_grad = input_grad.astype(jnp.bfloat16).reshape(states_dev, query_tok, width)
    weight_part = lax.dot_general(
        scaled, proj_grad_b, (((0,), (0,)), ((), ())), preferred_element_type=jnp.float32
    )
    gain_part = jnp.sum(scaled_grad * normed, axis=0)
    weight_sum, gain_sum = (
        lax.psum(weight_part.astype(jnp.bfloat16), "lemma").astype(jnp.float32),
        lax.psum(gain_part.astype(jnp.bfloat16), "lemma").astype(jnp.float32),
    )
    weight_sum, gain_sum = (
        lax.psum_scatter(
            weight_sum.astype(jnp.bfloat16), "grp", scatter_dimension=0, tiled=True
        ).astype(jnp.float32),
        lax.psum_scatter(
            gain_sum.astype(jnp.bfloat16), "grp", scatter_dimension=0, tiled=True
        ).astype(jnp.float32),
    )
    squares = jnp.sum(weight_sum * weight_sum) + jnp.sum(gain_sum * gain_sum)
    total_squares = lax.psum(squares, "grp")
    factor = jnp.minimum(1.0, grad_limit / jnp.sqrt(total_squares + norm_eps))
    return (loss, hidden_grad, weight_sum * factor, gain_sum * factor)


NT = (((1,), (1,)), ((), ()))
MESH = pl.DeviceIdType.MESH


def fused_kernel(
    lemma_axis, group_axis, lemma_dev, lemma_tok, states_dev, query_tok,
    hidden_ref, gain_ref, weight_ref, emb_ref, len_ref, qlen_ref, pos_ref,
    loss_ref, hgrad_ref, wgrad_ref, ggrad_ref,
    hid, emb, hout, w_all, keys, live, powers_b, scaled_b, scaled_t,
    part, pair_in, half, chip_in, quarter, grp_in, raw, sq,
    local_sem, w_send, w_recv, wf_send, wf_recv, k_send, k_recv, kf_send, kf_recv,
    p_sem, c_send, c_recv, g_send, g_recv, a_send, a_recv, s_send, s_recv,
):
    chips = lemma_axis // 2
    me, grp = lax.axis_index("lemma"), lax.axis_index("grp")
    chip, core = me // 2, lax.rem(me, 2)
    pair = chip * 2 + (1 - core)
    rows, width = hid.shape
    gain_row = gain_ref[...].reshape(1, width)
    proj_width = weight_ref.shape[1]
    wrows = weight_ref.shape[0]
    hrows = wrows // 2
    block_tok = lemma_dev * lemma_tok
    lemmas_all = lemma_dev * lemma_axis

    def chip_peer(step):
        return lax.rem(chip + step, chips) * 2 + core

    def chip_from(step):
        return lax.rem(chip + chips - step, chips) * 2 + core

    def grp_peer(step):
        return lax.rem(grp + step, group_axis)

    def grp_from(step):
        return lax.rem(grp + group_axis - step, group_axis)

    def remote(src, dst, send_sem, recv_sem, to_lemma, to_grp):
        return pltpu.make_async_remote_copy(
            src_ref=src, dst_ref=dst, send_sem=send_sem, recv_sem=recv_sem,
            device_id=(to_lemma, to_grp), device_id_type=MESH,
        )

    emb_copy = pltpu.make_async_copy(emb_ref, emb, local_sem.at[0])
    hid_copy = pltpu.make_async_copy(hidden_ref, hid, local_sem.at[1])
    w_copy = pltpu.make_async_copy(weight_ref, w_all.at[grp], local_sem.at[2])
    emb_copy.start()
    w_copy.start()
    hid_copy.start()

    barrier = pltpu.get_barrier_semaphore()
    for step in range(1, lemma_axis):
        pl.semaphore_signal(
            barrier, inc=1, device_id=(lax.rem(me + step, lemma_axis), grp), device_id_type=MESH
        )
    for step in range(1, group_axis):
        pl.semaphore_signal(barrier, inc=1, device_id=(me, grp_peer(step)), device_id_type=MESH)

    emb_copy.wait()
    tokens = emb[...].astype(jnp.float32)
    token_scale = lax.rsqrt(
        jnp.mean(tokens * tokens, axis=1, keepdims=True) + norm_eps
    ) / math.sqrt(proj_width)
    keys[me] = (tokens * token_scale).astype(jnp.bfloat16)
    w_copy.wait()
    pl.semaphore_wait(barrier, lemma_axis - 1 + group_axis - 1)

    my_half = pl.ds(pl.multiple_of(core * hrows, hrows), hrows)
    w_out = []
    for step in range(1, group_axis):
        src = w_all.at[grp, my_half]
        copy = remote(src, src, w_send.at[step], w_recv.at[step], me, grp_peer(step))
        copy.start()
        w_out.append(copy)
    k_out = []
    for step in range(1, chips):
        copy = remote(
            keys.at[me], keys.at[me], k_send.at[step], k_recv.at[step], chip_peer(step), grp
        )
        copy.start()
        k_out.append(copy)
    kf_out = [remote(keys.at[me], keys.at[me], kf_send.at[0], kf_recv.at[0], pair, grp)]
    kf_out[0].start()

    token_of = lax.broadcasted_iota(
        jnp.int32, (block_tok, lemmas_all), 0
    ) - lemma_tok * lax.broadcasted_iota(jnp.int32, (block_tok, lemmas_all), 1)
    lengths = jnp.minimum(len_ref[...].reshape(1, lemmas_all), lemma_tok)
    for block in range(lemma_axis):
        first = -block * block_tok
        member = (token_of >= first) & (token_of < lengths + first)
        live[block] = jnp.where(member, 1.0, 0.0).astype(jnp.bfloat16)

    hid_copy.wait()
    in_float = hid[...].astype(jnp.float32)
    inv_rms = lax.rsqrt(jnp.mean(in_float * in_float, axis=1, keepdims=True) + norm_eps)
    scaled = (in_float * inv_rms * gain_row).astype(jnp.bfloat16)
    scaled_b[...] = scaled
    scaled_t[...] = scaled.T

    wf_out = []
    for step in range(1, group_axis):
        dst = w_all.at[grp_from(step), my_half]
        remote(dst, dst, w_send.at[step], w_recv.at[step], me, grp_peer(step)).wait_recv()
        copy = remote(dst, dst, wf_send.at[step], wf_recv.at[step], pair, grp)
        copy.start()
        wf_out.append(copy)
    for step in range(1, chips):
        dst = keys.at[chip_from(step)]
        remote(dst, dst, k_send.at[step], k_recv.at[step], chip_peer(step), grp).wait_recv()
        copy = remote(dst, dst, kf_send.at[step], kf_recv.at[step], pair, grp)
        copy.start()
        kf_out.append(copy)
    other_half = pl.ds(pl.multiple_of((1 - core) * hrows, hrows), hrows)
    for step in range(1, group_axis):
        dst = w_all.at[grp_from(step), other_half]
        remote(dst, dst, wf_send.at[step], wf_recv.at[step], pair, grp).wait_recv()

    weight = w_all[...].reshape(width, proj_width)
    projected = jnp.dot(scaled_b[...], weight, preferred_element_type=jnp.float32)
    proj_scale = lax.rsqrt(
        jnp.mean(projected * projected, axis=1, keepdims=True) + norm_eps
    ) / math.sqrt(proj_width)
    query_unit = (projected * proj_scale).astype(jnp.bfloat16)

    def first_pass(block, total):
        scores = lax.dot_general(
            query_unit, keys[block], NT, preferred_element_type=jnp.float32
        )
        exp_terms = jnp.exp(scores * (1.0 / token_temp)).astype(jnp.bfloat16)
        powers_b[block] = exp_terms
        return total + jnp.dot(exp_terms, live[block], preferred_element_type=jnp.float32)

    total = first_pass(me, jnp.zeros((rows, lemmas_all), jnp.float32))
    for step in range(1, chips):
        total = first_pass(chip_from(step), total)
    for step in range(chips):
        block = lax.rem(chip + chips - step, chips) * 2 + (1 - core)
        dst = keys.at[block]
        remote(dst, dst, kf_send.at[step], kf_recv.at[step], pair, grp).wait_recv()
        total = first_pass(block, total)

    tok_lse = token_temp * jnp.log(total)
    first_state = (me * group_axis + grp) * states_dev
    ratios = []
    losses = jnp.zeros((1, 128), jnp.float32)
    lane = lax.broadcasted_iota(jnp.int32, (1, 128), 1)
    for state in range(states_dev):
        length = qlen_ref[first_state + state]
        target = pos_ref[first_state + state]
        length_f = jnp.full((1, lemmas_all), length, jnp.int32).astype(jnp.float32)
        span = slice(state * query_tok, (state + 1) * query_tok)
        row_ids = lax.broadcasted_iota(jnp.int32, (query_tok, lemmas_all), 0)
        live_rows = jnp.where(row_ids < length, 1.0, 0.0)
        similarity = jnp.sum(tok_lse[span] * live_rows, axis=0, keepdims=True) / length_f
        powers = jnp.exp(similarity / state_temp)
        lemma_ids = lax.broadcasted_iota(jnp.int32, (1, lemmas_all), 1)
        is_positive = jnp.where(lemma_ids == target, 1.0, 0.0)
        partition = jnp.sum(powers, axis=1, keepdims=True)
        pos_score = jnp.sum(similarity * is_positive, axis=1, keepdims=True)
        loss = jnp.log(partition) - pos_score / state_temp
        losses = jnp.where(lane == state, loss, losses)
        grad_sim = loss_scale * (powers / partition - is_positive) / state_temp
        ratios.append(live_rows * (grad_sim / length_f) / total[span])
    loss_ref[...] = losses
    ratio = jnp.concatenate(ratios, axis=0).astype(jnp.bfloat16)

    unit_grad = jnp.zeros((rows, proj_width), jnp.float32)
    for block in range(lemma_axis):
        spread = lax.dot_general(ratio, live[block], NT, preferred_element_type=jnp.float32)
        coef = (powers_b[block].astype(jnp.float32) * spread).astype(jnp.bfloat16)
        unit_grad += jnp.dot(coef, keys[block], preferred_element_type=jnp.float32)
    proj_grad = proj_scale * unit_grad - projected * (
        proj_scale * proj_scale * proj_scale
    ) * jnp.sum(projected * unit_grad, axis=1, keepdims=True)
    proj_grad_b = proj_grad.astype(jnp.bfloat16)

    weight_part = jnp.dot(scaled_t[...], proj_grad_b, preferred_element_type=jnp.float32)
    piece = wrows // lemma_axis
    for group in range(group_axis):
        for owner in range(lemma_axis):
            start = group * wrows + owner * piece
            part[owner % 2, owner // 2, group] = weight_part[start : start + piece].astype(
                jnp.bfloat16
            )
    pair_copy = remote(part.at[1 - core], pair_in, p_sem.at[0], p_sem.at[1], pair, grp)
    pair_copy.start()
    pair_copy.wait()
    half[...] = (part[core].astype(jnp.float32) + pair_in[...].astype(jnp.float32)).astype(
        jnp.bfloat16
    )
    c_out = []
    for step in range(1, chips):
        copy = remote(
            half.at[lax.rem(chip + step, chips)], chip_in.at[step - 1],
            c_send.at[step], c_recv.at[step], chip_peer(step), grp,
        )
        copy.start()
        c_out.append(copy)

    scaled_grad = lax.dot_general(
        proj_grad_b, w_all[...].reshape(width, proj_width), NT, preferred_element_type=jnp.float32
    )
    row_dot = jnp.sum(projected * proj_grad_b.astype(jnp.float32), axis=1, keepdims=True)
    hout[...] = (
        inv_rms * (scaled_grad * gain_row)
        - hid[...].astype(jnp.float32) * (inv_rms * inv_rms * row_dot / width)
    ).astype(jnp.bfloat16)
    hout_copy = pltpu.make_async_copy(hout, hgrad_ref, local_sem.at[3])
    hout_copy.start()

    for copy in c_out:
        copy.wait()
    chip_sum = half[chip].astype(jnp.float32)
    for step in range(1, chips):
        chip_sum += chip_in[step - 1].astype(jnp.float32)
    quarter[...] = chip_sum.astype(jnp.bfloat16)
    g_out = []
    for step in range(1, group_axis):
        copy = remote(
            quarter.at[grp_peer(step)], grp_in.at[step - 1],
            g_send.at[step], g_recv.at[step], me, grp_peer(step),
        )
        copy.start()
        g_out.append(copy)
    for copy in g_out:
        copy.wait()
    grp_sum = quarter[grp].astype(jnp.float32)
    for step in range(1, group_axis):
        grp_sum += grp_in[step - 1].astype(jnp.float32)
    raw[me] = grp_sum.astype(jnp.bfloat16)
    a_out = []
    for step in range(1, lemma_axis):
        copy = remote(
            raw.at[me], raw.at[me], a_send.at[step], a_recv.at[step],
            lax.rem(me + step, lemma_axis), grp,
        )
        copy.start()
        a_out.append(copy)
    for step in range(1, lemma_axis):
        dst = raw.at[lax.rem(me + lemma_axis - step, lemma_axis)]
        remote(dst, dst, a_send.at[step], a_recv.at[step], me, grp_peer(1)).wait_recv()

    weight_raw = raw[...].reshape(wrows, proj_width).astype(jnp.float32)
    ones = jnp.ones((8, proj_width), jnp.float32)
    own_gain = gain_ref[pl.ds(pl.multiple_of(grp * wrows, 128), wrows)].reshape(1, wrows)
    gain_raw = lax.dot_general(
        ones, w_all[grp].astype(jnp.float32) * weight_raw, NT,
        preferred_element_type=jnp.float32, precision=lax.Precision.HIGHEST,
    )[:1] / own_gain
    squares = jnp.sum(weight_raw * weight_raw) + jnp.sum(gain_raw * gain_raw)
    sq[grp] = jnp.full((8, 128), squares, jnp.float32)
    s_out = []
    for step in range(1, group_axis):
        copy = remote(
            sq.at[grp], sq.at[grp], s_send.at[step], s_recv.at[step], me, grp_peer(step)
        )
        copy.start()
        s_out.append(copy)
    for step in range(1, group_axis):
        dst = sq.at[grp_from(step)]
        remote(dst, dst, s_send.at[step], s_recv.at[step], me, grp_peer(step)).wait_recv()
    squares_all = sq[0, :1, :]
    for group in range(1, group_axis):
        squares_all += sq[group, :1, :]
    factor = jnp.minimum(1.0, grad_limit / jnp.sqrt(squares_all + norm_eps))
    wgrad_ref[...] = weight_raw * factor
    ggrad_ref[...] = gain_raw * factor[:, :1]

    for copy in w_out + k_out + wf_out + kf_out + a_out + s_out:
        copy.wait_send()
    hout_copy.wait()


def place_kernel(loss, hgrad, wgrad, ggrad, loss_out, hgrad_out, wgrad_out, ggrad_out, sems):
    copies = [
        pltpu.make_async_copy(hgrad, hgrad_out, sems.at[0]),
        pltpu.make_async_copy(wgrad, wgrad_out, sems.at[1]),
    ]
    for copy in copies:
        copy.start()
    loss_out[...] = loss[0, : loss_out.shape[0]]
    ggrad_out[...] = ggrad[...].reshape(ggrad_out.shape)
    for copy in copies:
        copy.wait()


def fused_body(hidden, gain, weight, lemma_emb, lemma_len, query_len, positive):
    states_dev, query_tok, width = hidden.shape
    wrows, proj_width = weight.shape
    lemma_dev, lemma_tok = lemma_emb.shape[:2]
    lemma_axis, group_axis = lax.axis_size("lemma"), lax.axis_size("grp")
    chips = lemma_axis // 2
    rows, block_tok = states_dev * query_tok, lemma_dev * lemma_tok
    piece = wrows // lemma_axis
    lemmas_all = lemma_dev * lemma_axis
    vmem = pl.BlockSpec(memory_space=pltpu.VMEM)
    smem = pl.BlockSpec(memory_space=pltpu.SMEM)
    hbm = pl.BlockSpec(memory_space=pltpu.HBM)
    sem = pltpu.SemaphoreType.DMA
    bf16, f32 = jnp.bfloat16, jnp.float32
    outs = pl.pallas_call(
        functools.partial(
            fused_kernel, lemma_axis, group_axis, lemma_dev, lemma_tok, states_dev, query_tok
        ),
        out_shape=(
            jax.ShapeDtypeStruct((1, 128), f32),
            jax.ShapeDtypeStruct((rows, width), bf16),
            jax.ShapeDtypeStruct((wrows, proj_width), f32),
            jax.ShapeDtypeStruct((1, wrows), f32),
        ),
        in_specs=[hbm, vmem, hbm, hbm, vmem, smem, smem],
        out_specs=(vmem, hbm, vmem, vmem),
        scratch_shapes=[
            pltpu.VMEM((rows, width), bf16),
            pltpu.VMEM((block_tok, proj_width), bf16),
            pltpu.VMEM((rows, width), bf16),
            pltpu.VMEM((group_axis, wrows, proj_width), bf16),
            pltpu.VMEM((lemma_axis, block_tok, proj_width), bf16),
            pltpu.VMEM((lemma_axis, block_tok, lemmas_all), bf16),
            pltpu.VMEM((lemma_axis, rows, block_tok), bf16),
            pltpu.VMEM((rows, width), bf16),
            pltpu.VMEM((width, rows), bf16),
            pltpu.VMEM((2, chips, group_axis, piece, proj_width), bf16),
            pltpu.VMEM((chips, group_axis, piece, proj_width), bf16),
            pltpu.VMEM((chips, group_axis, piece, proj_width), bf16),
            pltpu.VMEM((chips - 1, group_axis, piece, proj_width), bf16),
            pltpu.VMEM((group_axis, piece, proj_width), bf16),
            pltpu.VMEM((group_axis - 1, piece, proj_width), bf16),
            pltpu.VMEM((lemma_axis, piece, proj_width), bf16),
            pltpu.VMEM((group_axis, 8, 128), f32),
            sem((4,)),
            sem((group_axis,)), sem((group_axis,)), sem((group_axis,)), sem((group_axis,)),
            sem((chips,)), sem((chips,)), sem((chips,)), sem((chips,)),
            sem((2,)),
            sem((chips,)), sem((chips,)),
            sem((group_axis,)), sem((group_axis,)),
            sem((lemma_axis,)), sem((lemma_axis,)),
            sem((group_axis,)), sem((group_axis,)),
        ],
        compiler_params=pltpu.CompilerParams(
            collective_id=0, has_side_effects=True, vmem_limit_bytes=62 * 1024 * 1024
        ),
        cost_estimate=pl.CostEstimate(
            flops=2 * rows * proj_width * (3 * width + 4 * block_tok * lemma_axis),
            bytes_accessed=4 * rows * width * 2,
            transcendentals=rows * block_tok * lemma_axis,
        ),
    )(
        hidden.reshape(rows, width), gain, weight,
        lemma_emb.reshape(block_tok, proj_width), lemma_len,
        query_len, positive,
    )
    loss, hidden_grad, weight_grad, gain_grad = pl.pallas_call(
        place_kernel,
        out_shape=(
            jax.ShapeDtypeStruct((states_dev,), f32),
            jax.ShapeDtypeStruct((rows, width), bf16),
            jax.ShapeDtypeStruct((wrows, proj_width), f32),
            jax.ShapeDtypeStruct((wrows,), f32),
        ),
        in_specs=[vmem, pl.BlockSpec(memory_space=pl.ANY), pl.BlockSpec(memory_space=pl.ANY), vmem],
        out_specs=(vmem, hbm, hbm, vmem),
        scratch_shapes=[sem((2,))],
        compiler_params=pltpu.CompilerParams(vmem_limit_bytes=62 * 1024 * 1024),
    )(*outs)
    return (loss, hidden_grad.reshape(hidden.shape), weight_grad, gain_grad)


def solution(mesh):
    in_specs = (
        P(("lemma", "grp"), None, None),
        P(),
        P("grp", None),
        P("lemma", None, None),
        P(),
        P(),
        P(),
    )
    out_specs = (P(("lemma", "grp")), P(("lemma", "grp"), None, None), P("grp", None), P("grp"))

    def run(hidden, gain, weight, *rest):
        rows = weight.shape[0] // mesh.shape["grp"]
        tiled = rows % (16 * mesh.shape["lemma"]) == 0 and rows % 128 == 0
        chosen = fused_body if tiled else body
        return jax.shard_map(
            chosen, mesh=mesh, in_specs=in_specs, out_specs=out_specs, check_vma=False
        )(hidden, gain, weight, *rest)

    return run
```

```python
import functools
import math

import jax
import jax.numpy as jnp
from jax import lax
from jax.experimental import pallas as pl
from jax.experimental.pallas import tpu as pltpu
from jax.sharding import PartitionSpec as P

token_temp = 0.05
state_temp = 0.05
loss_scale = 1024.0
grad_limit = 400.0
norm_eps = 1e-06


def contract_last(left, right):
    return lax.dot_general(
        left, right, (((1,), (1,)), ((), ())), preferred_element_type=jnp.float32
    )


def unit_rows(values):
    scale_rows = lax.rsqrt(jnp.mean(values * values, axis=-1, keepdims=True) + norm_eps)
    return values * scale_rows / math.sqrt(values.shape[-1])


def lemma_terms(queries, keys, key_live, lemma_count, lemma_tok):
    scores = contract_last(queries, keys)
    exp_terms = jnp.exp(scores / token_temp) * key_live[None, :]
    per_lemma = jnp.sum(exp_terms.reshape(queries.shape[0], lemma_count, lemma_tok), axis=2)
    return (exp_terms, per_lemma)


def token_grads(queries, grads, keys, key_live, lemma_count, lemma_tok):
    exp_terms, per_lemma = lemma_terms(queries, keys, key_live, lemma_count, lemma_tok)
    rows = queries.shape[0]
    weights = exp_terms.reshape(rows, lemma_count, lemma_tok) / per_lemma[:, :, None]
    coef = (weights * grads[:, :, None]).reshape(rows, lemma_count * lemma_tok).astype(jnp.bfloat16)
    return jnp.dot(coef, keys, preferred_element_type=jnp.float32)


def state_loss(tok_lse, live_rows, lengths_f, targets, lemma_ids):
    states = live_rows.shape[0]
    similarity = (
        jnp.sum(tok_lse.reshape(states, live_rows.shape[1], -1) * live_rows[:, :, None], axis=1)
        / lengths_f[:, None]
    )
    powers = jnp.exp(similarity / state_temp)
    is_positive = (lemma_ids[None, :] == targets[:, None]).astype(jnp.float32)
    return (similarity, powers, is_positive)


def body(hidden, gain, weight, lemma_emb, lemma_len, query_len, positive):
    states_dev, query_tok, width = hidden.shape
    proj_width = weight.shape[1]
    lemma_dev, lemma_tok = (lemma_emb.shape[0], lemma_emb.shape[1])
    lemma_axis = lax.axis_size("lemma")
    group_axis = lax.axis_size("grp")
    lemma_idx = lax.axis_index("lemma")
    group_idx = lax.axis_index("grp")
    own_rows = states_dev * query_tok
    lemmas_all = lemma_dev * lemma_axis
    in_float = hidden.reshape(own_rows, width).astype(jnp.float32)
    inv_rms = lax.rsqrt(jnp.mean(in_float * in_float, axis=1, keepdims=True) + norm_eps)
    normed = in_float * inv_rms
    scaled = (normed * gain[None, :]).astype(jnp.bfloat16)
    projected = jnp.dot(
        scaled,
        lax.all_gather(weight, "grp", axis=0, tiled=True),
        preferred_element_type=jnp.float32,
    )
    proj_scale = lax.rsqrt(
        jnp.mean(projected * projected, axis=1, keepdims=True) + norm_eps
    ) / math.sqrt(proj_width)
    query_unit = (projected * proj_scale).astype(jnp.bfloat16)
    lemma_unit = unit_rows(lemma_emb.astype(jnp.float32).reshape(-1, proj_width)).astype(
        jnp.bfloat16
    )
    all_live = (jnp.arange(lemma_tok)[None, :] < lemma_len[:, None]).astype(jnp.float32)
    block_start = (lemma_idx * group_axis + group_idx) * states_dev
    all_keys = lax.all_gather(lemma_unit, "lemma", axis=0, tiled=True)
    block_count = 8
    block_lemmas = lemmas_all // block_count
    key_blocks = all_keys.reshape(block_count, block_lemmas * lemma_tok, proj_width)
    live_blocks = all_live.reshape(block_count, block_lemmas * lemma_tok)
    own_len = lax.dynamic_slice_in_dim(query_len, block_start, states_dev)
    own_pos = lax.dynamic_slice_in_dim(positive, block_start, states_dev)
    live_rows = (jnp.arange(query_tok)[None, :] < own_len[:, None]).astype(jnp.float32)
    lengths_f = own_len.astype(jnp.float32)

    def block_lse(items):
        keys, key_live = items
        exp_terms, per_lemma = lemma_terms(query_unit, keys, key_live, block_lemmas, lemma_tok)
        return token_temp * jnp.log(per_lemma)

    tok_lse = lax.map(block_lse, (key_blocks, live_blocks))
    tok_lse = jnp.moveaxis(tok_lse, 0, 1).reshape(own_rows, lemmas_all)
    similarity, powers, is_positive = state_loss(
        tok_lse, live_rows, lengths_f, own_pos, jnp.arange(lemmas_all)
    )
    partition = jnp.sum(powers, axis=1)
    pos_score = jnp.sum(similarity * is_positive, axis=1)
    loss = jnp.log(partition) - pos_score / state_temp
    grad_sim = loss_scale * (powers / partition[:, None] - is_positive) / state_temp
    tok_grad = (grad_sim[:, None, :] * live_rows[:, :, None] / lengths_f[:, None, None]).reshape(
        own_rows, block_count, block_lemmas
    )
    grad_blocks = jnp.moveaxis(tok_grad, 1, 0)

    def add_block(acc, items):
        keys, key_live, grads = items
        return (acc + token_grads(query_unit, grads, keys, key_live, block_lemmas, lemma_tok), None)

    unit_grad, unused = lax.scan(
        add_block,
        jnp.zeros((own_rows, proj_width), jnp.float32),
        (key_blocks, live_blocks, grad_blocks),
    )
    proj_grad = proj_scale * unit_grad - projected * proj_scale**3 * jnp.sum(
        projected * unit_grad, axis=1, keepdims=True
    )
    proj_grad_b = proj_grad.astype(jnp.bfloat16)
    scaled_grad = contract_last(proj_grad_b, lax.all_gather(weight, "grp", axis=0, tiled=True))
    normed_grad = scaled_grad * gain[None, :]
    input_grad = (
        inv_rms * normed_grad
        - in_float * inv_rms**3 * jnp.sum(in_float * normed_grad, axis=1, keepdims=True) / width
    )
    hidden_grad = input_grad.astype(jnp.bfloat16).reshape(states_dev, query_tok, width)
    weight_part = lax.dot_general(
        scaled, proj_grad_b, (((0,), (0,)), ((), ())), preferred_element_type=jnp.float32
    )
    gain_part = jnp.sum(scaled_grad * normed, axis=0)
    weight_sum, gain_sum = (
        lax.psum(weight_part.astype(jnp.bfloat16), "lemma").astype(jnp.float32),
        lax.psum(gain_part.astype(jnp.bfloat16), "lemma").astype(jnp.float32),
    )
    weight_sum, gain_sum = (
        lax.psum_scatter(
            weight_sum.astype(jnp.bfloat16), "grp", scatter_dimension=0, tiled=True
        ).astype(jnp.float32),
        lax.psum_scatter(
            gain_sum.astype(jnp.bfloat16), "grp", scatter_dimension=0, tiled=True
        ).astype(jnp.float32),
    )
    squares = jnp.sum(weight_sum * weight_sum) + jnp.sum(gain_sum * gain_sum)
    total_squares = lax.psum(squares, "grp")
    factor = jnp.minimum(1.0, grad_limit / jnp.sqrt(total_squares + norm_eps))
    return (loss, hidden_grad, weight_sum * factor, gain_sum * factor)


NT = (((1,), (1,)), ((), ()))
MESH = pl.DeviceIdType.MESH


def fused_kernel(
    lemma_axis, group_axis, lemma_dev, lemma_tok, states_dev, query_tok,
    hidden_ref, gain_ref, weight_ref, emb_ref, len_ref, qlen_ref, pos_ref,
    loss_ref, hgrad_ref, wgrad_ref, ggrad_ref,
    hid, emb, hout, w_all, keys, live, powers_b, scaled_b, scaled_t,
    part, pair_in, half, chip_in, quarter, grp_in, raw, sq, over_gain,
    local_sem, w_send, w_recv, wf_send, wf_recv, k_send, k_recv, kf_send, kf_recv,
    p_send, p_recv, c_send, c_recv, g_send, g_recv, a_send, a_recv, s_send, s_recv,
):
    chips = lemma_axis // 2
    me, grp = lax.axis_index("lemma"), lax.axis_index("grp")
    chip, core = me // 2, lax.rem(me, 2)
    pair = chip * 2 + (1 - core)
    rows, width = hid.shape
    gain_row = gain_ref[...].reshape(1, width)
    proj_width = weight_ref.shape[1]
    wrows = weight_ref.shape[0]
    hrows = wrows // 2
    block_tok = lemma_dev * lemma_tok
    lemmas_all = lemma_dev * lemma_axis

    across = 2 - chips % 2
    along = chips // across
    chip_y, chip_x = chip // across, lax.rem(chip, across)

    def chip_to(step):
        step_y, step_x = step // across, step % across
        return lax.rem(chip_y + step_y, along) * across + lax.rem(chip_x + step_x, across)

    def chip_source(step):
        step_y, step_x = step // across, step % across
        return lax.rem(chip_y + along - step_y, along) * across + lax.rem(
            chip_x + across - step_x, across
        )

    def chip_peer(step):
        return chip_to(step) * 2 + core

    def chip_from(step):
        return chip_source(step) * 2 + core

    def grp_peer(step):
        return lax.rem(grp + step, group_axis)

    def grp_from(step):
        return lax.rem(grp + group_axis - step, group_axis)

    def remote(src, dst, send_sem, recv_sem, to_lemma, to_grp):
        return pltpu.make_async_remote_copy(
            src_ref=src, dst_ref=dst, send_sem=send_sem, recv_sem=recv_sem,
            device_id=(to_lemma, to_grp), device_id_type=MESH,
        )

    emb_copy = pltpu.make_async_copy(emb_ref, emb, local_sem.at[0])
    hid_copy = pltpu.make_async_copy(hidden_ref, hid, local_sem.at[1])
    w_copy = pltpu.make_async_copy(weight_ref, w_all.at[grp], local_sem.at[2])
    emb_copy.start()
    w_copy.start()
    hid_copy.start()

    barrier = pltpu.get_barrier_semaphore()
    others = [
        (lemma_step, grp_step)
        for lemma_step in range(lemma_axis)
        for grp_step in range(group_axis)
        if lemma_step or grp_step
    ]
    for lemma_step, grp_step in others:
        pl.semaphore_signal(
            barrier, inc=1, device_id_type=MESH,
            device_id=(lax.rem(me + lemma_step, lemma_axis), grp_peer(grp_step)),
        )

    emb_copy.wait()
    tokens = emb[...].astype(jnp.float32)
    token_scale = lax.rsqrt(
        jnp.mean(tokens * tokens, axis=1, keepdims=True) + norm_eps
    ) / math.sqrt(proj_width)
    keys[me] = (tokens * token_scale).astype(jnp.bfloat16)
    w_copy.wait()
    pl.semaphore_wait(barrier, len(others))

    my_half = pl.ds(pl.multiple_of(core * hrows, hrows), hrows)
    w_out = []
    for step in range(1, group_axis):
        src = w_all.at[grp, my_half]
        copy = remote(src, src, w_send.at[step], w_recv.at[step], me, grp_peer(step))
        copy.start()
        w_out.append(copy)
    k_out = []
    for step in reversed(range(1, chips)):
        copy = remote(
            keys.at[me], keys.at[me], k_send.at[step], k_recv.at[step], chip_peer(step), grp
        )
        copy.start()
        k_out.append(copy)
    kf_out = [remote(keys.at[me], keys.at[me], kf_send.at[0], kf_recv.at[0], pair, grp)]
    kf_out[0].start()

    token_of = lax.broadcasted_iota(
        jnp.int32, (block_tok, lemmas_all), 0
    ) - lemma_tok * lax.broadcasted_iota(jnp.int32, (block_tok, lemmas_all), 1)
    lengths = jnp.minimum(len_ref[...].reshape(1, lemmas_all), lemma_tok)
    for block in range(lemma_axis):
        first = -block * block_tok
        member = (token_of >= first) & (token_of < lengths + first)
        live[block] = jnp.where(member, 1.0, 0.0).astype(jnp.bfloat16)

    hid_copy.wait()
    in_float = hid[...].astype(jnp.float32)
    inv_rms = lax.rsqrt(jnp.mean(in_float * in_float, axis=1, keepdims=True) + norm_eps)
    scaled = (in_float * inv_rms * gain_row).astype(jnp.bfloat16)
    scaled_b[...] = scaled
    scaled_t[...] = scaled.T

    own_gain = gain_ref[pl.ds(pl.multiple_of(grp * wrows, 128), wrows)].reshape(1, wrows)
    gain_col = jnp.broadcast_to(own_gain, (proj_width, wrows)).T
    over_gain[...] = (w_all[grp].astype(jnp.float32) / gain_col).reshape(over_gain.shape)

    wf_out = []
    for step in range(1, group_axis):
        dst = w_all.at[grp_from(step), my_half]
        remote(dst, dst, w_send.at[step], w_recv.at[step], me, grp_peer(step)).wait_recv()
        copy = remote(dst, dst, wf_send.at[step], wf_recv.at[step], pair, grp)
        copy.start()
        wf_out.append(copy)
    other_half = pl.ds(pl.multiple_of((1 - core) * hrows, hrows), hrows)
    for step in range(1, group_axis):
        dst = w_all.at[grp_from(step), other_half]
        remote(dst, dst, wf_send.at[step], wf_recv.at[step], pair, grp).wait_recv()

    weight = w_all[...].reshape(width, proj_width)
    projected = jnp.dot(scaled_b[...], weight, preferred_element_type=jnp.float32)
    proj_scale = lax.rsqrt(
        jnp.mean(projected * projected, axis=1, keepdims=True) + norm_eps
    ) / math.sqrt(proj_width)
    query_unit = (projected * proj_scale).astype(jnp.bfloat16)

    def first_pass(block, total):
        scores = lax.dot_general(
            query_unit, keys[block], NT, preferred_element_type=jnp.float32
        )
        exp_terms = jnp.exp(scores * (1.0 / token_temp)).astype(jnp.bfloat16)
        powers_b[block] = exp_terms
        return total + jnp.dot(exp_terms, live[block], preferred_element_type=jnp.float32)

    def from_pair(step):
        block = chip_source(step) * 2 + (1 - core)
        dst = keys.at[block]
        remote(dst, dst, kf_send.at[step], kf_recv.at[step], pair, grp).wait_recv()
        return block

    total = first_pass(me, jnp.zeros((rows, lemmas_all), jnp.float32))
    total = first_pass(from_pair(0), total)
    for step in range(1, chips):
        dst = keys.at[chip_from(step)]
        remote(dst, dst, k_send.at[step], k_recv.at[step], chip_peer(step), grp).wait_recv()
        copy = remote(dst, dst, kf_send.at[step], kf_recv.at[step], pair, grp)
        copy.start()
        kf_out.append(copy)
    for step in range(1, chips):
        total = first_pass(chip_from(step), total)
    for step in range(1, chips):
        total = first_pass(from_pair(step), total)

    tok_lse = token_temp * jnp.log(total)
    first_state = (me * group_axis + grp) * states_dev
    ratios = []
    losses = jnp.zeros((1, 128), jnp.float32)
    lane = lax.broadcasted_iota(jnp.int32, (1, 128), 1)
    for state in range(states_dev):
        length = qlen_ref[first_state + state]
        target = pos_ref[first_state + state]
        length_f = jnp.full((1, lemmas_all), length, jnp.int32).astype(jnp.float32)
        span = slice(state * query_tok, (state + 1) * query_tok)
        row_ids = lax.broadcasted_iota(jnp.int32, (query_tok, lemmas_all), 0)
        live_rows = jnp.where(row_ids < length, 1.0, 0.0)
        similarity = jnp.sum(tok_lse[span] * live_rows, axis=0, keepdims=True) / length_f
        powers = jnp.exp(similarity / state_temp)
        lemma_ids = lax.broadcasted_iota(jnp.int32, (1, lemmas_all), 1)
        is_positive = jnp.where(lemma_ids == target, 1.0, 0.0)
        partition = jnp.sum(powers, axis=1, keepdims=True)
        pos_score = jnp.sum(similarity * is_positive, axis=1, keepdims=True)
        loss = jnp.log(partition) - pos_score / state_temp
        losses = jnp.where(lane == state, loss, losses)
        grad_sim = loss_scale * (powers / partition - is_positive) / state_temp
        ratios.append(live_rows * (grad_sim / length_f) / total[span])
    loss_ref[...] = losses
    ratio = jnp.concatenate(ratios, axis=0).astype(jnp.bfloat16)

    unit_grad = jnp.zeros((rows, proj_width), jnp.float32)
    for block in range(lemma_axis):
        spread = lax.dot_general(ratio, live[block], NT, preferred_element_type=jnp.float32)
        coef = (powers_b[block].astype(jnp.float32) * spread).astype(jnp.bfloat16)
        unit_grad += jnp.dot(coef, keys[block], preferred_element_type=jnp.float32)
    proj_grad = proj_scale * unit_grad - projected * (
        proj_scale * proj_scale * proj_scale
    ) * jnp.sum(projected * unit_grad, axis=1, keepdims=True)
    proj_grad_b = proj_grad.astype(jnp.bfloat16)

    weight_part = jnp.dot(scaled_t[...], proj_grad_b, preferred_element_type=jnp.float32)
    piece = wrows // lemma_axis
    for group in range(group_axis):
        for owner in range(lemma_axis):
            start = group * wrows + owner * piece
            part[owner % 2, owner // 2, group] = weight_part[start : start + piece].astype(
                jnp.bfloat16
            )
    order = list(reversed(range(chips)))
    p_out = []
    for step in order:
        target = chip_to(step)
        copy = remote(
            part.at[1 - core, target], pair_in.at[step], p_send.at[step], p_recv.at[step], pair, grp
        )
        copy.start()
        p_out.append(copy)
    c_out = []
    for step, pair_copy in zip(order, p_out):
        target = chip_to(step)
        pair_copy.wait_recv()
        half[step] = (
            part[core, target].astype(jnp.float32) + pair_in[step].astype(jnp.float32)
        ).astype(jnp.bfloat16)
        if step:
            copy = remote(
                half.at[step], chip_in.at[step - 1],
                c_send.at[step], c_recv.at[step], chip_peer(step), grp,
            )
            copy.start()
            c_out.append(copy)

    scaled_grad = lax.dot_general(
        proj_grad_b, w_all[...].reshape(width, proj_width), NT, preferred_element_type=jnp.float32
    )
    row_dot = jnp.sum(projected * proj_grad_b.astype(jnp.float32), axis=1, keepdims=True)
    hout[...] = (
        inv_rms * (scaled_grad * gain_row)
        - hid[...].astype(jnp.float32) * (inv_rms * inv_rms * row_dot / width)
    ).astype(jnp.bfloat16)
    hout_copy = pltpu.make_async_copy(hout, hgrad_ref, local_sem.at[3])
    hout_copy.start()

    for copy in c_out:
        copy.wait()
    chip_sum = half[0].astype(jnp.float32)
    for step in range(1, chips):
        chip_sum += chip_in[step - 1].astype(jnp.float32)
    quarter[...] = chip_sum.astype(jnp.bfloat16)
    g_out = []
    for step in range(1, group_axis):
        copy = remote(
            quarter.at[grp_peer(step)], grp_in.at[step - 1],
            g_send.at[step], g_recv.at[step], me, grp_peer(step),
        )
        copy.start()
        g_out.append(copy)
    for copy in g_out:
        copy.wait()
    grp_sum = quarter[grp].astype(jnp.float32)
    for step in range(1, group_axis):
        grp_sum += grp_in[step - 1].astype(jnp.float32)
    own_raw = grp_sum.astype(jnp.bfloat16)
    raw[me] = own_raw
    a_out = []
    for step in range(1, lemma_axis):
        copy = remote(
            raw.at[me], raw.at[me], a_send.at[step], a_recv.at[step],
            lax.rem(me + step, lemma_axis), grp,
        )
        copy.start()
        a_out.append(copy)
    own_raw = own_raw.astype(jnp.float32)
    own_gain_raw = jnp.sum(own_raw * over_gain[me], axis=1, keepdims=True)
    squares = jnp.sum(own_raw * own_raw) + jnp.sum(own_gain_raw * own_gain_raw)
    my_sq = sq.at[grp * lemma_axis + me]
    my_sq[...] = jnp.full((1, 128), squares, jnp.float32)
    for lemma_step, grp_step in others:
        copy = remote(
            my_sq, my_sq, s_send, s_recv,
            lax.rem(me + lemma_step, lemma_axis), grp_peer(grp_step),
        )
        copy.start()
    for step in range(1, lemma_axis):
        dst = raw.at[lax.rem(me + lemma_axis - step, lemma_axis)]
        remote(dst, dst, a_send.at[step], a_recv.at[step], pair, grp).wait_recv()

    weight_raw = raw[...].reshape(wrows, proj_width).astype(jnp.float32)
    ones = jnp.ones((8, proj_width), jnp.float32)
    gain_raw = lax.dot_general(
        ones, over_gain[...].reshape(wrows, proj_width) * weight_raw, NT,
        preferred_element_type=jnp.float32, precision=lax.Precision.HIGHEST,
    )[:1]
    all_but_one = sq.at[pl.ds(0, len(others))]
    remote(all_but_one, all_but_one, s_send, s_recv, pair, grp).wait()
    squares_all = jnp.sum(sq[...], axis=0)
    factor = jnp.minimum(1.0, grad_limit / jnp.sqrt(squares_all + norm_eps))
    wgrad_ref[...] = weight_raw * factor
    ggrad_ref[...] = gain_raw * factor[:, :1]

    for copy in w_out + k_out + wf_out + kf_out + p_out + a_out:
        copy.wait_send()
    hout_copy.wait()


def place_kernel(
    loss, hgrad, wgrad, ggrad, loss_out, hgrad_out, wgrad_out, ggrad_out,
    loss_in, hbuf, wbuf, ggrad_in, loss_row, ggrad_row, sems,
):
    pairs = [(hgrad, hbuf), (wgrad, wbuf), (loss, loss_in), (ggrad, ggrad_in)]
    copies = [pltpu.make_async_copy(a, b, sems.at[i]) for i, (a, b) in enumerate(pairs)]
    for copy in copies:
        copy.start()
    pairs = [(hbuf, hgrad_out), (wbuf, wgrad_out), (loss_row, loss_out), (ggrad_row, ggrad_out)]
    backs = [pltpu.make_async_copy(a, b, sems.at[4 + i]) for i, (a, b) in enumerate(pairs)]
    copies[0].wait()
    backs[0].start()
    copies[1].wait()
    backs[1].start()
    copies[2].wait()
    loss_row[...] = loss_in[0, : loss_row.shape[0]]
    backs[2].start()
    copies[3].wait()
    ggrad_row[...] = ggrad_in[...].reshape(ggrad_row.shape)
    backs[3].start()
    for copy in backs:
        copy.wait()


def fused_body(hidden, gain, weight, lemma_emb, lemma_len, query_len, positive):
    states_dev, query_tok, width = hidden.shape
    wrows, proj_width = weight.shape
    lemma_dev, lemma_tok = lemma_emb.shape[:2]
    lemma_axis, group_axis = lax.axis_size("lemma"), lax.axis_size("grp")
    chips = lemma_axis // 2
    rows, block_tok = states_dev * query_tok, lemma_dev * lemma_tok
    piece = wrows // lemma_axis
    lemmas_all = lemma_dev * lemma_axis
    vmem = pl.BlockSpec(memory_space=pltpu.VMEM)
    smem = pl.BlockSpec(memory_space=pltpu.SMEM)
    hbm = pl.BlockSpec(memory_space=pltpu.HBM)
    sem = pltpu.SemaphoreType.DMA
    bf16, f32 = jnp.bfloat16, jnp.float32
    outs = pl.pallas_call(
        functools.partial(
            fused_kernel, lemma_axis, group_axis, lemma_dev, lemma_tok, states_dev, query_tok
        ),
        out_shape=(
            jax.ShapeDtypeStruct((1, 128), f32),
            jax.ShapeDtypeStruct((rows, width), bf16),
            jax.ShapeDtypeStruct((wrows, proj_width), f32),
            jax.ShapeDtypeStruct((1, wrows), f32),
        ),
        in_specs=[hbm, vmem, hbm, hbm, vmem, smem, smem],
        out_specs=(vmem, hbm, vmem, vmem),
        scratch_shapes=[
            pltpu.VMEM((rows, width), bf16),
            pltpu.VMEM((block_tok, proj_width), bf16),
            pltpu.VMEM((rows, width), bf16),
            pltpu.VMEM((group_axis, wrows, proj_width), bf16),
            pltpu.VMEM((lemma_axis, block_tok, proj_width), bf16),
            pltpu.VMEM((lemma_axis, block_tok, lemmas_all), bf16),
            pltpu.VMEM((lemma_axis, rows, block_tok), bf16),
            pltpu.VMEM((rows, width), bf16),
            pltpu.VMEM((width, rows), bf16),
            pltpu.VMEM((2, chips, group_axis, piece, proj_width), bf16),
            pltpu.VMEM((chips, group_axis, piece, proj_width), bf16),
            pltpu.VMEM((chips, group_axis, piece, proj_width), bf16),
            pltpu.VMEM((chips - 1, group_axis, piece, proj_width), bf16),
            pltpu.VMEM((group_axis, piece, proj_width), bf16),
            pltpu.VMEM((group_axis - 1, piece, proj_width), bf16),
            pltpu.VMEM((lemma_axis, piece, proj_width), bf16),
            pltpu.VMEM((group_axis * lemma_axis, 1, 128), f32),
            pltpu.VMEM((lemma_axis, piece, proj_width), f32),
            sem((4,)),
            sem((group_axis,)), sem((group_axis,)), sem((group_axis,)), sem((group_axis,)),
            sem((chips,)), sem((chips,)), sem((chips,)), sem((chips,)),
            sem((chips,)), sem((chips,)),
            sem((chips,)), sem((chips,)),
            sem((group_axis,)), sem((group_axis,)),
            sem((lemma_axis,)), sem((lemma_axis,)),
            sem, sem,
        ],
        compiler_params=pltpu.CompilerParams(
            collective_id=0, has_side_effects=True, vmem_limit_bytes=62 * 1024 * 1024
        ),
        cost_estimate=pl.CostEstimate(
            flops=2 * rows * proj_width * (3 * width + 4 * block_tok * lemma_axis),
            bytes_accessed=4 * rows * width * 2,
            transcendentals=rows * block_tok * lemma_axis,
        ),
    )(
        hidden.reshape(rows, width), gain, weight,
        lemma_emb.reshape(block_tok, proj_width), lemma_len,
        query_len, positive,
    )
    loss, hidden_grad, weight_grad, gain_grad = pl.pallas_call(
        place_kernel,
        out_shape=(
            jax.ShapeDtypeStruct((states_dev,), f32),
            jax.ShapeDtypeStruct((rows, width), bf16),
            jax.ShapeDtypeStruct((wrows, proj_width), f32),
            jax.ShapeDtypeStruct((wrows,), f32),
        ),
        in_specs=[hbm] * 4,
        out_specs=(hbm,) * 4,
        scratch_shapes=[
            pltpu.VMEM((1, 128), f32),
            pltpu.VMEM((rows, width), bf16),
            pltpu.VMEM((wrows, proj_width), f32),
            pltpu.VMEM((1, wrows), f32),
            pltpu.VMEM((states_dev,), f32),
            pltpu.VMEM((wrows,), f32),
            sem((8,)),
        ],
        compiler_params=pltpu.CompilerParams(vmem_limit_bytes=62 * 1024 * 1024),
    )(*outs)
    return (loss, hidden_grad.reshape(hidden.shape), weight_grad, gain_grad)


def solution(mesh):
    in_specs = (
        P(("lemma", "grp"), None, None),
        P(),
        P("grp", None),
        P("lemma", None, None),
        P(),
        P(),
        P(),
    )
    out_specs = (P(("lemma", "grp")), P(("lemma", "grp"), None, None), P("grp", None), P("grp"))

    def run(hidden, gain, weight, *rest):
        rows = weight.shape[0] // mesh.shape["grp"]
        tiled = rows % (16 * mesh.shape["lemma"]) == 0 and rows % 128 == 0
        chosen = fused_body if tiled else body
        return jax.shard_map(
            chosen, mesh=mesh, in_specs=in_specs, out_specs=out_specs, check_vma=False
        )(hidden, gain, weight, *rest)

    return run
```

```python
import functools
import math

import jax
import jax.numpy as jnp
from jax import lax
from jax.experimental import pallas as pl
from jax.experimental.pallas import tpu as pltpu
from jax.sharding import PartitionSpec as P

token_temp = 0.05
state_temp = 0.05
loss_scale = 1024.0
grad_limit = 400.0
norm_eps = 1e-06


def contract_last(left, right):
    return lax.dot_general(
        left, right, (((1,), (1,)), ((), ())), preferred_element_type=jnp.float32
    )


def unit_rows(values):
    scale_rows = lax.rsqrt(jnp.mean(values * values, axis=-1, keepdims=True) + norm_eps)
    return values * scale_rows / math.sqrt(values.shape[-1])


def lemma_terms(queries, keys, key_live, lemma_count, lemma_tok):
    scores = contract_last(queries, keys)
    exp_terms = jnp.exp(scores / token_temp) * key_live[None, :]
    per_lemma = jnp.sum(exp_terms.reshape(queries.shape[0], lemma_count, lemma_tok), axis=2)
    return (exp_terms, per_lemma)


def token_grads(queries, grads, keys, key_live, lemma_count, lemma_tok):
    exp_terms, per_lemma = lemma_terms(queries, keys, key_live, lemma_count, lemma_tok)
    rows = queries.shape[0]
    weights = exp_terms.reshape(rows, lemma_count, lemma_tok) / per_lemma[:, :, None]
    coef = (weights * grads[:, :, None]).reshape(rows, lemma_count * lemma_tok).astype(jnp.bfloat16)
    return jnp.dot(coef, keys, preferred_element_type=jnp.float32)


def state_loss(tok_lse, live_rows, lengths_f, targets, lemma_ids):
    states = live_rows.shape[0]
    similarity = (
        jnp.sum(tok_lse.reshape(states, live_rows.shape[1], -1) * live_rows[:, :, None], axis=1)
        / lengths_f[:, None]
    )
    powers = jnp.exp(similarity / state_temp)
    is_positive = (lemma_ids[None, :] == targets[:, None]).astype(jnp.float32)
    return (similarity, powers, is_positive)


def body(hidden, gain, weight, lemma_emb, lemma_len, query_len, positive):
    states_dev, query_tok, width = hidden.shape
    proj_width = weight.shape[1]
    lemma_dev, lemma_tok = (lemma_emb.shape[0], lemma_emb.shape[1])
    lemma_axis = lax.axis_size("lemma")
    group_axis = lax.axis_size("grp")
    lemma_idx = lax.axis_index("lemma")
    group_idx = lax.axis_index("grp")
    own_rows = states_dev * query_tok
    lemmas_all = lemma_dev * lemma_axis
    in_float = hidden.reshape(own_rows, width).astype(jnp.float32)
    inv_rms = lax.rsqrt(jnp.mean(in_float * in_float, axis=1, keepdims=True) + norm_eps)
    normed = in_float * inv_rms
    scaled = (normed * gain[None, :]).astype(jnp.bfloat16)
    projected = jnp.dot(
        scaled,
        lax.all_gather(weight, "grp", axis=0, tiled=True),
        preferred_element_type=jnp.float32,
    )
    proj_scale = lax.rsqrt(
        jnp.mean(projected * projected, axis=1, keepdims=True) + norm_eps
    ) / math.sqrt(proj_width)
    query_unit = (projected * proj_scale).astype(jnp.bfloat16)
    lemma_unit = unit_rows(lemma_emb.astype(jnp.float32).reshape(-1, proj_width)).astype(
        jnp.bfloat16
    )
    all_live = (jnp.arange(lemma_tok)[None, :] < lemma_len[:, None]).astype(jnp.float32)
    block_start = (lemma_idx * group_axis + group_idx) * states_dev
    all_keys = lax.all_gather(lemma_unit, "lemma", axis=0, tiled=True)
    block_count = 8
    block_lemmas = lemmas_all // block_count
    key_blocks = all_keys.reshape(block_count, block_lemmas * lemma_tok, proj_width)
    live_blocks = all_live.reshape(block_count, block_lemmas * lemma_tok)
    own_len = lax.dynamic_slice_in_dim(query_len, block_start, states_dev)
    own_pos = lax.dynamic_slice_in_dim(positive, block_start, states_dev)
    live_rows = (jnp.arange(query_tok)[None, :] < own_len[:, None]).astype(jnp.float32)
    lengths_f = own_len.astype(jnp.float32)

    def block_lse(items):
        keys, key_live = items
        exp_terms, per_lemma = lemma_terms(query_unit, keys, key_live, block_lemmas, lemma_tok)
        return token_temp * jnp.log(per_lemma)

    tok_lse = lax.map(block_lse, (key_blocks, live_blocks))
    tok_lse = jnp.moveaxis(tok_lse, 0, 1).reshape(own_rows, lemmas_all)
    similarity, powers, is_positive = state_loss(
        tok_lse, live_rows, lengths_f, own_pos, jnp.arange(lemmas_all)
    )
    partition = jnp.sum(powers, axis=1)
    pos_score = jnp.sum(similarity * is_positive, axis=1)
    loss = jnp.log(partition) - pos_score / state_temp
    grad_sim = loss_scale * (powers / partition[:, None] - is_positive) / state_temp
    tok_grad = (grad_sim[:, None, :] * live_rows[:, :, None] / lengths_f[:, None, None]).reshape(
        own_rows, block_count, block_lemmas
    )
    grad_blocks = jnp.moveaxis(tok_grad, 1, 0)

    def add_block(acc, items):
        keys, key_live, grads = items
        return (acc + token_grads(query_unit, grads, keys, key_live, block_lemmas, lemma_tok), None)

    unit_grad, unused = lax.scan(
        add_block,
        jnp.zeros((own_rows, proj_width), jnp.float32),
        (key_blocks, live_blocks, grad_blocks),
    )
    proj_grad = proj_scale * unit_grad - projected * proj_scale**3 * jnp.sum(
        projected * unit_grad, axis=1, keepdims=True
    )
    proj_grad_b = proj_grad.astype(jnp.bfloat16)
    scaled_grad = contract_last(proj_grad_b, lax.all_gather(weight, "grp", axis=0, tiled=True))
    normed_grad = scaled_grad * gain[None, :]
    input_grad = (
        inv_rms * normed_grad
        - in_float * inv_rms**3 * jnp.sum(in_float * normed_grad, axis=1, keepdims=True) / width
    )
    hidden_grad = input_grad.astype(jnp.bfloat16).reshape(states_dev, query_tok, width)
    weight_part = lax.dot_general(
        scaled, proj_grad_b, (((0,), (0,)), ((), ())), preferred_element_type=jnp.float32
    )
    gain_part = jnp.sum(scaled_grad * normed, axis=0)
    weight_sum, gain_sum = (
        lax.psum(weight_part.astype(jnp.bfloat16), "lemma").astype(jnp.float32),
        lax.psum(gain_part.astype(jnp.bfloat16), "lemma").astype(jnp.float32),
    )
    weight_sum, gain_sum = (
        lax.psum_scatter(
            weight_sum.astype(jnp.bfloat16), "grp", scatter_dimension=0, tiled=True
        ).astype(jnp.float32),
        lax.psum_scatter(
            gain_sum.astype(jnp.bfloat16), "grp", scatter_dimension=0, tiled=True
        ).astype(jnp.float32),
    )
    squares = jnp.sum(weight_sum * weight_sum) + jnp.sum(gain_sum * gain_sum)
    total_squares = lax.psum(squares, "grp")
    factor = jnp.minimum(1.0, grad_limit / jnp.sqrt(total_squares + norm_eps))
    return (loss, hidden_grad, weight_sum * factor, gain_sum * factor)


NT = (((1,), (1,)), ((), ()))
MESH = pl.DeviceIdType.MESH


def fused_kernel(
    lemma_axis, group_axis, lemma_dev, lemma_tok, states_dev, query_tok,
    hidden_ref, gain_ref, weight_ref, emb_ref, len_ref, qlen_ref, pos_ref,
    loss_ref, hgrad_ref, wgrad_ref, ggrad_ref,
    hid, emb, hout, w_all, keys, live, live_t, powers_b, scaled_b, scaled_t,
    part, pair_in, half, chip_in, quarter, grp_in, raw, sq, over_gain,
    local_sem, w_send, w_recv, wf_send, wf_recv, k_send, k_recv, kf_send, kf_recv,
    p_send, p_recv, c_send, c_recv, g_send, g_recv, a_send, a_recv, s_send, s_recv,
):
    chips = lemma_axis // 2
    me, grp = lax.axis_index("lemma"), lax.axis_index("grp")
    chip, core = me // 2, lax.rem(me, 2)
    pair = chip * 2 + (1 - core)
    rows, width = hid.shape
    gain_row = gain_ref[...].reshape(1, width)
    proj_width = weight_ref.shape[1]
    wrows = weight_ref.shape[0]
    hrows = wrows // 2
    block_tok = lemma_dev * lemma_tok
    lemmas_all = lemma_dev * lemma_axis

    across = 2 - chips % 2
    along = chips // across
    chip_y, chip_x = chip // across, lax.rem(chip, across)

    def chip_to(step):
        step_y, step_x = step // across, step % across
        return lax.rem(chip_y + step_y, along) * across + lax.rem(chip_x + step_x, across)

    def chip_source(step):
        step_y, step_x = step // across, step % across
        return lax.rem(chip_y + along - step_y, along) * across + lax.rem(
            chip_x + across - step_x, across
        )

    def chip_peer(step):
        return chip_to(step) * 2 + core

    def chip_from(step):
        return chip_source(step) * 2 + core

    def grp_peer(step):
        return lax.rem(grp + step, group_axis)

    def grp_from(step):
        return lax.rem(grp + group_axis - step, group_axis)

    def remote(src, dst, send_sem, recv_sem, to_lemma, to_grp):
        return pltpu.make_async_remote_copy(
            src_ref=src, dst_ref=dst, send_sem=send_sem, recv_sem=recv_sem,
            device_id=(to_lemma, to_grp), device_id_type=MESH,
        )

    emb_copy = pltpu.make_async_copy(emb_ref, emb, local_sem.at[0])
    hid_copy = pltpu.make_async_copy(hidden_ref, hid, local_sem.at[1])
    w_copy = pltpu.make_async_copy(weight_ref, w_all.at[grp], local_sem.at[2])
    emb_copy.start()
    w_copy.start()
    hid_copy.start()

    barrier = pltpu.get_barrier_semaphore()
    others = [
        (lemma_step, grp_step)
        for lemma_step in range(lemma_axis)
        for grp_step in range(group_axis)
        if lemma_step or grp_step
    ]
    for lemma_step, grp_step in others:
        pl.semaphore_signal(
            barrier, inc=1, device_id_type=MESH,
            device_id=(lax.rem(me + lemma_step, lemma_axis), grp_peer(grp_step)),
        )

    emb_copy.wait()
    tokens = emb[...].astype(jnp.float32)
    token_scale = lax.rsqrt(
        jnp.mean(tokens * tokens, axis=1, keepdims=True) + norm_eps
    ) / math.sqrt(proj_width)
    keys[chip, core] = (tokens * token_scale).astype(jnp.bfloat16)
    w_copy.wait()
    pl.semaphore_wait(barrier, len(others))

    my_half = pl.ds(pl.multiple_of(core * hrows, hrows), hrows)
    w_out = []
    for step in range(1, group_axis):
        src = w_all.at[grp, my_half]
        copy = remote(src, src, w_send.at[step], w_recv.at[step], me, grp_peer(step))
        copy.start()
        w_out.append(copy)
    k_out = []
    for step in reversed(range(1, chips)):
        copy = remote(
            keys.at[chip, core], keys.at[chip, core], k_send.at[step], k_recv.at[step], chip_peer(step), grp
        )
        copy.start()
        k_out.append(copy)
    kf_out = [remote(keys.at[chip, core], keys.at[chip, core], kf_send.at[0], kf_recv.at[0], pair, grp)]
    kf_out[0].start()

    chip_tok = 2 * block_tok
    token_of = lax.broadcasted_iota(
        jnp.int32, (chip_tok, lemmas_all), 0
    ) - lemma_tok * lax.broadcasted_iota(jnp.int32, (chip_tok, lemmas_all), 1)
    token_of_t = lax.broadcasted_iota(
        jnp.int32, (lemmas_all, chip_tok), 1
    ) - lemma_tok * lax.broadcasted_iota(jnp.int32, (lemmas_all, chip_tok), 0)
    lengths = jnp.minimum(len_ref[...].reshape(1, lemmas_all), lemma_tok)
    lengths_t = jnp.broadcast_to(
        lengths.astype(jnp.float32), (lemmas_all, lemmas_all)
    ).T[:, :1].astype(jnp.int32)
    for block in range(chips):
        first = -block * chip_tok
        member = (token_of >= first) & (token_of < lengths + first)
        live[block] = jnp.where(member, 1.0, 0.0).astype(jnp.bfloat16)
        member = (token_of_t >= first) & (token_of_t < lengths_t + first)
        live_t[block] = jnp.where(member, 1.0, 0.0).astype(jnp.bfloat16)

    hid_copy.wait()
    in_float = hid[...].astype(jnp.float32)
    inv_rms = lax.rsqrt(jnp.mean(in_float * in_float, axis=1, keepdims=True) + norm_eps)
    scaled = (in_float * inv_rms * gain_row).astype(jnp.bfloat16)
    scaled_b[...] = scaled
    scaled_rows = scaled.T
    piece = wrows // lemma_axis
    for group in range(group_axis):
        for owner in range(lemma_axis):
            start = group * wrows + owner * piece
            scaled_t[owner // 2, owner % 2, group] = scaled_rows[start : start + piece]

    own_gain = gain_ref[pl.ds(pl.multiple_of(grp * wrows, 128), wrows)].reshape(1, wrows)
    gain_col = jnp.broadcast_to(own_gain, (proj_width, wrows)).T
    over_gain[...] = (w_all[grp].astype(jnp.float32) / gain_col).reshape(over_gain.shape)

    wf_out = []
    for step in range(1, group_axis):
        dst = w_all.at[grp_from(step), my_half]
        remote(dst, dst, w_send.at[step], w_recv.at[step], me, grp_peer(step)).wait_recv()
        copy = remote(dst, dst, wf_send.at[step], wf_recv.at[step], pair, grp)
        copy.start()
        wf_out.append(copy)
    other_half = pl.ds(pl.multiple_of((1 - core) * hrows, hrows), hrows)
    for step in range(1, group_axis):
        dst = w_all.at[grp_from(step), other_half]
        remote(dst, dst, wf_send.at[step], wf_recv.at[step], pair, grp).wait_recv()

    weight = w_all[...].reshape(width, proj_width)
    projected = jnp.dot(scaled_b[...], weight, preferred_element_type=jnp.float32)
    proj_scale = lax.rsqrt(
        jnp.mean(projected * projected, axis=1, keepdims=True) + norm_eps
    ) / math.sqrt(proj_width)
    query_unit = (projected * proj_scale).astype(jnp.bfloat16)

    def first_pass(block, total):
        scores = lax.dot_general(
            query_unit, keys[block].reshape(chip_tok, proj_width), NT, preferred_element_type=jnp.float32
        )
        exp_terms = jnp.exp(scores * (1.0 / token_temp)).astype(jnp.bfloat16)
        powers_b[block] = exp_terms
        return total + jnp.dot(exp_terms, live[block], preferred_element_type=jnp.float32)

    def forward(step):
        dst = keys.at[chip_source(step), core]
        remote(dst, dst, k_send.at[step], k_recv.at[step], chip_peer(step), grp).wait_recv()
        copy = remote(dst, dst, kf_send.at[step], kf_recv.at[step], pair, grp)
        copy.start()
        kf_out.append(copy)

    def chip_pass(step, total):
        source = chip_source(step)
        dst = keys.at[source, 1 - core]
        remote(dst, dst, kf_send.at[step], kf_recv.at[step], pair, grp).wait_recv()
        return first_pass(source, total)

    total = chip_pass(0, jnp.zeros((rows, lemmas_all), jnp.float32))
    for step in range(1, chips):
        forward(step)
        if step > 1:
            total = chip_pass(step - 1, total)
    total = chip_pass(chips - 1, total)

    tok_lse = token_temp * jnp.log(total)
    first_state = (me * group_axis + grp) * states_dev
    ratios = []
    losses = jnp.zeros((1, 128), jnp.float32)
    lane = lax.broadcasted_iota(jnp.int32, (1, 128), 1)
    for state in range(states_dev):
        length = qlen_ref[first_state + state]
        target = pos_ref[first_state + state]
        length_f = jnp.full((1, lemmas_all), length, jnp.int32).astype(jnp.float32)
        span = slice(state * query_tok, (state + 1) * query_tok)
        row_ids = lax.broadcasted_iota(jnp.int32, (query_tok, lemmas_all), 0)
        live_rows = jnp.where(row_ids < length, 1.0, 0.0)
        similarity = jnp.sum(tok_lse[span] * live_rows, axis=0, keepdims=True) / length_f
        powers = jnp.exp(similarity / state_temp)
        lemma_ids = lax.broadcasted_iota(jnp.int32, (1, lemmas_all), 1)
        is_positive = jnp.where(lemma_ids == target, 1.0, 0.0)
        partition = jnp.sum(powers, axis=1, keepdims=True)
        pos_score = jnp.sum(similarity * is_positive, axis=1, keepdims=True)
        loss = jnp.log(partition) - pos_score / state_temp
        losses = jnp.where(lane == state, loss, losses)
        grad_sim = loss_scale * (powers / partition - is_positive) / state_temp
        ratios.append(live_rows * (grad_sim / length_f) / total[span])
    loss_ref[...] = losses
    ratio = jnp.concatenate(ratios, axis=0).astype(jnp.bfloat16)

    unit_grad = jnp.zeros((rows, proj_width), jnp.float32)
    for block in range(chips):
        spread = jnp.dot(ratio, live_t[block], preferred_element_type=jnp.float32)
        coef = (powers_b[block].astype(jnp.float32) * spread).astype(jnp.bfloat16)
        unit_grad += jnp.dot(
            coef, keys[block].reshape(chip_tok, proj_width), preferred_element_type=jnp.float32
        )
    proj_grad = proj_scale * unit_grad - projected * (
        proj_scale * proj_scale * proj_scale
    ) * jnp.sum(projected * unit_grad, axis=1, keepdims=True)
    proj_grad_b = proj_grad.astype(jnp.bfloat16)

    def weight_part(target, side):
        left = scaled_t[target, side].reshape(group_axis * piece, rows)
        return jnp.dot(left, proj_grad_b, preferred_element_type=jnp.float32).reshape(
            group_axis, piece, proj_width
        )

    order = list(reversed(range(chips)))
    p_out = []
    for step in order:
        part[step] = weight_part(chip_to(step), 1 - core).astype(jnp.bfloat16)
        copy = remote(part.at[step], pair_in.at[step], p_send.at[step], p_recv.at[step], pair, grp)
        copy.start()
        p_out.append(copy)
    grp_order = list(reversed(range(group_axis)))
    c_out = {}
    for step, pair_copy in zip(order, p_out):
        mine = weight_part(chip_to(step), core)
        pair_copy.wait_recv()
        half[step] = (mine + pair_in[step].astype(jnp.float32)).astype(jnp.bfloat16)
        if step:
            for grp_step in grp_order:
                copy = remote(
                    half.at[step, grp_peer(grp_step)], chip_in.at[step - 1, grp_step],
                    c_send.at[step - 1, grp_step], c_recv.at[step - 1, grp_step],
                    chip_peer(step), grp,
                )
                copy.start()
                c_out[step, grp_step] = copy

    row_dot = jnp.sum(projected * proj_grad_b.astype(jnp.float32), axis=1, keepdims=True)
    row_scale = inv_rms * inv_rms * row_dot / width

    def hidden_part(state):
        span = slice(state * query_tok, (state + 1) * query_tok)
        scaled_grad = lax.dot_general(
            proj_grad_b[span], w_all[...].reshape(width, proj_width), NT,
            preferred_element_type=jnp.float32,
        )
        hout[span] = (
            inv_rms[span] * (scaled_grad * gain_row)
            - hid[span].astype(jnp.float32) * row_scale[span]
        ).astype(jnp.bfloat16)
        copy = pltpu.make_async_copy(hout.at[span], hgrad_ref.at[span], local_sem.at[3 + state])
        copy.start()
        return copy

    hout_copies = [hidden_part(0)]

    g_out = []
    for grp_step in grp_order:
        chip_sum = half[0, grp_peer(grp_step)].astype(jnp.float32)
        for step in range(1, chips):
            c_out[step, grp_step].wait_recv()
            chip_sum += chip_in[step - 1, grp_step].astype(jnp.float32)
        if grp_step:
            quarter[grp_step] = chip_sum.astype(jnp.bfloat16)
            copy = remote(
                quarter.at[grp_step], grp_in.at[grp_step - 1],
                g_send.at[grp_step], g_recv.at[grp_step], me, grp_peer(grp_step),
            )
            copy.start()
            g_out.append(copy)
        else:
            grp_sum = chip_sum
    hout_copies += [hidden_part(state) for state in range(1, states_dev)]
    for copy in g_out:
        copy.wait_recv()
    for step in range(1, group_axis):
        grp_sum += grp_in[step - 1].astype(jnp.float32)
    own_raw = grp_sum.astype(jnp.bfloat16)
    raw[me] = own_raw
    a_out = []
    for step in range(1, lemma_axis):
        copy = remote(
            raw.at[me], raw.at[me], a_send.at[step], a_recv.at[step],
            lax.rem(me + step, lemma_axis), grp,
        )
        copy.start()
        a_out.append(copy)
    own_raw = own_raw.astype(jnp.float32)
    own_gain_raw = jnp.sum(own_raw * over_gain[me], axis=1, keepdims=True)
    squares = jnp.sum(own_raw * own_raw) + jnp.sum(own_gain_raw * own_gain_raw)
    my_sq = sq.at[grp * lemma_axis + me]
    my_sq[...] = jnp.full((1, 128), squares, jnp.float32)
    for lemma_step, grp_step in others:
        copy = remote(
            my_sq, my_sq, s_send, s_recv,
            lax.rem(me + lemma_step, lemma_axis), grp_peer(grp_step),
        )
        copy.start()
    for step in range(1, lemma_axis):
        dst = raw.at[lax.rem(me + lemma_axis - step, lemma_axis)]
        remote(dst, dst, a_send.at[step], a_recv.at[step], pair, grp).wait_recv()

    weight_raw = raw[...].reshape(wrows, proj_width).astype(jnp.float32)
    ones = jnp.ones((8, proj_width), jnp.float32)
    gain_raw = lax.dot_general(
        ones, over_gain[...].reshape(wrows, proj_width) * weight_raw, NT,
        preferred_element_type=jnp.float32, precision=lax.Precision.HIGHEST,
    )[:1]
    all_but_one = sq.at[pl.ds(0, len(others))]
    remote(all_but_one, all_but_one, s_send, s_recv, pair, grp).wait()
    squares_all = jnp.sum(sq[...], axis=0)
    factor = jnp.minimum(1.0, grad_limit / jnp.sqrt(squares_all + norm_eps))
    wgrad_ref[...] = weight_raw * factor
    ggrad_ref[...] = gain_raw * factor[:, :1]

    for copy in w_out + k_out + wf_out + kf_out + p_out + list(c_out.values()) + g_out + a_out:
        copy.wait_send()
    for copy in hout_copies:
        copy.wait()


def place_kernel(
    loss, hgrad, wgrad, ggrad, loss_out, hgrad_out, wgrad_out, ggrad_out,
    loss_in, hbuf, wbuf, ggrad_in, loss_row, ggrad_row, sems,
):
    pairs = [(hgrad, hbuf), (wgrad, wbuf), (loss, loss_in), (ggrad, ggrad_in)]
    copies = [pltpu.make_async_copy(a, b, sems.at[i]) for i, (a, b) in enumerate(pairs)]
    for copy in copies:
        copy.start()
    pairs = [(hbuf, hgrad_out), (wbuf, wgrad_out), (loss_row, loss_out), (ggrad_row, ggrad_out)]
    backs = [pltpu.make_async_copy(a, b, sems.at[4 + i]) for i, (a, b) in enumerate(pairs)]
    copies[0].wait()
    backs[0].start()
    copies[1].wait()
    backs[1].start()
    copies[2].wait()
    loss_row[...] = loss_in[0, : loss_row.shape[0]]
    backs[2].start()
    copies[3].wait()
    ggrad_row[...] = ggrad_in[...].reshape(ggrad_row.shape)
    backs[3].start()
    for copy in backs:
        copy.wait()


def fused_body(hidden, gain, weight, lemma_emb, lemma_len, query_len, positive):
    states_dev, query_tok, width = hidden.shape
    wrows, proj_width = weight.shape
    lemma_dev, lemma_tok = lemma_emb.shape[:2]
    lemma_axis, group_axis = lax.axis_size("lemma"), lax.axis_size("grp")
    chips = lemma_axis // 2
    rows, block_tok = states_dev * query_tok, lemma_dev * lemma_tok
    piece = wrows // lemma_axis
    lemmas_all = lemma_dev * lemma_axis
    vmem = pl.BlockSpec(memory_space=pltpu.VMEM)
    smem = pl.BlockSpec(memory_space=pltpu.SMEM)
    hbm = pl.BlockSpec(memory_space=pltpu.HBM)
    sem = pltpu.SemaphoreType.DMA
    bf16, f32 = jnp.bfloat16, jnp.float32
    outs = pl.pallas_call(
        functools.partial(
            fused_kernel, lemma_axis, group_axis, lemma_dev, lemma_tok, states_dev, query_tok
        ),
        out_shape=(
            jax.ShapeDtypeStruct((1, 128), f32),
            jax.ShapeDtypeStruct((rows, width), bf16),
            jax.ShapeDtypeStruct((wrows, proj_width), f32),
            jax.ShapeDtypeStruct((1, wrows), f32),
        ),
        in_specs=[hbm, vmem, hbm, hbm, vmem, smem, smem],
        out_specs=(vmem, hbm, vmem, vmem),
        scratch_shapes=[
            pltpu.VMEM((rows, width), bf16),
            pltpu.VMEM((block_tok, proj_width), bf16),
            pltpu.VMEM((rows, width), bf16),
            pltpu.VMEM((group_axis, wrows, proj_width), bf16),
            pltpu.VMEM((chips, 2, block_tok, proj_width), bf16),
            pltpu.VMEM((chips, 2 * block_tok, lemmas_all), bf16),
            pltpu.VMEM((chips, lemmas_all, 2 * block_tok), bf16),
            pltpu.VMEM((chips, rows, 2 * block_tok), bf16),
            pltpu.VMEM((rows, width), bf16),
            pltpu.VMEM((chips, 2, group_axis, piece, rows), bf16),
            pltpu.VMEM((chips, group_axis, piece, proj_width), bf16),
            pltpu.VMEM((chips, group_axis, piece, proj_width), bf16),
            pltpu.VMEM((chips, group_axis, piece, proj_width), bf16),
            pltpu.VMEM((chips - 1, group_axis, piece, proj_width), bf16),
            pltpu.VMEM((group_axis, piece, proj_width), bf16),
            pltpu.VMEM((group_axis - 1, piece, proj_width), bf16),
            pltpu.VMEM((lemma_axis, piece, proj_width), bf16),
            pltpu.VMEM((group_axis * lemma_axis, 1, 128), f32),
            pltpu.VMEM((lemma_axis, piece, proj_width), f32),
            sem((3 + states_dev,)),
            sem((group_axis,)), sem((group_axis,)), sem((group_axis,)), sem((group_axis,)),
            sem((chips,)), sem((chips,)), sem((chips,)), sem((chips,)),
            sem((chips,)), sem((chips,)),
            sem((chips - 1, group_axis)), sem((chips - 1, group_axis)),
            sem((group_axis,)), sem((group_axis,)),
            sem((lemma_axis,)), sem((lemma_axis,)),
            sem, sem,
        ],
        compiler_params=pltpu.CompilerParams(
            collective_id=0, has_side_effects=True, vmem_limit_bytes=62 * 1024 * 1024
        ),
        cost_estimate=pl.CostEstimate(
            flops=2 * rows * proj_width * (3 * width + 4 * block_tok * lemma_axis),
            bytes_accessed=4 * rows * width * 2,
            transcendentals=rows * block_tok * lemma_axis,
        ),
    )(
        hidden.reshape(rows, width), gain, weight,
        lemma_emb.reshape(block_tok, proj_width), lemma_len,
        query_len, positive,
    )
    loss, hidden_grad, weight_grad, gain_grad = pl.pallas_call(
        place_kernel,
        out_shape=(
            jax.ShapeDtypeStruct((states_dev,), f32),
            jax.ShapeDtypeStruct((rows, width), bf16),
            jax.ShapeDtypeStruct((wrows, proj_width), f32),
            jax.ShapeDtypeStruct((wrows,), f32),
        ),
        in_specs=[hbm] * 4,
        out_specs=(hbm,) * 4,
        scratch_shapes=[
            pltpu.VMEM((1, 128), f32),
            pltpu.VMEM((rows, width), bf16),
            pltpu.VMEM((wrows, proj_width), f32),
            pltpu.VMEM((1, wrows), f32),
            pltpu.VMEM((states_dev,), f32),
            pltpu.VMEM((wrows,), f32),
            sem((8,)),
        ],
        compiler_params=pltpu.CompilerParams(vmem_limit_bytes=62 * 1024 * 1024),
    )(*outs)
    return (loss, hidden_grad.reshape(hidden.shape), weight_grad, gain_grad)


def solution(mesh):
    in_specs = (
        P(("lemma", "grp"), None, None),
        P(),
        P("grp", None),
        P("lemma", None, None),
        P(),
        P(),
        P(),
    )
    out_specs = (P(("lemma", "grp")), P(("lemma", "grp"), None, None), P("grp", None), P("grp"))

    def run(hidden, gain, weight, *rest):
        rows = weight.shape[0] // mesh.shape["grp"]
        tiled = rows % (16 * mesh.shape["lemma"]) == 0 and rows % 128 == 0
        chosen = fused_body if tiled else body
        return jax.shard_map(
            chosen, mesh=mesh, in_specs=in_specs, out_specs=out_specs, check_vma=False
        )(hidden, gain, weight, *rest)

    return run
```

```python
import functools
import math

import jax
import jax.numpy as jnp
from jax import lax
from jax.experimental import pallas as pl
from jax.experimental.pallas import tpu as pltpu
from jax.sharding import PartitionSpec as P

token_temp = 0.05
state_temp = 0.05
loss_scale = 1024.0
grad_limit = 400.0
norm_eps = 1e-06


def contract_last(left, right):
    return lax.dot_general(
        left, right, (((1,), (1,)), ((), ())), preferred_element_type=jnp.float32
    )


def unit_rows(values):
    scale_rows = lax.rsqrt(jnp.mean(values * values, axis=-1, keepdims=True) + norm_eps)
    return values * scale_rows / math.sqrt(values.shape[-1])


def lemma_terms(queries, keys, key_live, lemma_count, lemma_tok):
    scores = contract_last(queries, keys)
    exp_terms = jnp.exp(scores / token_temp) * key_live[None, :]
    per_lemma = jnp.sum(exp_terms.reshape(queries.shape[0], lemma_count, lemma_tok), axis=2)
    return (exp_terms, per_lemma)


def token_grads(queries, grads, keys, key_live, lemma_count, lemma_tok):
    exp_terms, per_lemma = lemma_terms(queries, keys, key_live, lemma_count, lemma_tok)
    rows = queries.shape[0]
    weights = exp_terms.reshape(rows, lemma_count, lemma_tok) / per_lemma[:, :, None]
    coef = (weights * grads[:, :, None]).reshape(rows, lemma_count * lemma_tok).astype(jnp.bfloat16)
    return jnp.dot(coef, keys, preferred_element_type=jnp.float32)


def state_loss(tok_lse, live_rows, lengths_f, targets, lemma_ids):
    states = live_rows.shape[0]
    similarity = (
        jnp.sum(tok_lse.reshape(states, live_rows.shape[1], -1) * live_rows[:, :, None], axis=1)
        / lengths_f[:, None]
    )
    powers = jnp.exp(similarity / state_temp)
    is_positive = (lemma_ids[None, :] == targets[:, None]).astype(jnp.float32)
    return (similarity, powers, is_positive)


def body(hidden, gain, weight, lemma_emb, lemma_len, query_len, positive):
    states_dev, query_tok, width = hidden.shape
    proj_width = weight.shape[1]
    lemma_dev, lemma_tok = (lemma_emb.shape[0], lemma_emb.shape[1])
    lemma_axis = lax.axis_size("lemma")
    group_axis = lax.axis_size("grp")
    lemma_idx = lax.axis_index("lemma")
    group_idx = lax.axis_index("grp")
    own_rows = states_dev * query_tok
    lemmas_all = lemma_dev * lemma_axis
    in_float = hidden.reshape(own_rows, width).astype(jnp.float32)
    inv_rms = lax.rsqrt(jnp.mean(in_float * in_float, axis=1, keepdims=True) + norm_eps)
    normed = in_float * inv_rms
    scaled = (normed * gain[None, :]).astype(jnp.bfloat16)
    projected = jnp.dot(
        scaled,
        lax.all_gather(weight, "grp", axis=0, tiled=True),
        preferred_element_type=jnp.float32,
    )
    proj_scale = lax.rsqrt(
        jnp.mean(projected * projected, axis=1, keepdims=True) + norm_eps
    ) / math.sqrt(proj_width)
    query_unit = (projected * proj_scale).astype(jnp.bfloat16)
    lemma_unit = unit_rows(lemma_emb.astype(jnp.float32).reshape(-1, proj_width)).astype(
        jnp.bfloat16
    )
    all_live = (jnp.arange(lemma_tok)[None, :] < lemma_len[:, None]).astype(jnp.float32)
    block_start = (lemma_idx * group_axis + group_idx) * states_dev
    all_keys = lax.all_gather(lemma_unit, "lemma", axis=0, tiled=True)
    block_count = 8
    block_lemmas = lemmas_all // block_count
    key_blocks = all_keys.reshape(block_count, block_lemmas * lemma_tok, proj_width)
    live_blocks = all_live.reshape(block_count, block_lemmas * lemma_tok)
    own_len = lax.dynamic_slice_in_dim(query_len, block_start, states_dev)
    own_pos = lax.dynamic_slice_in_dim(positive, block_start, states_dev)
    live_rows = (jnp.arange(query_tok)[None, :] < own_len[:, None]).astype(jnp.float32)
    lengths_f = own_len.astype(jnp.float32)

    def block_lse(items):
        keys, key_live = items
        exp_terms, per_lemma = lemma_terms(query_unit, keys, key_live, block_lemmas, lemma_tok)
        return token_temp * jnp.log(per_lemma)

    tok_lse = lax.map(block_lse, (key_blocks, live_blocks))
    tok_lse = jnp.moveaxis(tok_lse, 0, 1).reshape(own_rows, lemmas_all)
    similarity, powers, is_positive = state_loss(
        tok_lse, live_rows, lengths_f, own_pos, jnp.arange(lemmas_all)
    )
    partition = jnp.sum(powers, axis=1)
    pos_score = jnp.sum(similarity * is_positive, axis=1)
    loss = jnp.log(partition) - pos_score / state_temp
    grad_sim = loss_scale * (powers / partition[:, None] - is_positive) / state_temp
    tok_grad = (grad_sim[:, None, :] * live_rows[:, :, None] / lengths_f[:, None, None]).reshape(
        own_rows, block_count, block_lemmas
    )
    grad_blocks = jnp.moveaxis(tok_grad, 1, 0)

    def add_block(acc, items):
        keys, key_live, grads = items
        return (acc + token_grads(query_unit, grads, keys, key_live, block_lemmas, lemma_tok), None)

    unit_grad, unused = lax.scan(
        add_block,
        jnp.zeros((own_rows, proj_width), jnp.float32),
        (key_blocks, live_blocks, grad_blocks),
    )
    proj_grad = proj_scale * unit_grad - projected * proj_scale**3 * jnp.sum(
        projected * unit_grad, axis=1, keepdims=True
    )
    proj_grad_b = proj_grad.astype(jnp.bfloat16)
    scaled_grad = contract_last(proj_grad_b, lax.all_gather(weight, "grp", axis=0, tiled=True))
    normed_grad = scaled_grad * gain[None, :]
    input_grad = (
        inv_rms * normed_grad
        - in_float * inv_rms**3 * jnp.sum(in_float * normed_grad, axis=1, keepdims=True) / width
    )
    hidden_grad = input_grad.astype(jnp.bfloat16).reshape(states_dev, query_tok, width)
    weight_part = lax.dot_general(
        scaled, proj_grad_b, (((0,), (0,)), ((), ())), preferred_element_type=jnp.float32
    )
    gain_part = jnp.sum(scaled_grad * normed, axis=0)
    weight_sum, gain_sum = (
        lax.psum(weight_part.astype(jnp.bfloat16), "lemma").astype(jnp.float32),
        lax.psum(gain_part.astype(jnp.bfloat16), "lemma").astype(jnp.float32),
    )
    weight_sum, gain_sum = (
        lax.psum_scatter(
            weight_sum.astype(jnp.bfloat16), "grp", scatter_dimension=0, tiled=True
        ).astype(jnp.float32),
        lax.psum_scatter(
            gain_sum.astype(jnp.bfloat16), "grp", scatter_dimension=0, tiled=True
        ).astype(jnp.float32),
    )
    squares = jnp.sum(weight_sum * weight_sum) + jnp.sum(gain_sum * gain_sum)
    total_squares = lax.psum(squares, "grp")
    factor = jnp.minimum(1.0, grad_limit / jnp.sqrt(total_squares + norm_eps))
    return (loss, hidden_grad, weight_sum * factor, gain_sum * factor)


NT = (((1,), (1,)), ((), ()))
MESH = pl.DeviceIdType.MESH


def fused_kernel(
    lemma_axis, group_axis, lemma_dev, lemma_tok, states_dev, query_tok,
    hidden_ref, gain_ref, weight_ref, emb_ref, len_ref, qlen_ref, pos_ref,
    loss_ref, hgrad_ref, wgrad_ref, ggrad_ref,
    hid, emb, hout, w_all, keys, live, live_t, powers_b, scaled_b, scaled_t,
    part, pair_in, half, chip_in, quarter, grp_in, raw, sq, over_gain,
    local_sem, w_send, w_recv, wf_send, wf_recv, k_send, k_recv, kf_send, kf_recv,
    p_send, p_recv, c_send, c_recv, g_send, g_recv, a_send, a_recv, s_send, s_recv,
):
    chips = lemma_axis // 2
    me, grp = lax.axis_index("lemma"), lax.axis_index("grp")
    chip, core = me // 2, lax.rem(me, 2)
    pair = chip * 2 + (1 - core)
    rows, width = hid.shape
    proj_width = weight_ref.shape[1]
    wrows = weight_ref.shape[0]
    hrows = wrows // 2
    block_tok = lemma_dev * lemma_tok
    lemmas_all = lemma_dev * lemma_axis

    across = 2 - chips % 2
    along = chips // across
    chip_y, chip_x = chip // across, lax.rem(chip, across)

    def split(step):
        if isinstance(step, int):
            return step // across, step % across
        return lax.div(step, across), lax.rem(step, across)

    def chip_to(step):
        step_y, step_x = split(step)
        return lax.rem(chip_y + step_y, along) * across + lax.rem(chip_x + step_x, across)

    def chip_source(step):
        step_y, step_x = split(step)
        return lax.rem(chip_y + along - step_y, along) * across + lax.rem(
            chip_x + across - step_x, across
        )

    def chip_peer(step):
        return chip_to(step) * 2 + core

    def chip_from(step):
        return chip_source(step) * 2 + core

    def grp_peer(step):
        return lax.rem(grp + step, group_axis)

    def grp_from(step):
        return lax.rem(grp + group_axis - step, group_axis)

    def remote(src, dst, send_sem, recv_sem, to_lemma, to_grp):
        return pltpu.make_async_remote_copy(
            src_ref=src, dst_ref=dst, send_sem=send_sem, recv_sem=recv_sem,
            device_id=(to_lemma, to_grp), device_id_type=MESH,
        )

    emb_copy = pltpu.make_async_copy(emb_ref, emb, local_sem.at[0])
    hid_copy = pltpu.make_async_copy(hidden_ref, hid, local_sem.at[1])
    w_copy = pltpu.make_async_copy(weight_ref, w_all.at[grp], local_sem.at[2])
    emb_copy.start()
    w_copy.start()
    hid_copy.start()

    barrier = pltpu.get_barrier_semaphore()
    others = [
        (lemma_step, grp_step)
        for lemma_step in range(lemma_axis)
        for grp_step in range(group_axis)
        if lemma_step or grp_step
    ]
    for lemma_step, grp_step in others:
        pl.semaphore_signal(
            barrier, inc=1, device_id_type=MESH,
            device_id=(lax.rem(me + lemma_step, lemma_axis), grp_peer(grp_step)),
        )

    emb_copy.wait()
    tokens = emb[...].astype(jnp.float32)
    token_scale = lax.rsqrt(
        jnp.mean(tokens * tokens, axis=1, keepdims=True) + norm_eps
    ) / math.sqrt(proj_width)
    keys[chip, core] = (tokens * token_scale).astype(jnp.bfloat16)
    w_copy.wait()
    pl.semaphore_wait(barrier, len(others))

    my_half = pl.ds(pl.multiple_of(core * hrows, hrows), hrows)
    w_out = []
    for step in range(1, group_axis):
        src = w_all.at[grp, my_half]
        copy = remote(src, src, w_send.at[step], w_recv.at[step], me, grp_peer(step))
        copy.start()
        w_out.append(copy)
    k_out = []
    for step in reversed(range(1, chips)):
        copy = remote(
            keys.at[chip, core], keys.at[chip, core], k_send.at[step], k_recv.at[step], chip_peer(step), grp
        )
        copy.start()
        k_out.append(copy)
    kf_out = [remote(keys.at[chip, core], keys.at[chip, core], kf_send.at[0], kf_recv.at[0], pair, grp)]
    kf_out[0].start()

    chip_tok = 2 * block_tok
    token_of = lax.broadcasted_iota(
        jnp.int32, (chip_tok, lemmas_all), 0
    ) - lemma_tok * lax.broadcasted_iota(jnp.int32, (chip_tok, lemmas_all), 1)
    token_of_t = lax.broadcasted_iota(
        jnp.int32, (lemmas_all, chip_tok), 1
    ) - lemma_tok * lax.broadcasted_iota(jnp.int32, (lemmas_all, chip_tok), 0)
    lengths = jnp.minimum(len_ref[...].reshape(1, lemmas_all), lemma_tok)
    lengths_t = jnp.broadcast_to(
        lengths.astype(jnp.float32), (lemmas_all, lemmas_all)
    ).T[:, :1].astype(jnp.int32)
    @pl.loop(0, chips)
    def _(block):
        first = -block * chip_tok
        member = (token_of >= first) & (token_of < lengths + first)
        live[block] = jnp.where(member, 1.0, 0.0).astype(jnp.bfloat16)
        member = (token_of_t >= first) & (token_of_t < lengths_t + first)
        live_t[block] = jnp.where(member, 1.0, 0.0).astype(jnp.bfloat16)

    hid_copy.wait()
    piece = wrows // lemma_axis

    def group_cols(group):
        return pl.ds(pl.multiple_of(group * wrows, 128), wrows)

    def add_squares(group, acc):
        in_float = hid[:, group_cols(group)].astype(jnp.float32)
        return acc + jnp.sum(in_float * in_float, axis=1, keepdims=True)

    mean_sq = lax.fori_loop(0, group_axis, add_squares, jnp.zeros((rows, 1), jnp.float32)) / width
    inv_rms = lax.rsqrt(mean_sq + norm_eps)

    @pl.loop(0, group_axis)
    def _(group):
        cols = group_cols(group)
        in_float = hid[:, cols].astype(jnp.float32)
        scaled = (in_float * inv_rms * gain_ref[cols].reshape(1, wrows)).astype(jnp.bfloat16)
        scaled_b[group] = scaled
        scaled_rows = scaled.T
        for owner in range(lemma_axis):
            scaled_t[owner // 2, owner % 2, group] = scaled_rows[
                owner * piece : (owner + 1) * piece
            ]

    own_gain = gain_ref[pl.ds(pl.multiple_of(grp * wrows, 128), wrows)].reshape(1, wrows)
    gain_col = jnp.broadcast_to(own_gain, (proj_width, wrows)).T
    over_gain[...] = (w_all[grp].astype(jnp.float32) / gain_col).reshape(over_gain.shape)

    wf_out = []
    for step in range(1, group_axis):
        dst = w_all.at[grp_from(step), my_half]
        remote(dst, dst, w_send.at[step], w_recv.at[step], me, grp_peer(step)).wait_recv()
        copy = remote(dst, dst, wf_send.at[step], wf_recv.at[step], pair, grp)
        copy.start()
        wf_out.append(copy)
    other_half = pl.ds(pl.multiple_of((1 - core) * hrows, hrows), hrows)
    for step in range(1, group_axis):
        dst = w_all.at[grp_from(step), other_half]
        remote(dst, dst, wf_send.at[step], wf_recv.at[step], pair, grp).wait_recv()

    def project(group, acc):
        return acc + jnp.dot(scaled_b[group], w_all[group], preferred_element_type=jnp.float32)

    projected = lax.fori_loop(
        0, group_axis, project, jnp.zeros((rows, proj_width), jnp.float32)
    )
    proj_scale = lax.rsqrt(
        jnp.mean(projected * projected, axis=1, keepdims=True) + norm_eps
    ) / math.sqrt(proj_width)
    query_unit = (projected * proj_scale).astype(jnp.bfloat16)

    def first_pass(block, total):
        scores = lax.dot_general(
            query_unit, keys[block].reshape(chip_tok, proj_width), NT, preferred_element_type=jnp.float32
        )
        exp_terms = jnp.exp(scores * (1.0 / token_temp)).astype(jnp.bfloat16)
        powers_b[block] = exp_terms
        return total + jnp.dot(exp_terms, live[block], preferred_element_type=jnp.float32)

    def forward(step):
        dst = keys.at[chip_source(step), core]
        remote(dst, dst, k_send.at[step], k_recv.at[step], chip_peer(step), grp).wait_recv()
        remote(dst, dst, kf_send.at[step], kf_recv.at[step], pair, grp).start()

    def chip_pass(step, total):
        @pl.when(step + 1 < chips)
        def _():
            forward(step + 1)

        source = chip_source(step)
        dst = keys.at[source, 1 - core]
        remote(dst, dst, kf_send.at[step], kf_recv.at[step], pair, grp).wait_recv()
        return first_pass(source, total)

    total = lax.fori_loop(0, chips, chip_pass, jnp.zeros((rows, lemmas_all), jnp.float32))

    tok_lse = token_temp * jnp.log(total)
    first_state = (me * group_axis + grp) * states_dev
    ratios = []
    losses = jnp.zeros((1, 128), jnp.float32)
    lane = lax.broadcasted_iota(jnp.int32, (1, 128), 1)
    for state in range(states_dev):
        length = qlen_ref[first_state + state]
        target = pos_ref[first_state + state]
        length_f = jnp.full((1, lemmas_all), length, jnp.int32).astype(jnp.float32)
        span = slice(state * query_tok, (state + 1) * query_tok)
        row_ids = lax.broadcasted_iota(jnp.int32, (query_tok, lemmas_all), 0)
        live_rows = jnp.where(row_ids < length, 1.0, 0.0)
        similarity = jnp.sum(tok_lse[span] * live_rows, axis=0, keepdims=True) / length_f
        powers = jnp.exp(similarity / state_temp)
        lemma_ids = lax.broadcasted_iota(jnp.int32, (1, lemmas_all), 1)
        is_positive = jnp.where(lemma_ids == target, 1.0, 0.0)
        partition = jnp.sum(powers, axis=1, keepdims=True)
        pos_score = jnp.sum(similarity * is_positive, axis=1, keepdims=True)
        loss = jnp.log(partition) - pos_score / state_temp
        losses = jnp.where(lane == state, loss, losses)
        grad_sim = loss_scale * (powers / partition - is_positive) / state_temp
        ratios.append(live_rows * (grad_sim / length_f) / total[span])
    loss_ref[...] = losses
    ratio = jnp.concatenate(ratios, axis=0).astype(jnp.bfloat16)

    def second_pass(block, acc):
        spread = jnp.dot(ratio, live_t[block], preferred_element_type=jnp.float32)
        coef = (powers_b[block].astype(jnp.float32) * spread).astype(jnp.bfloat16)
        return acc + jnp.dot(
            coef, keys[block].reshape(chip_tok, proj_width), preferred_element_type=jnp.float32
        )

    unit_grad = lax.fori_loop(0, chips, second_pass, jnp.zeros((rows, proj_width), jnp.float32))
    proj_grad = proj_scale * unit_grad - projected * (
        proj_scale * proj_scale * proj_scale
    ) * jnp.sum(projected * unit_grad, axis=1, keepdims=True)
    proj_grad_b = proj_grad.astype(jnp.bfloat16)

    def weight_part(target, side):
        left = scaled_t[target, side].reshape(group_axis * piece, rows)
        return jnp.dot(left, proj_grad_b, preferred_element_type=jnp.float32).reshape(
            group_axis, piece, proj_width
        )

    def pair_copy(step):
        return remote(
            part.at[step], pair_in.at[step], p_send.at[step], p_recv.at[step], pair, grp
        )

    def chip_copy(step, grp_step):
        return remote(
            half.at[step, grp_peer(grp_step)], chip_in.at[step - 1, grp_step],
            c_send.at[step - 1, grp_step], c_recv.at[step - 1, grp_step],
            chip_peer(step), grp,
        )

    @pl.loop(0, chips)
    def _(turn):
        step = chips - 1 - turn
        part[step] = weight_part(chip_to(step), 1 - core).astype(jnp.bfloat16)
        pair_copy(step).start()

    @pl.loop(0, chips)
    def _(turn):
        step = chips - 1 - turn
        mine = weight_part(chip_to(step), core)
        pair_copy(step).wait_recv()
        half[step] = (mine + pair_in[step].astype(jnp.float32)).astype(jnp.bfloat16)

        @pl.when(step > 0)
        def _():
            for grp_step in reversed(range(group_axis)):
                chip_copy(step, grp_step).start()

    row_dot = jnp.sum(projected * proj_grad_b.astype(jnp.float32), axis=1, keepdims=True)
    row_scale = inv_rms * inv_rms * row_dot / width

    def hidden_part(group):
        cols = group_cols(group)
        scaled_grad = lax.dot_general(
            proj_grad_b, w_all[group], NT, preferred_element_type=jnp.float32
        )
        hout[:, cols] = (
            inv_rms * (scaled_grad * gain_ref[cols].reshape(1, wrows))
            - hid[:, cols].astype(jnp.float32) * row_scale
        ).astype(jnp.bfloat16)

    pl.loop(0, group_axis // 2)(hidden_part)

    g_out = []
    for grp_step in reversed(range(group_axis)):
        chip_sum = half[0, grp_peer(grp_step)].astype(jnp.float32)
        for step in range(1, chips):
            chip_copy(step, grp_step).wait_recv()
            chip_sum += chip_in[step - 1, grp_step].astype(jnp.float32)
        if grp_step:
            quarter[grp_step] = chip_sum.astype(jnp.bfloat16)
            copy = remote(
                quarter.at[grp_step], grp_in.at[grp_step - 1],
                g_send.at[grp_step], g_recv.at[grp_step], me, grp_peer(grp_step),
            )
            copy.start()
            g_out.append(copy)
        else:
            grp_sum = chip_sum
    pl.loop(group_axis // 2, group_axis)(hidden_part)
    hout_copy = pltpu.make_async_copy(hout, hgrad_ref, local_sem.at[3])
    hout_copy.start()
    for copy in g_out:
        copy.wait_recv()
    for step in range(1, group_axis):
        grp_sum += grp_in[step - 1].astype(jnp.float32)
    own_raw = grp_sum.astype(jnp.bfloat16)
    raw[me] = own_raw
    a_out = []
    for step in range(1, lemma_axis):
        copy = remote(
            raw.at[me], raw.at[me], a_send.at[step], a_recv.at[step],
            lax.rem(me + step, lemma_axis), grp,
        )
        copy.start()
        a_out.append(copy)
    own_raw = own_raw.astype(jnp.float32)
    own_gain_raw = jnp.sum(own_raw * over_gain[me], axis=1, keepdims=True)
    squares = jnp.sum(own_raw * own_raw) + jnp.sum(own_gain_raw * own_gain_raw)
    my_sq = sq.at[grp * lemma_axis + me]
    my_sq[...] = jnp.full((1, 128), squares, jnp.float32)
    for lemma_step, grp_step in others:
        copy = remote(
            my_sq, my_sq, s_send, s_recv,
            lax.rem(me + lemma_step, lemma_axis), grp_peer(grp_step),
        )
        copy.start()
    for step in range(1, lemma_axis):
        dst = raw.at[lax.rem(me + lemma_axis - step, lemma_axis)]
        remote(dst, dst, a_send.at[step], a_recv.at[step], pair, grp).wait_recv()

    weight_raw = raw[...].reshape(wrows, proj_width).astype(jnp.float32)
    ones = jnp.ones((8, proj_width), jnp.float32)
    gain_raw = lax.dot_general(
        ones, over_gain[...].reshape(wrows, proj_width) * weight_raw, NT,
        preferred_element_type=jnp.float32, precision=lax.Precision.HIGHEST,
    )[:1]
    all_but_one = sq.at[pl.ds(0, len(others))]
    remote(all_but_one, all_but_one, s_send, s_recv, pair, grp).wait()
    squares_all = jnp.sum(sq[...], axis=0)
    factor = jnp.minimum(1.0, grad_limit / jnp.sqrt(squares_all + norm_eps))
    wgrad_ref[...] = weight_raw * factor
    ggrad_ref[...] = gain_raw * factor[:, :1]

    for copy in w_out + k_out + wf_out + kf_out + g_out + a_out:
        copy.wait_send()
    for step in range(chips):
        pair_copy(step).wait_send()
        if step:
            dst = keys.at[chip_source(step), core]
            remote(dst, dst, kf_send.at[step], kf_recv.at[step], pair, grp).wait_send()
            for grp_step in range(group_axis):
                chip_copy(step, grp_step).wait_send()
    hout_copy.wait()


def place_kernel(
    loss, hgrad, wgrad, ggrad, loss_out, hgrad_out, wgrad_out, ggrad_out,
    loss_in, hbuf, wbuf, ggrad_in, loss_row, ggrad_row, sems,
):
    pairs = [(hgrad, hbuf), (wgrad, wbuf), (loss, loss_in), (ggrad, ggrad_in)]
    copies = [pltpu.make_async_copy(a, b, sems.at[i]) for i, (a, b) in enumerate(pairs)]
    for copy in copies:
        copy.start()
    pairs = [(hbuf, hgrad_out), (wbuf, wgrad_out), (loss_row, loss_out), (ggrad_row, ggrad_out)]
    backs = [pltpu.make_async_copy(a, b, sems.at[4 + i]) for i, (a, b) in enumerate(pairs)]
    copies[0].wait()
    backs[0].start()
    copies[1].wait()
    backs[1].start()
    copies[2].wait()
    loss_row[...] = loss_in[0, : loss_row.shape[0]]
    backs[2].start()
    copies[3].wait()
    ggrad_row[...] = ggrad_in[...].reshape(ggrad_row.shape)
    backs[3].start()
    for copy in backs:
        copy.wait()


def fused_body(hidden, gain, weight, lemma_emb, lemma_len, query_len, positive):
    states_dev, query_tok, width = hidden.shape
    wrows, proj_width = weight.shape
    lemma_dev, lemma_tok = lemma_emb.shape[:2]
    lemma_axis, group_axis = lax.axis_size("lemma"), lax.axis_size("grp")
    chips = lemma_axis // 2
    rows, block_tok = states_dev * query_tok, lemma_dev * lemma_tok
    piece = wrows // lemma_axis
    lemmas_all = lemma_dev * lemma_axis
    vmem = pl.BlockSpec(memory_space=pltpu.VMEM)
    smem = pl.BlockSpec(memory_space=pltpu.SMEM)
    hbm = pl.BlockSpec(memory_space=pltpu.HBM)
    sem = pltpu.SemaphoreType.DMA
    bf16, f32 = jnp.bfloat16, jnp.float32
    outs = pl.pallas_call(
        functools.partial(
            fused_kernel, lemma_axis, group_axis, lemma_dev, lemma_tok, states_dev, query_tok
        ),
        out_shape=(
            jax.ShapeDtypeStruct((1, 128), f32),
            jax.ShapeDtypeStruct((rows, width), bf16),
            jax.ShapeDtypeStruct((wrows, proj_width), f32),
            jax.ShapeDtypeStruct((1, wrows), f32),
        ),
        in_specs=[hbm, vmem, hbm, hbm, vmem, smem, smem],
        out_specs=(vmem, hbm, vmem, vmem),
        scratch_shapes=[
            pltpu.VMEM((rows, width), bf16),
            pltpu.VMEM((block_tok, proj_width), bf16),
            pltpu.VMEM((rows, width), bf16),
            pltpu.VMEM((group_axis, wrows, proj_width), bf16),
            pltpu.VMEM((chips, 2, block_tok, proj_width), bf16),
            pltpu.VMEM((chips, 2 * block_tok, lemmas_all), bf16),
            pltpu.VMEM((chips, lemmas_all, 2 * block_tok), bf16),
            pltpu.VMEM((chips, rows, 2 * block_tok), bf16),
            pltpu.VMEM((group_axis, rows, wrows), bf16),
            pltpu.VMEM((chips, 2, group_axis, piece, rows), bf16),
            pltpu.VMEM((chips, group_axis, piece, proj_width), bf16),
            pltpu.VMEM((chips, group_axis, piece, proj_width), bf16),
            pltpu.VMEM((chips, group_axis, piece, proj_width), bf16),
            pltpu.VMEM((chips - 1, group_axis, piece, proj_width), bf16),
            pltpu.VMEM((group_axis, piece, proj_width), bf16),
            pltpu.VMEM((group_axis - 1, piece, proj_width), bf16),
            pltpu.VMEM((lemma_axis, piece, proj_width), bf16),
            pltpu.VMEM((group_axis * lemma_axis, 1, 128), f32),
            pltpu.VMEM((lemma_axis, piece, proj_width), f32),
            sem((4,)),
            sem((group_axis,)), sem((group_axis,)), sem((group_axis,)), sem((group_axis,)),
            sem((chips,)), sem((chips,)), sem((chips,)), sem((chips,)),
            sem((chips,)), sem((chips,)),
            sem((chips - 1, group_axis)), sem((chips - 1, group_axis)),
            sem((group_axis,)), sem((group_axis,)),
            sem((lemma_axis,)), sem((lemma_axis,)),
            sem, sem,
        ],
        compiler_params=pltpu.CompilerParams(
            collective_id=0, has_side_effects=True, vmem_limit_bytes=62 * 1024 * 1024
        ),
        cost_estimate=pl.CostEstimate(
            flops=2 * rows * proj_width * (3 * width + 4 * block_tok * lemma_axis),
            bytes_accessed=4 * rows * width * 2,
            transcendentals=rows * block_tok * lemma_axis,
        ),
    )(
        hidden.reshape(rows, width), gain, weight,
        lemma_emb.reshape(block_tok, proj_width), lemma_len,
        query_len, positive,
    )
    loss, hidden_grad, weight_grad, gain_grad = pl.pallas_call(
        place_kernel,
        out_shape=(
            jax.ShapeDtypeStruct((states_dev,), f32),
            jax.ShapeDtypeStruct((rows, width), bf16),
            jax.ShapeDtypeStruct((wrows, proj_width), f32),
            jax.ShapeDtypeStruct((wrows,), f32),
        ),
        in_specs=[hbm] * 4,
        out_specs=(hbm,) * 4,
        scratch_shapes=[
            pltpu.VMEM((1, 128), f32),
            pltpu.VMEM((rows, width), bf16),
            pltpu.VMEM((wrows, proj_width), f32),
            pltpu.VMEM((1, wrows), f32),
            pltpu.VMEM((states_dev,), f32),
            pltpu.VMEM((wrows,), f32),
            sem((8,)),
        ],
        compiler_params=pltpu.CompilerParams(vmem_limit_bytes=62 * 1024 * 1024),
    )(*outs)
    return (loss, hidden_grad.reshape(hidden.shape), weight_grad, gain_grad)


def solution(mesh):
    in_specs = (
        P(("lemma", "grp"), None, None),
        P(),
        P("grp", None),
        P("lemma", None, None),
        P(),
        P(),
        P(),
    )
    out_specs = (P(("lemma", "grp")), P(("lemma", "grp"), None, None), P("grp", None), P("grp"))

    def run(hidden, gain, weight, *rest):
        rows = weight.shape[0] // mesh.shape["grp"]
        tiled = rows % (16 * mesh.shape["lemma"]) == 0 and rows % 128 == 0
        chosen = fused_body if tiled else body
        return jax.shard_map(
            chosen, mesh=mesh, in_specs=in_specs, out_specs=out_specs, check_vma=False
        )(hidden, gain, weight, *rest)

    return run
```

```python
import functools
import math

import jax
import jax.numpy as jnp
from jax import lax
from jax.experimental import pallas as pl
from jax.experimental.pallas import tpu as pltpu
from jax.sharding import PartitionSpec as P

token_temp = 0.05
state_temp = 0.05
loss_scale = 1024.0
grad_limit = 400.0
norm_eps = 1e-06


def contract_last(left, right):
    return lax.dot_general(
        left, right, (((1,), (1,)), ((), ())), preferred_element_type=jnp.float32
    )


def unit_rows(values):
    scale_rows = lax.rsqrt(jnp.mean(values * values, axis=-1, keepdims=True) + norm_eps)
    return values * scale_rows / math.sqrt(values.shape[-1])


def lemma_terms(queries, keys, key_live, lemma_count, lemma_tok):
    scores = contract_last(queries, keys)
    exp_terms = jnp.exp(scores / token_temp) * key_live[None, :]
    per_lemma = jnp.sum(exp_terms.reshape(queries.shape[0], lemma_count, lemma_tok), axis=2)
    return (exp_terms, per_lemma)


def token_grads(queries, grads, keys, key_live, lemma_count, lemma_tok):
    exp_terms, per_lemma = lemma_terms(queries, keys, key_live, lemma_count, lemma_tok)
    rows = queries.shape[0]
    weights = exp_terms.reshape(rows, lemma_count, lemma_tok) / per_lemma[:, :, None]
    coef = (weights * grads[:, :, None]).reshape(rows, lemma_count * lemma_tok).astype(jnp.bfloat16)
    return jnp.dot(coef, keys, preferred_element_type=jnp.float32)


def state_loss(tok_lse, live_rows, lengths_f, targets, lemma_ids):
    states = live_rows.shape[0]
    similarity = (
        jnp.sum(tok_lse.reshape(states, live_rows.shape[1], -1) * live_rows[:, :, None], axis=1)
        / lengths_f[:, None]
    )
    powers = jnp.exp(similarity / state_temp)
    is_positive = (lemma_ids[None, :] == targets[:, None]).astype(jnp.float32)
    return (similarity, powers, is_positive)


def body(hidden, gain, weight, lemma_emb, lemma_len, query_len, positive):
    states_dev, query_tok, width = hidden.shape
    proj_width = weight.shape[1]
    lemma_dev, lemma_tok = (lemma_emb.shape[0], lemma_emb.shape[1])
    lemma_axis = lax.axis_size("lemma")
    group_axis = lax.axis_size("grp")
    lemma_idx = lax.axis_index("lemma")
    group_idx = lax.axis_index("grp")
    own_rows = states_dev * query_tok
    lemmas_all = lemma_dev * lemma_axis
    in_float = hidden.reshape(own_rows, width).astype(jnp.float32)
    inv_rms = lax.rsqrt(jnp.mean(in_float * in_float, axis=1, keepdims=True) + norm_eps)
    normed = in_float * inv_rms
    scaled = (normed * gain[None, :]).astype(jnp.bfloat16)
    projected = jnp.dot(
        scaled,
        lax.all_gather(weight, "grp", axis=0, tiled=True),
        preferred_element_type=jnp.float32,
    )
    proj_scale = lax.rsqrt(
        jnp.mean(projected * projected, axis=1, keepdims=True) + norm_eps
    ) / math.sqrt(proj_width)
    query_unit = (projected * proj_scale).astype(jnp.bfloat16)
    lemma_unit = unit_rows(lemma_emb.astype(jnp.float32).reshape(-1, proj_width)).astype(
        jnp.bfloat16
    )
    all_live = (jnp.arange(lemma_tok)[None, :] < lemma_len[:, None]).astype(jnp.float32)
    block_start = (lemma_idx * group_axis + group_idx) * states_dev
    all_keys = lax.all_gather(lemma_unit, "lemma", axis=0, tiled=True)
    block_count = 8
    block_lemmas = lemmas_all // block_count
    key_blocks = all_keys.reshape(block_count, block_lemmas * lemma_tok, proj_width)
    live_blocks = all_live.reshape(block_count, block_lemmas * lemma_tok)
    own_len = lax.dynamic_slice_in_dim(query_len, block_start, states_dev)
    own_pos = lax.dynamic_slice_in_dim(positive, block_start, states_dev)
    live_rows = (jnp.arange(query_tok)[None, :] < own_len[:, None]).astype(jnp.float32)
    lengths_f = own_len.astype(jnp.float32)

    def block_lse(items):
        keys, key_live = items
        exp_terms, per_lemma = lemma_terms(query_unit, keys, key_live, block_lemmas, lemma_tok)
        return token_temp * jnp.log(per_lemma)

    tok_lse = lax.map(block_lse, (key_blocks, live_blocks))
    tok_lse = jnp.moveaxis(tok_lse, 0, 1).reshape(own_rows, lemmas_all)
    similarity, powers, is_positive = state_loss(
        tok_lse, live_rows, lengths_f, own_pos, jnp.arange(lemmas_all)
    )
    partition = jnp.sum(powers, axis=1)
    pos_score = jnp.sum(similarity * is_positive, axis=1)
    loss = jnp.log(partition) - pos_score / state_temp
    grad_sim = loss_scale * (powers / partition[:, None] - is_positive) / state_temp
    tok_grad = (grad_sim[:, None, :] * live_rows[:, :, None] / lengths_f[:, None, None]).reshape(
        own_rows, block_count, block_lemmas
    )
    grad_blocks = jnp.moveaxis(tok_grad, 1, 0)

    def add_block(acc, items):
        keys, key_live, grads = items
        return (acc + token_grads(query_unit, grads, keys, key_live, block_lemmas, lemma_tok), None)

    unit_grad, unused = lax.scan(
        add_block,
        jnp.zeros((own_rows, proj_width), jnp.float32),
        (key_blocks, live_blocks, grad_blocks),
    )
    proj_grad = proj_scale * unit_grad - projected * proj_scale**3 * jnp.sum(
        projected * unit_grad, axis=1, keepdims=True
    )
    proj_grad_b = proj_grad.astype(jnp.bfloat16)
    scaled_grad = contract_last(proj_grad_b, lax.all_gather(weight, "grp", axis=0, tiled=True))
    normed_grad = scaled_grad * gain[None, :]
    input_grad = (
        inv_rms * normed_grad
        - in_float * inv_rms**3 * jnp.sum(in_float * normed_grad, axis=1, keepdims=True) / width
    )
    hidden_grad = input_grad.astype(jnp.bfloat16).reshape(states_dev, query_tok, width)
    weight_part = lax.dot_general(
        scaled, proj_grad_b, (((0,), (0,)), ((), ())), preferred_element_type=jnp.float32
    )
    gain_part = jnp.sum(scaled_grad * normed, axis=0)
    weight_sum, gain_sum = (
        lax.psum(weight_part.astype(jnp.bfloat16), "lemma").astype(jnp.float32),
        lax.psum(gain_part.astype(jnp.bfloat16), "lemma").astype(jnp.float32),
    )
    weight_sum, gain_sum = (
        lax.psum_scatter(
            weight_sum.astype(jnp.bfloat16), "grp", scatter_dimension=0, tiled=True
        ).astype(jnp.float32),
        lax.psum_scatter(
            gain_sum.astype(jnp.bfloat16), "grp", scatter_dimension=0, tiled=True
        ).astype(jnp.float32),
    )
    squares = jnp.sum(weight_sum * weight_sum) + jnp.sum(gain_sum * gain_sum)
    total_squares = lax.psum(squares, "grp")
    factor = jnp.minimum(1.0, grad_limit / jnp.sqrt(total_squares + norm_eps))
    return (loss, hidden_grad, weight_sum * factor, gain_sum * factor)


NT = (((1,), (1,)), ((), ()))
MESH = pl.DeviceIdType.MESH


def fused_kernel(
    lemma_axis, group_axis, lemma_dev, lemma_tok, states_dev, query_tok,
    hidden_ref, gain_ref, weight_ref, emb_ref, len_ref, qlen_ref, pos_ref,
    loss_ref, hgrad_ref, wgrad_ref, ggrad_ref,
    hid, emb, hout, w_all, keys, live, live_t, powers_b, scaled_b, scaled_t,
    part, pair_in, half, chip_in, quarter, grp_in, raw, sq, over_gain,
    local_sem, w_send, w_recv, wf_send, wf_recv, k_send, k_recv, kf_send, kf_recv,
    p_send, p_recv, c_send, c_recv, g_send, g_recv, a_send, a_recv, s_send, s_recv,
):
    chips = lemma_axis // 2
    me, grp = lax.axis_index("lemma"), lax.axis_index("grp")
    chip, core = me // 2, lax.rem(me, 2)
    pair = chip * 2 + (1 - core)
    rows, width = hid.shape
    proj_width = weight_ref.shape[1]
    wrows = weight_ref.shape[0]
    hrows = wrows // 2
    block_tok = lemma_dev * lemma_tok
    lemmas_all = lemma_dev * lemma_axis

    across = 2 - chips % 2
    along = chips // across
    chip_y, chip_x = chip // across, lax.rem(chip, across)

    def split(step):
        if isinstance(step, int):
            return step // across, step % across
        return lax.div(step, across), lax.rem(step, across)

    def chip_to(step):
        step_y, step_x = split(step)
        return lax.rem(chip_y + step_y, along) * across + lax.rem(chip_x + step_x, across)

    def chip_source(step):
        step_y, step_x = split(step)
        return lax.rem(chip_y + along - step_y, along) * across + lax.rem(
            chip_x + across - step_x, across
        )

    def chip_peer(step):
        return chip_to(step) * 2 + core

    def chip_from(step):
        return chip_source(step) * 2 + core

    def grp_peer(step):
        return lax.rem(grp + step, group_axis)

    def grp_from(step):
        return lax.rem(grp + group_axis - step, group_axis)

    def remote(src, dst, send_sem, recv_sem, to_lemma, to_grp):
        return pltpu.make_async_remote_copy(
            src_ref=src, dst_ref=dst, send_sem=send_sem, recv_sem=recv_sem,
            device_id=(to_lemma, to_grp), device_id_type=MESH,
        )

    emb_copy = pltpu.make_async_copy(emb_ref, emb, local_sem.at[0])
    hid_copy = pltpu.make_async_copy(hidden_ref, hid, local_sem.at[1])
    w_copy = pltpu.make_async_copy(weight_ref, w_all.at[grp], local_sem.at[2])
    emb_copy.start()
    w_copy.start()
    hid_copy.start()

    barrier = pltpu.get_barrier_semaphore()
    others = [
        (lemma_step, grp_step)
        for lemma_step in range(lemma_axis)
        for grp_step in range(group_axis)
        if (lemma_step == 0) != (grp_step == 0)
    ]
    for lemma_step, grp_step in others:
        pl.semaphore_signal(
            barrier, inc=1, device_id_type=MESH,
            device_id=(lax.rem(me + lemma_step, lemma_axis), grp_peer(grp_step)),
        )

    emb_copy.wait()
    tokens = emb[...].astype(jnp.float32)
    token_scale = lax.rsqrt(
        jnp.mean(tokens * tokens, axis=1, keepdims=True) + norm_eps
    ) / math.sqrt(proj_width)
    keys[chip, core] = (tokens * token_scale).astype(jnp.bfloat16)
    w_copy.wait()
    pl.semaphore_wait(barrier, len(others))

    my_half = pl.ds(pl.multiple_of(core * hrows, hrows), hrows)
    w_out = []
    for step in range(1, group_axis):
        src = w_all.at[grp, my_half]
        copy = remote(src, src, w_send.at[step], w_recv.at[step], me, grp_peer(step))
        copy.start()
        w_out.append(copy)
    k_out = []
    for step in reversed(range(1, chips)):
        copy = remote(
            keys.at[chip, core], keys.at[chip, core], k_send.at[step], k_recv.at[step], chip_peer(step), grp
        )
        copy.start()
        k_out.append(copy)
    kf_out = [remote(keys.at[chip, core], keys.at[chip, core], kf_send.at[0], kf_recv.at[0], pair, grp)]
    kf_out[0].start()

    chip_tok = 2 * block_tok
    token_of = lax.broadcasted_iota(
        jnp.int32, (chip_tok, lemmas_all), 0
    ) - lemma_tok * lax.broadcasted_iota(jnp.int32, (chip_tok, lemmas_all), 1)
    token_of_t = lax.broadcasted_iota(
        jnp.int32, (lemmas_all, chip_tok), 1
    ) - lemma_tok * lax.broadcasted_iota(jnp.int32, (lemmas_all, chip_tok), 0)
    lengths = jnp.minimum(len_ref[...].reshape(1, lemmas_all), lemma_tok)
    lengths_t = jnp.broadcast_to(
        lengths.astype(jnp.float32), (lemmas_all, lemmas_all)
    ).T[:, :1].astype(jnp.int32)
    @pl.loop(0, chips)
    def _(block):
        first = -block * chip_tok
        member = (token_of >= first) & (token_of < lengths + first)
        live[block] = jnp.where(member, 1.0, 0.0).astype(jnp.bfloat16)
        member = (token_of_t >= first) & (token_of_t < lengths_t + first)
        live_t[block] = jnp.where(member, 1.0, 0.0).astype(jnp.bfloat16)

    hid_copy.wait()
    piece = wrows // lemma_axis

    def group_cols(group):
        return pl.ds(pl.multiple_of(group * wrows, 128), wrows)

    def add_squares(group, acc):
        in_float = hid[:, group_cols(group)].astype(jnp.float32)
        return acc + jnp.sum(in_float * in_float, axis=1, keepdims=True)

    mean_sq = lax.fori_loop(0, group_axis, add_squares, jnp.zeros((rows, 1), jnp.float32)) / width
    inv_rms = lax.rsqrt(mean_sq + norm_eps)

    @pl.loop(0, group_axis)
    def _(group):
        cols = group_cols(group)
        in_float = hid[:, cols].astype(jnp.float32)
        scaled = (in_float * inv_rms * gain_ref[cols].reshape(1, wrows)).astype(jnp.bfloat16)
        scaled_b[group] = scaled
        scaled_rows = scaled.T
        for owner in range(lemma_axis):
            scaled_t[owner // 2, owner % 2, group] = scaled_rows[
                owner * piece : (owner + 1) * piece
            ]

    own_gain = gain_ref[pl.ds(pl.multiple_of(grp * wrows, 128), wrows)].reshape(1, wrows)
    gain_col = jnp.broadcast_to(own_gain, (proj_width, wrows)).T
    over_gain[...] = (w_all[grp].astype(jnp.float32) / gain_col).reshape(over_gain.shape)

    wf_out = []
    for step in range(1, group_axis):
        dst = w_all.at[grp_from(step), my_half]
        remote(dst, dst, w_send.at[step], w_recv.at[step], me, grp_peer(step)).wait_recv()
        copy = remote(dst, dst, wf_send.at[step], wf_recv.at[step], pair, grp)
        copy.start()
        wf_out.append(copy)
    other_half = pl.ds(pl.multiple_of((1 - core) * hrows, hrows), hrows)
    for step in range(1, group_axis):
        dst = w_all.at[grp_from(step), other_half]
        remote(dst, dst, wf_send.at[step], wf_recv.at[step], pair, grp).wait_recv()

    def project(group, acc):
        return acc + jnp.dot(scaled_b[group], w_all[group], preferred_element_type=jnp.float32)

    projected = lax.fori_loop(
        0, group_axis, project, jnp.zeros((rows, proj_width), jnp.float32)
    )
    proj_scale = lax.rsqrt(
        jnp.mean(projected * projected, axis=1, keepdims=True) + norm_eps
    ) / math.sqrt(proj_width)
    query_unit = (projected * proj_scale).astype(jnp.bfloat16)

    def first_pass(block, total):
        scores = lax.dot_general(
            query_unit, keys[block].reshape(chip_tok, proj_width), NT, preferred_element_type=jnp.float32
        )
        exp_terms = jnp.exp(scores * (1.0 / token_temp)).astype(jnp.bfloat16)
        powers_b[block] = exp_terms
        return total + jnp.dot(exp_terms, live[block], preferred_element_type=jnp.float32)

    def forward(step):
        dst = keys.at[chip_source(step), core]
        remote(dst, dst, k_send.at[step], k_recv.at[step], chip_peer(step), grp).wait_recv()
        remote(dst, dst, kf_send.at[step], kf_recv.at[step], pair, grp).start()

    def chip_pass(step, total):
        @pl.when(step + 1 < chips)
        def _():
            forward(step + 1)

        source = chip_source(step)
        dst = keys.at[source, 1 - core]
        remote(dst, dst, kf_send.at[step], kf_recv.at[step], pair, grp).wait_recv()
        return first_pass(source, total)

    total = lax.fori_loop(0, chips, chip_pass, jnp.zeros((rows, lemmas_all), jnp.float32))

    tok_lse = token_temp * jnp.log(total)
    first_state = (me * group_axis + grp) * states_dev
    ratios = []
    losses = jnp.zeros((1, 128), jnp.float32)
    lane = lax.broadcasted_iota(jnp.int32, (1, 128), 1)
    for state in range(states_dev):
        length = qlen_ref[first_state + state]
        target = pos_ref[first_state + state]
        length_f = jnp.full((1, lemmas_all), length, jnp.int32).astype(jnp.float32)
        span = slice(state * query_tok, (state + 1) * query_tok)
        row_ids = lax.broadcasted_iota(jnp.int32, (query_tok, lemmas_all), 0)
        live_rows = jnp.where(row_ids < length, 1.0, 0.0)
        similarity = jnp.sum(tok_lse[span] * live_rows, axis=0, keepdims=True) / length_f
        powers = jnp.exp(similarity / state_temp)
        lemma_ids = lax.broadcasted_iota(jnp.int32, (1, lemmas_all), 1)
        is_positive = jnp.where(lemma_ids == target, 1.0, 0.0)
        partition = jnp.sum(powers, axis=1, keepdims=True)
        pos_score = jnp.sum(similarity * is_positive, axis=1, keepdims=True)
        loss = jnp.log(partition) - pos_score / state_temp
        losses = jnp.where(lane == state, loss, losses)
        grad_sim = loss_scale * (powers / partition - is_positive) / state_temp
        ratios.append(live_rows * (grad_sim / length_f) / total[span])
    loss_ref[...] = losses
    ratio = jnp.concatenate(ratios, axis=0).astype(jnp.bfloat16)

    def second_pass(block, acc):
        spread = jnp.dot(ratio, live_t[block], preferred_element_type=jnp.float32)
        coef = (powers_b[block].astype(jnp.float32) * spread).astype(jnp.bfloat16)
        return acc + jnp.dot(
            coef, keys[block].reshape(chip_tok, proj_width), preferred_element_type=jnp.float32
        )

    unit_grad = lax.fori_loop(0, chips, second_pass, jnp.zeros((rows, proj_width), jnp.float32))
    proj_grad = proj_scale * unit_grad - projected * (
        proj_scale * proj_scale * proj_scale
    ) * jnp.sum(projected * unit_grad, axis=1, keepdims=True)
    proj_grad_b = proj_grad.astype(jnp.bfloat16)

    def weight_part(target, side):
        left = scaled_t[target, side].reshape(group_axis * piece, rows)
        return jnp.dot(left, proj_grad_b, preferred_element_type=jnp.float32).reshape(
            group_axis, piece, proj_width
        )

    def pair_copy(step):
        return remote(
            part.at[step], pair_in.at[step], p_send.at[step], p_recv.at[step], pair, grp
        )

    def chip_copy(step, grp_step):
        return remote(
            half.at[step, grp_peer(grp_step)], chip_in.at[step - 1, grp_step],
            c_send.at[step - 1, grp_step], c_recv.at[step - 1, grp_step],
            chip_peer(step), grp,
        )

    @pl.loop(0, chips)
    def _(turn):
        step = chips - 1 - turn
        part[step] = weight_part(chip_to(step), 1 - core).astype(jnp.bfloat16)
        pair_copy(step).start()

    @pl.loop(0, chips)
    def _(turn):
        step = chips - 1 - turn
        mine = weight_part(chip_to(step), core)
        pair_copy(step).wait_recv()
        half[step] = (mine + pair_in[step].astype(jnp.float32)).astype(jnp.bfloat16)

        @pl.when(step > 0)
        def _():
            for grp_step in reversed(range(group_axis)):
                chip_copy(step, grp_step).start()

    row_dot = jnp.sum(projected * proj_grad_b.astype(jnp.float32), axis=1, keepdims=True)
    row_scale = inv_rms * inv_rms * row_dot / width

    def hidden_part(group):
        cols = group_cols(group)
        scaled_grad = lax.dot_general(
            proj_grad_b, w_all[group], NT, preferred_element_type=jnp.float32
        )
        hout[:, cols] = (
            inv_rms * (scaled_grad * gain_ref[cols].reshape(1, wrows))
            - hid[:, cols].astype(jnp.float32) * row_scale
        ).astype(jnp.bfloat16)

    pl.loop(0, group_axis // 2)(hidden_part)

    g_out = []
    for grp_step in reversed(range(group_axis)):
        chip_sum = half[0, grp_peer(grp_step)].astype(jnp.float32)
        for step in range(1, chips):
            chip_copy(step, grp_step).wait_recv()
            chip_sum += chip_in[step - 1, grp_step].astype(jnp.float32)
        if grp_step:
            quarter[grp_step] = chip_sum.astype(jnp.bfloat16)
            copy = remote(
                quarter.at[grp_step], grp_in.at[grp_step - 1],
                g_send.at[grp_step], g_recv.at[grp_step], me, grp_peer(grp_step),
            )
            copy.start()
            g_out.append(copy)
        else:
            grp_sum = chip_sum
    pl.loop(group_axis // 2, group_axis)(hidden_part)
    hout_copy = pltpu.make_async_copy(hout, hgrad_ref, local_sem.at[3])
    hout_copy.start()
    for copy in g_out:
        copy.wait_recv()
    for step in range(1, group_axis):
        grp_sum += grp_in[step - 1].astype(jnp.float32)
    raw[me] = grp_sum.astype(jnp.bfloat16)
    a_out = []
    for step in range(1, lemma_axis):
        copy = remote(
            raw.at[me], raw.at[me], a_send.at[step], a_recv.at[step],
            lax.rem(me + step, lemma_axis), grp,
        )
        copy.start()
        a_out.append(copy)
    for step in range(1, lemma_axis):
        dst = raw.at[lax.rem(me + lemma_axis - step, lemma_axis)]
        remote(dst, dst, a_send.at[step], a_recv.at[step], pair, grp).wait_recv()

    weight_raw = raw[...].reshape(wrows, proj_width).astype(jnp.float32)
    ones = jnp.ones((8, proj_width), jnp.float32)
    gain_raw = lax.dot_general(
        ones, over_gain[...].reshape(wrows, proj_width) * weight_raw, NT,
        preferred_element_type=jnp.float32, precision=lax.Precision.HIGHEST,
    )[:1]
    squares = jnp.sum(
        jnp.sum(weight_raw * weight_raw, axis=0, keepdims=True), axis=1, keepdims=True
    ) + jnp.sum(gain_raw * gain_raw, axis=1, keepdims=True)
    my_sq = sq.at[grp]
    my_sq[...] = jnp.broadcast_to(squares, (1, 128))
    s_out = []
    for step in range(1, group_axis):
        copy = remote(my_sq, my_sq, s_send.at[step], s_recv.at[step], me, grp_peer(step))
        copy.start()
        s_out.append(copy)
    for step in range(1, group_axis):
        dst = sq.at[grp_from(step)]
        remote(dst, dst, s_send.at[step], s_recv.at[step], me, grp_peer(step)).wait_recv()
    squares_all = jnp.sum(sq[...], axis=0)
    factor = jnp.minimum(1.0, grad_limit / jnp.sqrt(squares_all + norm_eps))
    wgrad_ref[...] = weight_raw * factor
    ggrad_ref[...] = gain_raw * factor[:, :1]

    for copy in w_out + k_out + wf_out + kf_out + g_out + a_out + s_out:
        copy.wait_send()
    for step in range(chips):
        pair_copy(step).wait_send()
        if step:
            dst = keys.at[chip_source(step), core]
            remote(dst, dst, kf_send.at[step], kf_recv.at[step], pair, grp).wait_send()
            for grp_step in range(group_axis):
                chip_copy(step, grp_step).wait_send()
    hout_copy.wait()


def place_kernel(
    loss, hgrad, wgrad, ggrad, loss_out, hgrad_out, wgrad_out, ggrad_out,
    loss_in, hbuf, wbuf, ggrad_in, loss_row, ggrad_row, sems,
):
    pairs = [(hgrad, hbuf), (wgrad, wbuf), (loss, loss_in), (ggrad, ggrad_in)]
    copies = [pltpu.make_async_copy(a, b, sems.at[i]) for i, (a, b) in enumerate(pairs)]
    for copy in copies:
        copy.start()
    pairs = [(hbuf, hgrad_out), (wbuf, wgrad_out), (loss_row, loss_out), (ggrad_row, ggrad_out)]
    backs = [pltpu.make_async_copy(a, b, sems.at[4 + i]) for i, (a, b) in enumerate(pairs)]
    copies[0].wait()
    backs[0].start()
    copies[1].wait()
    backs[1].start()
    copies[2].wait()
    loss_row[...] = loss_in[0, : loss_row.shape[0]]
    backs[2].start()
    copies[3].wait()
    ggrad_row[...] = ggrad_in[...].reshape(ggrad_row.shape)
    backs[3].start()
    for copy in backs:
        copy.wait()


def fused_body(hidden, gain, weight, lemma_emb, lemma_len, query_len, positive):
    states_dev, query_tok, width = hidden.shape
    wrows, proj_width = weight.shape
    lemma_dev, lemma_tok = lemma_emb.shape[:2]
    lemma_axis, group_axis = lax.axis_size("lemma"), lax.axis_size("grp")
    chips = lemma_axis // 2
    rows, block_tok = states_dev * query_tok, lemma_dev * lemma_tok
    piece = wrows // lemma_axis
    lemmas_all = lemma_dev * lemma_axis
    vmem = pl.BlockSpec(memory_space=pltpu.VMEM)
    smem = pl.BlockSpec(memory_space=pltpu.SMEM)
    hbm = pl.BlockSpec(memory_space=pltpu.HBM)
    sem = pltpu.SemaphoreType.DMA
    bf16, f32 = jnp.bfloat16, jnp.float32
    outs = pl.pallas_call(
        functools.partial(
            fused_kernel, lemma_axis, group_axis, lemma_dev, lemma_tok, states_dev, query_tok
        ),
        out_shape=(
            jax.ShapeDtypeStruct((1, 128), f32),
            jax.ShapeDtypeStruct((rows, width), bf16),
            jax.ShapeDtypeStruct((wrows, proj_width), f32),
            jax.ShapeDtypeStruct((1, wrows), f32),
        ),
        in_specs=[hbm, vmem, hbm, hbm, vmem, smem, smem],
        out_specs=(vmem, hbm, vmem, vmem),
        scratch_shapes=[
            pltpu.VMEM((rows, width), bf16),
            pltpu.VMEM((block_tok, proj_width), bf16),
            pltpu.VMEM((rows, width), bf16),
            pltpu.VMEM((group_axis, wrows, proj_width), bf16),
            pltpu.VMEM((chips, 2, block_tok, proj_width), bf16),
            pltpu.VMEM((chips, 2 * block_tok, lemmas_all), bf16),
            pltpu.VMEM((chips, lemmas_all, 2 * block_tok), bf16),
            pltpu.VMEM((chips, rows, 2 * block_tok), bf16),
            pltpu.VMEM((group_axis, rows, wrows), bf16),
            pltpu.VMEM((chips, 2, group_axis, piece, rows), bf16),
            pltpu.VMEM((chips, group_axis, piece, proj_width), bf16),
            pltpu.VMEM((chips, group_axis, piece, proj_width), bf16),
            pltpu.VMEM((chips, group_axis, piece, proj_width), bf16),
            pltpu.VMEM((chips - 1, group_axis, piece, proj_width), bf16),
            pltpu.VMEM((group_axis, piece, proj_width), bf16),
            pltpu.VMEM((group_axis - 1, piece, proj_width), bf16),
            pltpu.VMEM((lemma_axis, piece, proj_width), bf16),
            pltpu.VMEM((group_axis, 1, 128), f32),
            pltpu.VMEM((lemma_axis, piece, proj_width), f32),
            sem((4,)),
            sem((group_axis,)), sem((group_axis,)), sem((group_axis,)), sem((group_axis,)),
            sem((chips,)), sem((chips,)), sem((chips,)), sem((chips,)),
            sem((chips,)), sem((chips,)),
            sem((chips - 1, group_axis)), sem((chips - 1, group_axis)),
            sem((group_axis,)), sem((group_axis,)),
            sem((lemma_axis,)), sem((lemma_axis,)),
            sem((group_axis,)), sem((group_axis,)),
        ],
        compiler_params=pltpu.CompilerParams(
            collective_id=0, has_side_effects=True, vmem_limit_bytes=62 * 1024 * 1024
        ),
        cost_estimate=pl.CostEstimate(
            flops=2 * rows * proj_width * (3 * width + 4 * block_tok * lemma_axis),
            bytes_accessed=4 * rows * width * 2,
            transcendentals=rows * block_tok * lemma_axis,
        ),
    )(
        hidden.reshape(rows, width), gain, weight,
        lemma_emb.reshape(block_tok, proj_width), lemma_len,
        query_len, positive,
    )
    loss, hidden_grad, weight_grad, gain_grad = pl.pallas_call(
        place_kernel,
        out_shape=(
            jax.ShapeDtypeStruct((states_dev,), f32),
            jax.ShapeDtypeStruct((rows, width), bf16),
            jax.ShapeDtypeStruct((wrows, proj_width), f32),
            jax.ShapeDtypeStruct((wrows,), f32),
        ),
        in_specs=[hbm] * 4,
        out_specs=(hbm,) * 4,
        scratch_shapes=[
            pltpu.VMEM((1, 128), f32),
            pltpu.VMEM((rows, width), bf16),
            pltpu.VMEM((wrows, proj_width), f32),
            pltpu.VMEM((1, wrows), f32),
            pltpu.VMEM((states_dev,), f32),
            pltpu.VMEM((wrows,), f32),
            sem((8,)),
        ],
        compiler_params=pltpu.CompilerParams(vmem_limit_bytes=62 * 1024 * 1024),
    )(*outs)
    return (loss, hidden_grad.reshape(hidden.shape), weight_grad, gain_grad)


def solution(mesh):
    in_specs = (
        P(("lemma", "grp"), None, None),
        P(),
        P("grp", None),
        P("lemma", None, None),
        P(),
        P(),
        P(),
    )
    out_specs = (P(("lemma", "grp")), P(("lemma", "grp"), None, None), P("grp", None), P("grp"))

    def run(hidden, gain, weight, *rest):
        rows = weight.shape[0] // mesh.shape["grp"]
        tiled = rows % (16 * mesh.shape["lemma"]) == 0 and rows % 128 == 0
        chosen = fused_body if tiled else body
        return jax.shard_map(
            chosen, mesh=mesh, in_specs=in_specs, out_specs=out_specs, check_vma=False
        )(hidden, gain, weight, *rest)

    return run
```

```python
import functools
import math

import jax
import jax.numpy as jnp
from jax import lax
from jax.experimental import pallas as pl
from jax.experimental.pallas import tpu as pltpu
from jax.sharding import PartitionSpec as P

token_temp = 0.05
state_temp = 0.05
loss_scale = 1024.0
grad_limit = 400.0
norm_eps = 1e-06


def contract_last(left, right):
    return lax.dot_general(
        left, right, (((1,), (1,)), ((), ())), preferred_element_type=jnp.float32
    )


def unit_rows(values):
    scale_rows = lax.rsqrt(jnp.mean(values * values, axis=-1, keepdims=True) + norm_eps)
    return values * scale_rows / math.sqrt(values.shape[-1])


def lemma_terms(queries, keys, key_live, lemma_count, lemma_tok):
    scores = contract_last(queries, keys)
    exp_terms = jnp.exp(scores / token_temp) * key_live[None, :]
    per_lemma = jnp.sum(exp_terms.reshape(queries.shape[0], lemma_count, lemma_tok), axis=2)
    return (exp_terms, per_lemma)


def token_grads(queries, grads, keys, key_live, lemma_count, lemma_tok):
    exp_terms, per_lemma = lemma_terms(queries, keys, key_live, lemma_count, lemma_tok)
    rows = queries.shape[0]
    weights = exp_terms.reshape(rows, lemma_count, lemma_tok) / per_lemma[:, :, None]
    coef = (weights * grads[:, :, None]).reshape(rows, lemma_count * lemma_tok).astype(jnp.bfloat16)
    return jnp.dot(coef, keys, preferred_element_type=jnp.float32)


def state_loss(tok_lse, live_rows, lengths_f, targets, lemma_ids):
    states = live_rows.shape[0]
    similarity = (
        jnp.sum(tok_lse.reshape(states, live_rows.shape[1], -1) * live_rows[:, :, None], axis=1)
        / lengths_f[:, None]
    )
    powers = jnp.exp(similarity / state_temp)
    is_positive = (lemma_ids[None, :] == targets[:, None]).astype(jnp.float32)
    return (similarity, powers, is_positive)


def body(hidden, gain, weight, lemma_emb, lemma_len, query_len, positive):
    states_dev, query_tok, width = hidden.shape
    proj_width = weight.shape[1]
    lemma_dev, lemma_tok = (lemma_emb.shape[0], lemma_emb.shape[1])
    lemma_axis = lax.axis_size("lemma")
    group_axis = lax.axis_size("grp")
    lemma_idx = lax.axis_index("lemma")
    group_idx = lax.axis_index("grp")
    own_rows = states_dev * query_tok
    lemmas_all = lemma_dev * lemma_axis
    in_float = hidden.reshape(own_rows, width).astype(jnp.float32)
    inv_rms = lax.rsqrt(jnp.mean(in_float * in_float, axis=1, keepdims=True) + norm_eps)
    normed = in_float * inv_rms
    scaled = (normed * gain[None, :]).astype(jnp.bfloat16)
    projected = jnp.dot(
        scaled,
        lax.all_gather(weight, "grp", axis=0, tiled=True),
        preferred_element_type=jnp.float32,
    )
    proj_scale = lax.rsqrt(
        jnp.mean(projected * projected, axis=1, keepdims=True) + norm_eps
    ) / math.sqrt(proj_width)
    query_unit = (projected * proj_scale).astype(jnp.bfloat16)
    lemma_unit = unit_rows(lemma_emb.astype(jnp.float32).reshape(-1, proj_width)).astype(
        jnp.bfloat16
    )
    all_live = (jnp.arange(lemma_tok)[None, :] < lemma_len[:, None]).astype(jnp.float32)
    block_start = (lemma_idx * group_axis + group_idx) * states_dev
    all_keys = lax.all_gather(lemma_unit, "lemma", axis=0, tiled=True)
    block_count = 8
    block_lemmas = lemmas_all // block_count
    key_blocks = all_keys.reshape(block_count, block_lemmas * lemma_tok, proj_width)
    live_blocks = all_live.reshape(block_count, block_lemmas * lemma_tok)
    own_len = lax.dynamic_slice_in_dim(query_len, block_start, states_dev)
    own_pos = lax.dynamic_slice_in_dim(positive, block_start, states_dev)
    live_rows = (jnp.arange(query_tok)[None, :] < own_len[:, None]).astype(jnp.float32)
    lengths_f = own_len.astype(jnp.float32)

    def block_lse(items):
        keys, key_live = items
        exp_terms, per_lemma = lemma_terms(query_unit, keys, key_live, block_lemmas, lemma_tok)
        return token_temp * jnp.log(per_lemma)

    tok_lse = lax.map(block_lse, (key_blocks, live_blocks))
    tok_lse = jnp.moveaxis(tok_lse, 0, 1).reshape(own_rows, lemmas_all)
    similarity, powers, is_positive = state_loss(
        tok_lse, live_rows, lengths_f, own_pos, jnp.arange(lemmas_all)
    )
    partition = jnp.sum(powers, axis=1)
    pos_score = jnp.sum(similarity * is_positive, axis=1)
    loss = jnp.log(partition) - pos_score / state_temp
    grad_sim = loss_scale * (powers / partition[:, None] - is_positive) / state_temp
    tok_grad = (grad_sim[:, None, :] * live_rows[:, :, None] / lengths_f[:, None, None]).reshape(
        own_rows, block_count, block_lemmas
    )
    grad_blocks = jnp.moveaxis(tok_grad, 1, 0)

    def add_block(acc, items):
        keys, key_live, grads = items
        return (acc + token_grads(query_unit, grads, keys, key_live, block_lemmas, lemma_tok), None)

    unit_grad, unused = lax.scan(
        add_block,
        jnp.zeros((own_rows, proj_width), jnp.float32),
        (key_blocks, live_blocks, grad_blocks),
    )
    proj_grad = proj_scale * unit_grad - projected * proj_scale**3 * jnp.sum(
        projected * unit_grad, axis=1, keepdims=True
    )
    proj_grad_b = proj_grad.astype(jnp.bfloat16)
    scaled_grad = contract_last(proj_grad_b, lax.all_gather(weight, "grp", axis=0, tiled=True))
    normed_grad = scaled_grad * gain[None, :]
    input_grad = (
        inv_rms * normed_grad
        - in_float * inv_rms**3 * jnp.sum(in_float * normed_grad, axis=1, keepdims=True) / width
    )
    hidden_grad = input_grad.astype(jnp.bfloat16).reshape(states_dev, query_tok, width)
    weight_part = lax.dot_general(
        scaled, proj_grad_b, (((0,), (0,)), ((), ())), preferred_element_type=jnp.float32
    )
    gain_part = jnp.sum(scaled_grad * normed, axis=0)
    weight_sum, gain_sum = (
        lax.psum(weight_part.astype(jnp.bfloat16), "lemma").astype(jnp.float32),
        lax.psum(gain_part.astype(jnp.bfloat16), "lemma").astype(jnp.float32),
    )
    weight_sum, gain_sum = (
        lax.psum_scatter(
            weight_sum.astype(jnp.bfloat16), "grp", scatter_dimension=0, tiled=True
        ).astype(jnp.float32),
        lax.psum_scatter(
            gain_sum.astype(jnp.bfloat16), "grp", scatter_dimension=0, tiled=True
        ).astype(jnp.float32),
    )
    squares = jnp.sum(weight_sum * weight_sum) + jnp.sum(gain_sum * gain_sum)
    total_squares = lax.psum(squares, "grp")
    factor = jnp.minimum(1.0, grad_limit / jnp.sqrt(total_squares + norm_eps))
    return (loss, hidden_grad, weight_sum * factor, gain_sum * factor)


NT = (((1,), (1,)), ((), ()))
MESH = pl.DeviceIdType.MESH


def fused_kernel(
    lemma_axis, group_axis, lemma_dev, lemma_tok, states_dev, query_tok,
    hidden_ref, gain_hbm, weight_ref, emb_ref, len_hbm, qlen_hbm, pos_hbm,
    loss_ref, hgrad_ref, raw_ref, ggrad_ref, factor_ref,
    gain_ref, len_ref, qlen_ref, pos_ref, loss_row, gain_out, factor_row,
    hid, emb, hout, w_all, keys, live, live_t, powers_b, scaled_b, scaled_t,
    part, pair_in, half, chip_in, quarter, grp_in, raw, sq, over_gain,
    local_sem, table_sem, w_send, w_recv, wf_send, wf_recv, k_send, k_recv, kf_send, kf_recv,
    p_send, p_recv, c_send, c_recv, g_send, g_recv, a_send, a_recv, s_send, s_recv,
):
    chips = lemma_axis // 2
    me, grp = lax.axis_index("lemma"), lax.axis_index("grp")
    chip, core = me // 2, lax.rem(me, 2)
    pair = chip * 2 + (1 - core)
    rows, width = hid.shape
    proj_width = weight_ref.shape[1]
    wrows = weight_ref.shape[0]
    hrows = wrows // 2
    block_tok = lemma_dev * lemma_tok
    lemmas_all = lemma_dev * lemma_axis

    across = 2 - chips % 2
    along = chips // across
    chip_y, chip_x = chip // across, lax.rem(chip, across)

    def chip_to(step):
        step_y, step_x = step // across, step % across
        return lax.rem(chip_y + step_y, along) * across + lax.rem(chip_x + step_x, across)

    def chip_source(step):
        step_y, step_x = step // across, step % across
        return lax.rem(chip_y + along - step_y, along) * across + lax.rem(
            chip_x + across - step_x, across
        )

    def chip_peer(step):
        return chip_to(step) * 2 + core

    def chip_from(step):
        return chip_source(step) * 2 + core

    def grp_peer(step):
        return lax.rem(grp + step, group_axis)

    def grp_from(step):
        return lax.rem(grp + group_axis - step, group_axis)

    def remote(src, dst, send_sem, recv_sem, to_lemma, to_grp):
        return pltpu.make_async_remote_copy(
            src_ref=src, dst_ref=dst, send_sem=send_sem, recv_sem=recv_sem,
            device_id=(to_lemma, to_grp), device_id_type=MESH,
        )

    emb_copy = pltpu.make_async_copy(emb_ref, emb, local_sem.at[0])
    hid_copy = pltpu.make_async_copy(hidden_ref, hid, local_sem.at[1])
    w_copy = pltpu.make_async_copy(weight_ref, w_all.at[grp], local_sem.at[2])
    emb_copy.start()
    w_copy.start()

    barrier = pltpu.get_barrier_semaphore()
    others = [
        (lemma_step, grp_step)
        for lemma_step in range(lemma_axis)
        for grp_step in range(group_axis)
        if lemma_step or grp_step
    ]
    for lemma_step, grp_step in others:
        pl.semaphore_signal(
            barrier, inc=1, device_id_type=MESH,
            device_id=(lax.rem(me + lemma_step, lemma_axis), grp_peer(grp_step)),
        )

    tables = [
        pltpu.make_async_copy(src, dst, table_sem.at[index])
        for index, (src, dst) in enumerate(
            [(len_hbm, len_ref), (gain_hbm, gain_ref), (qlen_hbm, qlen_ref), (pos_hbm, pos_ref)]
        )
    ]
    hid_copy.start()
    for copy in tables:
        copy.start()

    emb_copy.wait()
    tokens = emb[...].astype(jnp.float32)
    token_scale = lax.rsqrt(
        jnp.mean(tokens * tokens, axis=1, keepdims=True) + norm_eps
    ) / math.sqrt(proj_width)
    keys[chip, core] = (tokens * token_scale).astype(jnp.bfloat16)
    w_copy.wait()
    pl.semaphore_wait(barrier, len(others))

    my_half = pl.ds(pl.multiple_of(core * hrows, hrows), hrows)
    w_out = []
    for step in range(1, group_axis):
        src = w_all.at[grp, my_half]
        copy = remote(src, src, w_send.at[step], w_recv.at[step], me, grp_peer(step))
        copy.start()
        w_out.append(copy)
    k_out = []
    for step in reversed(range(1, chips)):
        copy = remote(
            keys.at[chip, core], keys.at[chip, core], k_send.at[step], k_recv.at[step], chip_peer(step), grp
        )
        copy.start()
        k_out.append(copy)
    kf_out = [remote(keys.at[chip, core], keys.at[chip, core], kf_send.at[0], kf_recv.at[0], pair, grp)]
    kf_out[0].start()

    for copy in tables:
        copy.wait()
    gain_row = gain_ref[...].reshape(1, width)
    chip_tok = 2 * block_tok
    token_of = lax.broadcasted_iota(
        jnp.int32, (chip_tok, lemmas_all), 0
    ) - lemma_tok * lax.broadcasted_iota(jnp.int32, (chip_tok, lemmas_all), 1)
    token_of_t = lax.broadcasted_iota(
        jnp.int32, (lemmas_all, chip_tok), 1
    ) - lemma_tok * lax.broadcasted_iota(jnp.int32, (lemmas_all, chip_tok), 0)
    lengths = jnp.minimum(len_ref[...].reshape(1, lemmas_all), lemma_tok)
    lengths_t = jnp.broadcast_to(
        lengths.astype(jnp.float32), (lemmas_all, lemmas_all)
    ).T[:, :1].astype(jnp.int32)
    for block in range(chips):
        first = -block * chip_tok
        member = (token_of >= first) & (token_of < lengths + first)
        live[block] = jnp.where(member, 1.0, 0.0).astype(jnp.bfloat16)
        member = (token_of_t >= first) & (token_of_t < lengths_t + first)
        live_t[block] = jnp.where(member, 1.0, 0.0).astype(jnp.bfloat16)

    hid_copy.wait()
    in_float = hid[...].astype(jnp.float32)
    inv_rms = lax.rsqrt(jnp.mean(in_float * in_float, axis=1, keepdims=True) + norm_eps)
    scaled = (in_float * inv_rms * gain_row).astype(jnp.bfloat16)
    scaled_b[...] = scaled
    scaled_rows = scaled.T
    piece = wrows // lemma_axis
    for group in range(group_axis):
        for owner in range(lemma_axis):
            start = group * wrows + owner * piece
            scaled_t[owner // 2, owner % 2, group] = scaled_rows[start : start + piece]

    own_gain = gain_ref[pl.ds(pl.multiple_of(grp * wrows, 128), wrows)].reshape(1, wrows)
    gain_col = jnp.broadcast_to(own_gain, (proj_width, wrows)).T
    over_gain[...] = (w_all[grp].astype(jnp.float32) / gain_col).reshape(over_gain.shape)

    wf_out = []
    for step in range(1, group_axis):
        dst = w_all.at[grp_from(step), my_half]
        remote(dst, dst, w_send.at[step], w_recv.at[step], me, grp_peer(step)).wait_recv()
        copy = remote(dst, dst, wf_send.at[step], wf_recv.at[step], pair, grp)
        copy.start()
        wf_out.append(copy)
    other_half = pl.ds(pl.multiple_of((1 - core) * hrows, hrows), hrows)
    for step in range(1, group_axis):
        dst = w_all.at[grp_from(step), other_half]
        remote(dst, dst, wf_send.at[step], wf_recv.at[step], pair, grp).wait_recv()

    weight = w_all[...].reshape(width, proj_width)
    projected = jnp.dot(scaled_b[...], weight, preferred_element_type=jnp.float32)
    proj_scale = lax.rsqrt(
        jnp.mean(projected * projected, axis=1, keepdims=True) + norm_eps
    ) / math.sqrt(proj_width)
    query_unit = (projected * proj_scale).astype(jnp.bfloat16)

    def first_pass(block, total):
        scores = lax.dot_general(
            query_unit, keys[block].reshape(chip_tok, proj_width), NT, preferred_element_type=jnp.float32
        )
        exp_terms = jnp.exp(scores * (1.0 / token_temp)).astype(jnp.bfloat16)
        powers_b[block] = exp_terms
        return total + jnp.dot(exp_terms, live[block], preferred_element_type=jnp.float32)

    def forward(step):
        dst = keys.at[chip_source(step), core]
        remote(dst, dst, k_send.at[step], k_recv.at[step], chip_peer(step), grp).wait_recv()
        copy = remote(dst, dst, kf_send.at[step], kf_recv.at[step], pair, grp)
        copy.start()
        kf_out.append(copy)

    def chip_pass(step, total):
        source = chip_source(step)
        dst = keys.at[source, 1 - core]
        remote(dst, dst, kf_send.at[step], kf_recv.at[step], pair, grp).wait_recv()
        return first_pass(source, total)

    total = chip_pass(0, jnp.zeros((rows, lemmas_all), jnp.float32))
    for step in range(1, chips):
        forward(step)
        if step > 1:
            total = chip_pass(step - 1, total)
    total = chip_pass(chips - 1, total)

    tok_lse = token_temp * jnp.log(total)
    first_state = (me * group_axis + grp) * states_dev
    ratios = []
    losses = jnp.zeros((1, 128), jnp.float32)
    lane = lax.broadcasted_iota(jnp.int32, (1, 128), 1)
    for state in range(states_dev):
        length = qlen_ref[first_state + state]
        target = pos_ref[first_state + state]
        length_f = jnp.full((1, lemmas_all), length, jnp.int32).astype(jnp.float32)
        span = slice(state * query_tok, (state + 1) * query_tok)
        row_ids = lax.broadcasted_iota(jnp.int32, (query_tok, lemmas_all), 0)
        live_rows = jnp.where(row_ids < length, 1.0, 0.0)
        similarity = jnp.sum(tok_lse[span] * live_rows, axis=0, keepdims=True) / length_f
        powers = jnp.exp(similarity / state_temp)
        lemma_ids = lax.broadcasted_iota(jnp.int32, (1, lemmas_all), 1)
        is_positive = jnp.where(lemma_ids == target, 1.0, 0.0)
        partition = jnp.sum(powers, axis=1, keepdims=True)
        pos_score = jnp.sum(similarity * is_positive, axis=1, keepdims=True)
        loss = jnp.log(partition) - pos_score / state_temp
        losses = jnp.where(lane == state, loss, losses)
        grad_sim = loss_scale * (powers / partition - is_positive) / state_temp
        ratios.append(live_rows * (grad_sim / length_f) / total[span])
    loss_row[...] = losses
    loss_copy = pltpu.make_async_copy(loss_row, loss_ref, table_sem.at[4])
    loss_copy.start()
    ratio = jnp.concatenate(ratios, axis=0).astype(jnp.bfloat16)

    unit_grad = jnp.zeros((rows, proj_width), jnp.float32)
    for block in range(chips):
        spread = jnp.dot(ratio, live_t[block], preferred_element_type=jnp.float32)
        coef = (powers_b[block].astype(jnp.float32) * spread).astype(jnp.bfloat16)
        unit_grad += jnp.dot(
            coef, keys[block].reshape(chip_tok, proj_width), preferred_element_type=jnp.float32
        )
    proj_grad = proj_scale * unit_grad - projected * (
        proj_scale * proj_scale * proj_scale
    ) * jnp.sum(projected * unit_grad, axis=1, keepdims=True)
    proj_grad_b = proj_grad.astype(jnp.bfloat16)

    def weight_part(target, side):
        left = scaled_t[target, side].reshape(group_axis * piece, rows)
        return jnp.dot(left, proj_grad_b, preferred_element_type=jnp.float32).reshape(
            group_axis, piece, proj_width
        )

    order = list(reversed(range(chips)))
    p_out = []
    for step in order:
        part[step] = weight_part(chip_to(step), 1 - core).astype(jnp.bfloat16)
        copy = remote(part.at[step], pair_in.at[step], p_send.at[step], p_recv.at[step], pair, grp)
        copy.start()
        p_out.append(copy)
    grp_order = list(reversed(range(group_axis)))
    c_out = {}
    for step, pair_copy in zip(order, p_out):
        mine = weight_part(chip_to(step), core)
        pair_copy.wait_recv()
        half[step] = (mine + pair_in[step].astype(jnp.float32)).astype(jnp.bfloat16)
        if step:
            for grp_step in grp_order:
                copy = remote(
                    half.at[step, grp_peer(grp_step)], chip_in.at[step - 1, grp_step],
                    c_send.at[step - 1, grp_step], c_recv.at[step - 1, grp_step],
                    chip_peer(step), grp,
                )
                copy.start()
                c_out[step, grp_step] = copy

    row_dot = jnp.sum(projected * proj_grad_b.astype(jnp.float32), axis=1, keepdims=True)
    row_scale = inv_rms * inv_rms * row_dot / width

    def hidden_part(state):
        span = slice(state * query_tok, (state + 1) * query_tok)
        scaled_grad = lax.dot_general(
            proj_grad_b[span], w_all[...].reshape(width, proj_width), NT,
            preferred_element_type=jnp.float32,
        )
        hout[span] = (
            inv_rms[span] * (scaled_grad * gain_row)
            - hid[span].astype(jnp.float32) * row_scale[span]
        ).astype(jnp.bfloat16)
        copy = pltpu.make_async_copy(hout.at[span], hgrad_ref.at[span], local_sem.at[3 + state])
        copy.start()
        return copy

    hout_copies = [hidden_part(0)]

    g_out = []
    for grp_step in grp_order:
        chip_sum = half[0, grp_peer(grp_step)].astype(jnp.float32)
        for step in range(1, chips):
            c_out[step, grp_step].wait_recv()
            chip_sum += chip_in[step - 1, grp_step].astype(jnp.float32)
        if grp_step:
            quarter[grp_step] = chip_sum.astype(jnp.bfloat16)
            copy = remote(
                quarter.at[grp_step], grp_in.at[grp_step - 1],
                g_send.at[grp_step], g_recv.at[grp_step], me, grp_peer(grp_step),
            )
            copy.start()
            g_out.append(copy)
        else:
            grp_sum = chip_sum
    hout_copies += [hidden_part(state) for state in range(1, states_dev)]
    for copy in g_out:
        copy.wait_recv()
    for step in range(1, group_axis):
        grp_sum += grp_in[step - 1].astype(jnp.float32)
    own_raw = grp_sum.astype(jnp.bfloat16)
    raw[me] = own_raw
    own_raw = own_raw.astype(jnp.float32)
    own_gain_raw = jnp.sum(own_raw * over_gain[me], axis=1, keepdims=True)
    squares = jnp.sum(own_raw * own_raw) + jnp.sum(own_gain_raw * own_gain_raw)
    my_sq = sq.at[grp * lemma_axis + me]
    my_sq[...] = jnp.full((1, 128), squares, jnp.float32)
    for lemma_step, grp_step in reversed(others):
        copy = remote(
            my_sq, my_sq, s_send, s_recv,
            lax.rem(me + lemma_step, lemma_axis), grp_peer(grp_step),
        )
        copy.start()
    a_out = []
    for step in range(1, lemma_axis):
        copy = remote(
            raw.at[me], raw.at[me], a_send.at[step], a_recv.at[step],
            lax.rem(me + step, lemma_axis), grp,
        )
        copy.start()
        a_out.append(copy)
    for step in range(1, lemma_axis):
        dst = raw.at[lax.rem(me + lemma_axis - step, lemma_axis)]
        remote(dst, dst, a_send.at[step], a_recv.at[step], pair, grp).wait_recv()

    raw_copy = pltpu.make_async_copy(raw, raw_ref, table_sem.at[5])
    raw_copy.start()
    weight_raw = raw[...].reshape(wrows, proj_width).astype(jnp.float32)
    ones = jnp.ones((8, proj_width), jnp.float32)
    gain_raw = lax.dot_general(
        ones, over_gain[...].reshape(wrows, proj_width) * weight_raw, NT,
        preferred_element_type=jnp.float32, precision=lax.Precision.HIGHEST,
    )[:1]
    gain_out[...] = gain_raw
    gain_copy = pltpu.make_async_copy(gain_out, ggrad_ref, table_sem.at[6])
    gain_copy.start()
    all_but_one = sq.at[pl.ds(0, len(others))]
    remote(all_but_one, all_but_one, s_send, s_recv, pair, grp).wait()
    squares_all = jnp.sum(sq[...], axis=0)
    factor = jnp.minimum(1.0, grad_limit / jnp.sqrt(squares_all + norm_eps))
    factor_row[...] = factor
    factor_copy = pltpu.make_async_copy(factor_row, factor_ref, table_sem.at[7])
    factor_copy.start()

    for copy in w_out + k_out + wf_out + kf_out + p_out + list(c_out.values()) + g_out + a_out:
        copy.wait_send()
    for copy in hout_copies + [loss_copy, raw_copy, gain_copy, factor_copy]:
        copy.wait()


def place_kernel(
    loss, hgrad, raw, gain_raw, factor, loss_out, hgrad_out, wgrad_out, ggrad_out,
    loss_in, hbuf, raw_in, gain_in, factor_in, loss_row, wbuf, ggrad_row, sems,
):
    pairs = [(factor, factor_in), (raw, raw_in), (gain_raw, gain_in), (loss, loss_in), (hgrad, hbuf)]
    copies = [pltpu.make_async_copy(a, b, sems.at[i]) for i, (a, b) in enumerate(pairs)]
    for copy in copies:
        copy.start()
    pairs = [(wbuf, wgrad_out), (ggrad_row, ggrad_out), (loss_row, loss_out), (hbuf, hgrad_out)]
    backs = [pltpu.make_async_copy(a, b, sems.at[5 + i]) for i, (a, b) in enumerate(pairs)]
    copies[4].wait()
    backs[3].start()
    copies[0].wait()
    copies[1].wait()
    wbuf[...] = raw_in[...].reshape(wbuf.shape).astype(jnp.float32) * factor_in[...]
    backs[0].start()
    copies[2].wait()
    ggrad_row[...] = (gain_in[...] * factor_in[:, :1]).reshape(ggrad_row.shape)
    backs[1].start()
    copies[3].wait()
    loss_row[...] = loss_in[0, : loss_row.shape[0]]
    backs[2].start()
    for copy in backs:
        copy.wait()


def fused_body(hidden, gain, weight, lemma_emb, lemma_len, query_len, positive):
    states_dev, query_tok, width = hidden.shape
    wrows, proj_width = weight.shape
    lemma_dev, lemma_tok = lemma_emb.shape[:2]
    lemma_axis, group_axis = lax.axis_size("lemma"), lax.axis_size("grp")
    chips = lemma_axis // 2
    rows, block_tok = states_dev * query_tok, lemma_dev * lemma_tok
    piece = wrows // lemma_axis
    lemmas_all = lemma_dev * lemma_axis
    hbm = pl.BlockSpec(memory_space=pltpu.HBM)
    sem = pltpu.SemaphoreType.DMA
    bf16, f32 = jnp.bfloat16, jnp.float32
    outs = pl.pallas_call(
        functools.partial(
            fused_kernel, lemma_axis, group_axis, lemma_dev, lemma_tok, states_dev, query_tok
        ),
        out_shape=(
            jax.ShapeDtypeStruct((1, 128), f32),
            jax.ShapeDtypeStruct((rows, width), bf16),
            jax.ShapeDtypeStruct((lemma_axis, piece, proj_width), bf16),
            jax.ShapeDtypeStruct((1, wrows), f32),
            jax.ShapeDtypeStruct((1, 128), f32),
        ),
        in_specs=[hbm] * 7,
        out_specs=(hbm,) * 5,
        scratch_shapes=[
            pltpu.VMEM((width,), f32),
            pltpu.VMEM((lemmas_all,), jnp.int32),
            pltpu.SMEM(query_len.shape, jnp.int32),
            pltpu.SMEM(positive.shape, jnp.int32),
            pltpu.VMEM((1, 128), f32),
            pltpu.VMEM((1, wrows), f32),
            pltpu.VMEM((1, 128), f32),
            pltpu.VMEM((rows, width), bf16),
            pltpu.VMEM((block_tok, proj_width), bf16),
            pltpu.VMEM((rows, width), bf16),
            pltpu.VMEM((group_axis, wrows, proj_width), bf16),
            pltpu.VMEM((chips, 2, block_tok, proj_width), bf16),
            pltpu.VMEM((chips, 2 * block_tok, lemmas_all), bf16),
            pltpu.VMEM((chips, lemmas_all, 2 * block_tok), bf16),
            pltpu.VMEM((chips, rows, 2 * block_tok), bf16),
            pltpu.VMEM((rows, width), bf16),
            pltpu.VMEM((chips, 2, group_axis, piece, rows), bf16),
            pltpu.VMEM((chips, group_axis, piece, proj_width), bf16),
            pltpu.VMEM((chips, group_axis, piece, proj_width), bf16),
            pltpu.VMEM((chips, group_axis, piece, proj_width), bf16),
            pltpu.VMEM((chips - 1, group_axis, piece, proj_width), bf16),
            pltpu.VMEM((group_axis, piece, proj_width), bf16),
            pltpu.VMEM((group_axis - 1, piece, proj_width), bf16),
            pltpu.VMEM((lemma_axis, piece, proj_width), bf16),
            pltpu.VMEM((group_axis * lemma_axis, 1, 128), f32),
            pltpu.VMEM((lemma_axis, piece, proj_width), f32),
            sem((3 + states_dev,)), sem((8,)),
            sem((group_axis,)), sem((group_axis,)), sem((group_axis,)), sem((group_axis,)),
            sem((chips,)), sem((chips,)), sem((chips,)), sem((chips,)),
            sem((chips,)), sem((chips,)),
            sem((chips - 1, group_axis)), sem((chips - 1, group_axis)),
            sem((group_axis,)), sem((group_axis,)),
            sem((lemma_axis,)), sem((lemma_axis,)),
            sem, sem,
        ],
        compiler_params=pltpu.CompilerParams(
            collective_id=0, has_side_effects=True, vmem_limit_bytes=62 * 1024 * 1024
        ),
        cost_estimate=pl.CostEstimate(
            flops=2 * rows * proj_width * (3 * width + 4 * block_tok * lemma_axis),
            bytes_accessed=4 * rows * width * 2,
            transcendentals=rows * block_tok * lemma_axis,
        ),
    )(
        hidden.reshape(rows, width), gain, weight,
        lemma_emb.reshape(block_tok, proj_width), lemma_len,
        query_len, positive,
    )
    loss, hidden_grad, weight_grad, gain_grad = pl.pallas_call(
        place_kernel,
        out_shape=(
            jax.ShapeDtypeStruct((states_dev,), f32),
            jax.ShapeDtypeStruct((rows, width), bf16),
            jax.ShapeDtypeStruct((wrows, proj_width), f32),
            jax.ShapeDtypeStruct((wrows,), f32),
        ),
        in_specs=[hbm] * 5,
        out_specs=(hbm,) * 4,
        scratch_shapes=[
            pltpu.VMEM((1, 128), f32),
            pltpu.VMEM((rows, width), bf16),
            pltpu.VMEM((lemma_axis, piece, proj_width), bf16),
            pltpu.VMEM((1, wrows), f32),
            pltpu.VMEM((1, 128), f32),
            pltpu.VMEM((states_dev,), f32),
            pltpu.VMEM((wrows, proj_width), f32),
            pltpu.VMEM((wrows,), f32),
            sem((9,)),
        ],
        compiler_params=pltpu.CompilerParams(vmem_limit_bytes=62 * 1024 * 1024),
    )(*outs)
    return (loss, hidden_grad.reshape(hidden.shape), weight_grad, gain_grad)


def solution(mesh):
    in_specs = (
        P(("lemma", "grp"), None, None),
        P(),
        P("grp", None),
        P("lemma", None, None),
        P(),
        P(),
        P(),
    )
    out_specs = (P(("lemma", "grp")), P(("lemma", "grp"), None, None), P("grp", None), P("grp"))

    def run(hidden, gain, weight, *rest):
        rows = weight.shape[0] // mesh.shape["grp"]
        tiled = rows % (16 * mesh.shape["lemma"]) == 0 and rows % 128 == 0
        chosen = fused_body if tiled else body
        return jax.shard_map(
            chosen, mesh=mesh, in_specs=in_specs, out_specs=out_specs, check_vma=False
        )(hidden, gain, weight, *rest)

    return run
```

```python
import functools
import math

import jax
import jax.numpy as jnp
from jax import lax
from jax.experimental import pallas as pl
from jax.experimental.pallas import tpu as pltpu
from jax.sharding import PartitionSpec as P

token_temp = 0.05
state_temp = 0.05
loss_scale = 1024.0
grad_limit = 400.0
norm_eps = 1e-06


def contract_last(left, right):
    return lax.dot_general(
        left, right, (((1,), (1,)), ((), ())), preferred_element_type=jnp.float32
    )


def unit_rows(values):
    scale_rows = lax.rsqrt(jnp.mean(values * values, axis=-1, keepdims=True) + norm_eps)
    return values * scale_rows / math.sqrt(values.shape[-1])


def lemma_terms(queries, keys, key_live, lemma_count, lemma_tok):
    scores = contract_last(queries, keys)
    exp_terms = jnp.exp(scores / token_temp) * key_live[None, :]
    per_lemma = jnp.sum(exp_terms.reshape(queries.shape[0], lemma_count, lemma_tok), axis=2)
    return (exp_terms, per_lemma)


def token_grads(queries, grads, keys, key_live, lemma_count, lemma_tok):
    exp_terms, per_lemma = lemma_terms(queries, keys, key_live, lemma_count, lemma_tok)
    rows = queries.shape[0]
    weights = exp_terms.reshape(rows, lemma_count, lemma_tok) / per_lemma[:, :, None]
    coef = (weights * grads[:, :, None]).reshape(rows, lemma_count * lemma_tok).astype(jnp.bfloat16)
    return jnp.dot(coef, keys, preferred_element_type=jnp.float32)


def state_loss(tok_lse, live_rows, lengths_f, targets, lemma_ids):
    states = live_rows.shape[0]
    similarity = (
        jnp.sum(tok_lse.reshape(states, live_rows.shape[1], -1) * live_rows[:, :, None], axis=1)
        / lengths_f[:, None]
    )
    powers = jnp.exp(similarity / state_temp)
    is_positive = (lemma_ids[None, :] == targets[:, None]).astype(jnp.float32)
    return (similarity, powers, is_positive)


def body(hidden, gain, weight, lemma_emb, lemma_len, query_len, positive):
    states_dev, query_tok, width = hidden.shape
    proj_width = weight.shape[1]
    lemma_dev, lemma_tok = (lemma_emb.shape[0], lemma_emb.shape[1])
    lemma_axis = lax.axis_size("lemma")
    group_axis = lax.axis_size("grp")
    lemma_idx = lax.axis_index("lemma")
    group_idx = lax.axis_index("grp")
    own_rows = states_dev * query_tok
    lemmas_all = lemma_dev * lemma_axis
    in_float = hidden.reshape(own_rows, width).astype(jnp.float32)
    inv_rms = lax.rsqrt(jnp.mean(in_float * in_float, axis=1, keepdims=True) + norm_eps)
    normed = in_float * inv_rms
    scaled = (normed * gain[None, :]).astype(jnp.bfloat16)
    projected = jnp.dot(
        scaled,
        lax.all_gather(weight, "grp", axis=0, tiled=True),
        preferred_element_type=jnp.float32,
    )
    proj_scale = lax.rsqrt(
        jnp.mean(projected * projected, axis=1, keepdims=True) + norm_eps
    ) / math.sqrt(proj_width)
    query_unit = (projected * proj_scale).astype(jnp.bfloat16)
    lemma_unit = unit_rows(lemma_emb.astype(jnp.float32).reshape(-1, proj_width)).astype(
        jnp.bfloat16
    )
    all_live = (jnp.arange(lemma_tok)[None, :] < lemma_len[:, None]).astype(jnp.float32)
    block_start = (lemma_idx * group_axis + group_idx) * states_dev
    all_keys = lax.all_gather(lemma_unit, "lemma", axis=0, tiled=True)
    block_count = 8
    block_lemmas = lemmas_all // block_count
    key_blocks = all_keys.reshape(block_count, block_lemmas * lemma_tok, proj_width)
    live_blocks = all_live.reshape(block_count, block_lemmas * lemma_tok)
    own_len = lax.dynamic_slice_in_dim(query_len, block_start, states_dev)
    own_pos = lax.dynamic_slice_in_dim(positive, block_start, states_dev)
    live_rows = (jnp.arange(query_tok)[None, :] < own_len[:, None]).astype(jnp.float32)
    lengths_f = own_len.astype(jnp.float32)

    def block_lse(items):
        keys, key_live = items
        exp_terms, per_lemma = lemma_terms(query_unit, keys, key_live, block_lemmas, lemma_tok)
        return token_temp * jnp.log(per_lemma)

    tok_lse = lax.map(block_lse, (key_blocks, live_blocks))
    tok_lse = jnp.moveaxis(tok_lse, 0, 1).reshape(own_rows, lemmas_all)
    similarity, powers, is_positive = state_loss(
        tok_lse, live_rows, lengths_f, own_pos, jnp.arange(lemmas_all)
    )
    partition = jnp.sum(powers, axis=1)
    pos_score = jnp.sum(similarity * is_positive, axis=1)
    loss = jnp.log(partition) - pos_score / state_temp
    grad_sim = loss_scale * (powers / partition[:, None] - is_positive) / state_temp
    tok_grad = (grad_sim[:, None, :] * live_rows[:, :, None] / lengths_f[:, None, None]).reshape(
        own_rows, block_count, block_lemmas
    )
    grad_blocks = jnp.moveaxis(tok_grad, 1, 0)

    def add_block(acc, items):
        keys, key_live, grads = items
        return (acc + token_grads(query_unit, grads, keys, key_live, block_lemmas, lemma_tok), None)

    unit_grad, unused = lax.scan(
        add_block,
        jnp.zeros((own_rows, proj_width), jnp.float32),
        (key_blocks, live_blocks, grad_blocks),
    )
    proj_grad = proj_scale * unit_grad - projected * proj_scale**3 * jnp.sum(
        projected * unit_grad, axis=1, keepdims=True
    )
    proj_grad_b = proj_grad.astype(jnp.bfloat16)
    scaled_grad = contract_last(proj_grad_b, lax.all_gather(weight, "grp", axis=0, tiled=True))
    normed_grad = scaled_grad * gain[None, :]
    input_grad = (
        inv_rms * normed_grad
        - in_float * inv_rms**3 * jnp.sum(in_float * normed_grad, axis=1, keepdims=True) / width
    )
    hidden_grad = input_grad.astype(jnp.bfloat16).reshape(states_dev, query_tok, width)
    weight_part = lax.dot_general(
        scaled, proj_grad_b, (((0,), (0,)), ((), ())), preferred_element_type=jnp.float32
    )
    gain_part = jnp.sum(scaled_grad * normed, axis=0)
    weight_sum, gain_sum = (
        lax.psum(weight_part.astype(jnp.bfloat16), "lemma").astype(jnp.float32),
        lax.psum(gain_part.astype(jnp.bfloat16), "lemma").astype(jnp.float32),
    )
    weight_sum, gain_sum = (
        lax.psum_scatter(
            weight_sum.astype(jnp.bfloat16), "grp", scatter_dimension=0, tiled=True
        ).astype(jnp.float32),
        lax.psum_scatter(
            gain_sum.astype(jnp.bfloat16), "grp", scatter_dimension=0, tiled=True
        ).astype(jnp.float32),
    )
    squares = jnp.sum(weight_sum * weight_sum) + jnp.sum(gain_sum * gain_sum)
    total_squares = lax.psum(squares, "grp")
    factor = jnp.minimum(1.0, grad_limit / jnp.sqrt(total_squares + norm_eps))
    return (loss, hidden_grad, weight_sum * factor, gain_sum * factor)


NT = (((1,), (1,)), ((), ()))
MESH = pl.DeviceIdType.MESH


def fused_kernel(
    lemma_axis, group_axis, lemma_dev, lemma_tok, states_dev, query_tok,
    hidden_ref, gain_hbm, weight_ref, emb_ref, len_hbm, qlen_hbm, pos_hbm,
    loss_ref, hgrad_ref, raw_ref, ggrad_ref, factor_ref,
    gain_ref, len_ref, qlen_ref, pos_ref, loss_row, gain_out, factor_row,
    hid, emb, hout, w_all, keys, live, live_t, powers_b, scaled_b, scaled_t,
    part, pair_in, half, chip_in, quarter, grp_in, raw, sq, over_gain,
    local_sem, table_sem, w_send, w_recv, wf_send, wf_recv, k_send, k_recv, kf_send, kf_recv,
    p_send, p_recv, c_send, c_recv, g_send, g_recv, a_send, a_recv, s_send, s_recv,
):
    chips = lemma_axis // 2
    me, grp = lax.axis_index("lemma"), lax.axis_index("grp")
    chip, core = me // 2, lax.rem(me, 2)
    pair = chip * 2 + (1 - core)
    rows, width = hid.shape
    proj_width = weight_ref.shape[1]
    wrows = weight_ref.shape[0]
    hrows = wrows // 2
    block_tok = lemma_dev * lemma_tok
    lemmas_all = lemma_dev * lemma_axis

    across = 2 - chips % 2
    along = chips // across
    chip_y, chip_x = chip // across, lax.rem(chip, across)

    def chip_to(step):
        step_y, step_x = step // across, step % across
        return lax.rem(chip_y + step_y, along) * across + lax.rem(chip_x + step_x, across)

    def chip_source(step):
        step_y, step_x = step // across, step % across
        return lax.rem(chip_y + along - step_y, along) * across + lax.rem(
            chip_x + across - step_x, across
        )

    def chip_peer(step):
        return chip_to(step) * 2 + core

    def chip_from(step):
        return chip_source(step) * 2 + core

    def grp_peer(step):
        return lax.rem(grp + step, group_axis)

    def grp_from(step):
        return lax.rem(grp + group_axis - step, group_axis)

    def remote(src, dst, send_sem, recv_sem, to_lemma, to_grp):
        return pltpu.make_async_remote_copy(
            src_ref=src, dst_ref=dst, send_sem=send_sem, recv_sem=recv_sem,
            device_id=(to_lemma, to_grp), device_id_type=MESH,
        )

    emb_copy = pltpu.make_async_copy(emb_ref, emb, local_sem.at[0])
    hid_copy = pltpu.make_async_copy(hidden_ref, hid, local_sem.at[1])
    w_copy = pltpu.make_async_copy(weight_ref, w_all.at[grp], local_sem.at[2])
    emb_copy.start()
    w_copy.start()

    barrier = pltpu.get_barrier_semaphore()
    others = [
        (lemma_step, grp_step)
        for lemma_step in range(lemma_axis)
        for grp_step in range(group_axis)
        if lemma_step or grp_step
    ]
    for lemma_step, grp_step in others:
        pl.semaphore_signal(
            barrier, inc=1, device_id_type=MESH,
            device_id=(lax.rem(me + lemma_step, lemma_axis), grp_peer(grp_step)),
        )

    tables = [
        pltpu.make_async_copy(src, dst, table_sem.at[index])
        for index, (src, dst) in enumerate(
            [(len_hbm, len_ref), (gain_hbm, gain_ref), (qlen_hbm, qlen_ref), (pos_hbm, pos_ref)]
        )
    ]
    hid_copy.start()
    for copy in tables:
        copy.start()

    emb_copy.wait()
    tokens = emb[...].astype(jnp.float32)
    token_scale = lax.rsqrt(
        jnp.mean(tokens * tokens, axis=1, keepdims=True) + norm_eps
    ) / math.sqrt(proj_width)
    keys[chip, core] = (tokens * token_scale).astype(jnp.bfloat16)
    w_copy.wait()
    pl.semaphore_wait(barrier, len(others))

    my_half = pl.ds(pl.multiple_of(core * hrows, hrows), hrows)
    w_out = []
    for step in range(1, group_axis):
        src = w_all.at[grp, my_half]
        copy = remote(src, src, w_send.at[step], w_recv.at[step], me, grp_peer(step))
        copy.start()
        w_out.append(copy)
    k_out = []
    for step in reversed(range(1, chips)):
        copy = remote(
            keys.at[chip, core], keys.at[chip, core], k_send.at[step], k_recv.at[step], chip_peer(step), grp
        )
        copy.start()
        k_out.append(copy)
    kf_out = [remote(keys.at[chip, core], keys.at[chip, core], kf_send.at[0], kf_recv.at[0], pair, grp)]
    kf_out[0].start()

    for copy in tables:
        copy.wait()
    gain_row = gain_ref[...].reshape(1, width)
    chip_tok = 2 * block_tok
    token_of = lax.broadcasted_iota(
        jnp.int32, (chip_tok, lemmas_all), 0
    ) - lemma_tok * lax.broadcasted_iota(jnp.int32, (chip_tok, lemmas_all), 1)
    token_of_t = lax.broadcasted_iota(
        jnp.int32, (lemmas_all, chip_tok), 1
    ) - lemma_tok * lax.broadcasted_iota(jnp.int32, (lemmas_all, chip_tok), 0)
    lengths = jnp.minimum(len_ref[...].reshape(1, lemmas_all), lemma_tok)
    lengths_t = jnp.broadcast_to(
        lengths.astype(jnp.float32), (lemmas_all, lemmas_all)
    ).T[:, :1].astype(jnp.int32)
    for block in range(chips):
        first = -block * chip_tok
        member = (token_of >= first) & (token_of < lengths + first)
        live[block] = jnp.where(member, 1.0, 0.0).astype(jnp.bfloat16)
        member = (token_of_t >= first) & (token_of_t < lengths_t + first)
        live_t[block] = jnp.where(member, 1.0, 0.0).astype(jnp.bfloat16)

    hid_copy.wait()
    in_float = hid[...].astype(jnp.float32)
    inv_rms = lax.rsqrt(jnp.mean(in_float * in_float, axis=1, keepdims=True) + norm_eps)
    scaled = (in_float * inv_rms * gain_row).astype(jnp.bfloat16)
    scaled_b[...] = scaled
    scaled_rows = scaled.T
    piece = wrows // lemma_axis
    for group in range(group_axis):
        for owner in range(lemma_axis):
            start = group * wrows + owner * piece
            scaled_t[owner // 2, owner % 2, group] = scaled_rows[start : start + piece]

    own_gain = gain_ref[pl.ds(pl.multiple_of(grp * wrows, 128), wrows)].reshape(1, wrows)
    gain_col = jnp.broadcast_to(own_gain, (proj_width, wrows)).T
    over_gain[...] = (w_all[grp].astype(jnp.float32) / gain_col).reshape(over_gain.shape)

    wf_out = []
    for step in range(1, group_axis):
        dst = w_all.at[grp_from(step), my_half]
        remote(dst, dst, w_send.at[step], w_recv.at[step], me, grp_peer(step)).wait_recv()
        copy = remote(dst, dst, wf_send.at[step], wf_recv.at[step], pair, grp)
        copy.start()
        wf_out.append(copy)
    def forward(step):
        dst = keys.at[chip_source(step), core]
        remote(dst, dst, k_send.at[step], k_recv.at[step], chip_peer(step), grp).wait_recv()
        copy = remote(dst, dst, kf_send.at[step], kf_recv.at[step], pair, grp)
        copy.start()
        kf_out.append(copy)

    for step in range(1, chips - 1):
        forward(step)
    other_half = pl.ds(pl.multiple_of((1 - core) * hrows, hrows), hrows)
    for step in range(1, group_axis):
        dst = w_all.at[grp_from(step), other_half]
        remote(dst, dst, wf_send.at[step], wf_recv.at[step], pair, grp).wait_recv()

    weight = w_all[...].reshape(width, proj_width)
    projected = jnp.dot(scaled_b[...], weight, preferred_element_type=jnp.float32)
    proj_scale = lax.rsqrt(
        jnp.mean(projected * projected, axis=1, keepdims=True) + norm_eps
    ) / math.sqrt(proj_width)
    query_unit = (projected * proj_scale).astype(jnp.bfloat16)

    def first_pass(block, total):
        scores = lax.dot_general(
            query_unit, keys[block].reshape(chip_tok, proj_width), NT, preferred_element_type=jnp.float32
        )
        exp_terms = jnp.exp(scores * (1.0 / token_temp)).astype(jnp.bfloat16)
        powers_b[block] = exp_terms
        return total + jnp.dot(exp_terms, live[block], preferred_element_type=jnp.float32)

    def chip_pass(step, total):
        source = chip_source(step)
        dst = keys.at[source, 1 - core]
        remote(dst, dst, kf_send.at[step], kf_recv.at[step], pair, grp).wait_recv()
        return first_pass(source, total)

    forward(chips - 1)
    total = jnp.zeros((rows, lemmas_all), jnp.float32)
    for step in range(chips):
        total = chip_pass(step, total)

    tok_lse = token_temp * jnp.log(total)
    first_state = (me * group_axis + grp) * states_dev
    ratios = []
    losses = jnp.zeros((1, 128), jnp.float32)
    lane = lax.broadcasted_iota(jnp.int32, (1, 128), 1)
    for state in range(states_dev):
        length = qlen_ref[first_state + state]
        target = pos_ref[first_state + state]
        length_f = jnp.full((1, lemmas_all), length, jnp.int32).astype(jnp.float32)
        span = slice(state * query_tok, (state + 1) * query_tok)
        row_ids = lax.broadcasted_iota(jnp.int32, (query_tok, lemmas_all), 0)
        live_rows = jnp.where(row_ids < length, 1.0, 0.0)
        similarity = jnp.sum(tok_lse[span] * live_rows, axis=0, keepdims=True) / length_f
        powers = jnp.exp(similarity / state_temp)
        lemma_ids = lax.broadcasted_iota(jnp.int32, (1, lemmas_all), 1)
        is_positive = jnp.where(lemma_ids == target, 1.0, 0.0)
        partition = jnp.sum(powers, axis=1, keepdims=True)
        pos_score = jnp.sum(similarity * is_positive, axis=1, keepdims=True)
        loss = jnp.log(partition) - pos_score / state_temp
        losses = jnp.where(lane == state, loss, losses)
        grad_sim = loss_scale * (powers / partition - is_positive) / state_temp
        ratios.append(live_rows * (grad_sim / length_f) / total[span])
    loss_row[...] = losses
    loss_copy = pltpu.make_async_copy(loss_row, loss_ref, table_sem.at[4])
    loss_copy.start()
    ratio = jnp.concatenate(ratios, axis=0).astype(jnp.bfloat16)

    unit_grad = jnp.zeros((rows, proj_width), jnp.float32)
    for block in range(chips):
        spread = jnp.dot(ratio, live_t[block], preferred_element_type=jnp.float32)
        coef = (powers_b[block].astype(jnp.float32) * spread).astype(jnp.bfloat16)
        unit_grad += jnp.dot(
            coef, keys[block].reshape(chip_tok, proj_width), preferred_element_type=jnp.float32
        )
    proj_grad = proj_scale * unit_grad - projected * (
        proj_scale * proj_scale * proj_scale
    ) * jnp.sum(projected * unit_grad, axis=1, keepdims=True)
    proj_grad_b = proj_grad.astype(jnp.bfloat16)

    def weight_part(target, side):
        left = scaled_t[target, side].reshape(group_axis * piece, rows)
        return jnp.dot(left, proj_grad_b, preferred_element_type=jnp.float32).reshape(
            group_axis, piece, proj_width
        )

    order = list(reversed(range(chips)))
    p_out = []
    for step in order:
        part[step] = weight_part(chip_to(step), 1 - core).astype(jnp.bfloat16)
        copy = remote(part.at[step], pair_in.at[step], p_send.at[step], p_recv.at[step], pair, grp)
        copy.start()
        p_out.append(copy)
    grp_order = list(reversed(range(group_axis)))
    c_out = {}
    for step, pair_copy in zip(order, p_out):
        mine = weight_part(chip_to(step), core)
        pair_copy.wait_recv()
        half[step] = (mine + pair_in[step].astype(jnp.float32)).astype(jnp.bfloat16)
        if step:
            for grp_step in grp_order:
                copy = remote(
                    half.at[step, grp_peer(grp_step)], chip_in.at[step - 1, grp_step],
                    c_send.at[step - 1, grp_step], c_recv.at[step - 1, grp_step],
                    chip_peer(step), grp,
                )
                copy.start()
                c_out[step, grp_step] = copy

    row_dot = jnp.sum(projected * proj_grad_b.astype(jnp.float32), axis=1, keepdims=True)
    row_scale = inv_rms * inv_rms * row_dot / width

    def hidden_part(state):
        span = slice(state * query_tok, (state + 1) * query_tok)
        scaled_grad = lax.dot_general(
            proj_grad_b[span], w_all[...].reshape(width, proj_width), NT,
            preferred_element_type=jnp.float32,
        )
        hout[span] = (
            inv_rms[span] * (scaled_grad * gain_row)
            - hid[span].astype(jnp.float32) * row_scale[span]
        ).astype(jnp.bfloat16)
        copy = pltpu.make_async_copy(hout.at[span], hgrad_ref.at[span], local_sem.at[3 + state])
        copy.start()
        return copy

    hout_copies = [hidden_part(0)]

    g_out = []
    for grp_step in grp_order:
        chip_sum = half[0, grp_peer(grp_step)].astype(jnp.float32)
        for step in range(1, chips):
            c_out[step, grp_step].wait_recv()
            chip_sum += chip_in[step - 1, grp_step].astype(jnp.float32)
        if grp_step:
            quarter[grp_step] = chip_sum.astype(jnp.bfloat16)
            copy = remote(
                quarter.at[grp_step], grp_in.at[grp_step - 1],
                g_send.at[grp_step], g_recv.at[grp_step], me, grp_peer(grp_step),
            )
            copy.start()
            g_out.append(copy)
        else:
            grp_sum = chip_sum
    hout_copies += [hidden_part(state) for state in range(1, states_dev)]
    for copy in g_out:
        copy.wait_recv()
    for step in range(1, group_axis):
        grp_sum += grp_in[step - 1].astype(jnp.float32)
    own_raw = grp_sum.astype(jnp.bfloat16)
    raw[me] = own_raw
    own_raw = own_raw.astype(jnp.float32)
    own_gain_raw = jnp.sum(own_raw * over_gain[me], axis=1, keepdims=True)
    squares = jnp.sum(own_raw * own_raw) + jnp.sum(own_gain_raw * own_gain_raw)
    my_sq = sq.at[grp * lemma_axis + me]
    my_sq[...] = jnp.full((1, 128), squares, jnp.float32)
    for lemma_step, grp_step in reversed(others):
        copy = remote(
            my_sq, my_sq, s_send, s_recv,
            lax.rem(me + lemma_step, lemma_axis), grp_peer(grp_step),
        )
        copy.start()
    a_out = []
    for step in range(1, lemma_axis):
        copy = remote(
            raw.at[me], raw.at[me], a_send.at[step], a_recv.at[step],
            lax.rem(me + step, lemma_axis), grp,
        )
        copy.start()
        a_out.append(copy)
    for step in range(1, lemma_axis):
        dst = raw.at[lax.rem(me + lemma_axis - step, lemma_axis)]
        remote(dst, dst, a_send.at[step], a_recv.at[step], pair, grp).wait_recv()

    raw_copy = pltpu.make_async_copy(raw, raw_ref, table_sem.at[5])
    raw_copy.start()
    weight_raw = raw[...].reshape(wrows, proj_width).astype(jnp.float32)
    ones = jnp.ones((8, proj_width), jnp.float32)
    gain_raw = lax.dot_general(
        ones, over_gain[...].reshape(wrows, proj_width) * weight_raw, NT,
        preferred_element_type=jnp.float32, precision=lax.Precision.HIGHEST,
    )[:1]
    gain_out[...] = gain_raw
    gain_copy = pltpu.make_async_copy(gain_out, ggrad_ref, table_sem.at[6])
    gain_copy.start()
    all_but_one = sq.at[pl.ds(0, len(others))]
    remote(all_but_one, all_but_one, s_send, s_recv, pair, grp).wait()
    squares_all = jnp.sum(sq[...], axis=0)
    factor = jnp.minimum(1.0, grad_limit / jnp.sqrt(squares_all + norm_eps))
    factor_row[...] = factor
    factor_copy = pltpu.make_async_copy(factor_row, factor_ref, table_sem.at[7])
    factor_copy.start()

    for copy in w_out + k_out + wf_out + kf_out + p_out + list(c_out.values()) + g_out + a_out:
        copy.wait_send()
    for copy in hout_copies + [loss_copy, raw_copy, gain_copy, factor_copy]:
        copy.wait()


def place_kernel(
    loss, hgrad, raw, gain_raw, factor, loss_out, hgrad_out, wgrad_out, ggrad_out,
    loss_in, hbuf, raw_in, gain_in, factor_in, loss_row, wbuf, ggrad_row, sems,
):
    pairs = [(factor, factor_in), (raw, raw_in), (gain_raw, gain_in), (loss, loss_in), (hgrad, hbuf)]
    copies = [pltpu.make_async_copy(a, b, sems.at[i]) for i, (a, b) in enumerate(pairs)]
    for copy in copies:
        copy.start()
    pairs = [(wbuf, wgrad_out), (ggrad_row, ggrad_out), (loss_row, loss_out), (hbuf, hgrad_out)]
    backs = [pltpu.make_async_copy(a, b, sems.at[5 + i]) for i, (a, b) in enumerate(pairs)]
    copies[4].wait()
    backs[3].start()
    copies[0].wait()
    copies[1].wait()
    wbuf[...] = raw_in[...].reshape(wbuf.shape).astype(jnp.float32) * factor_in[...]
    backs[0].start()
    copies[2].wait()
    ggrad_row[...] = (gain_in[...] * factor_in[:, :1]).reshape(ggrad_row.shape)
    backs[1].start()
    copies[3].wait()
    loss_row[...] = loss_in[0, : loss_row.shape[0]]
    backs[2].start()
    for copy in backs:
        copy.wait()


def fused_body(hidden, gain, weight, lemma_emb, lemma_len, query_len, positive):
    states_dev, query_tok, width = hidden.shape
    wrows, proj_width = weight.shape
    lemma_dev, lemma_tok = lemma_emb.shape[:2]
    lemma_axis, group_axis = lax.axis_size("lemma"), lax.axis_size("grp")
    chips = lemma_axis // 2
    rows, block_tok = states_dev * query_tok, lemma_dev * lemma_tok
    piece = wrows // lemma_axis
    lemmas_all = lemma_dev * lemma_axis
    hbm = pl.BlockSpec(memory_space=pltpu.HBM)
    sem = pltpu.SemaphoreType.DMA
    bf16, f32 = jnp.bfloat16, jnp.float32
    outs = pl.pallas_call(
        functools.partial(
            fused_kernel, lemma_axis, group_axis, lemma_dev, lemma_tok, states_dev, query_tok
        ),
        out_shape=(
            jax.ShapeDtypeStruct((1, 128), f32),
            jax.ShapeDtypeStruct((rows, width), bf16),
            jax.ShapeDtypeStruct((lemma_axis, piece, proj_width), bf16),
            jax.ShapeDtypeStruct((1, wrows), f32),
            jax.ShapeDtypeStruct((1, 128), f32),
        ),
        in_specs=[hbm] * 7,
        out_specs=(hbm,) * 5,
        scratch_shapes=[
            pltpu.VMEM((width,), f32),
            pltpu.VMEM((lemmas_all,), jnp.int32),
            pltpu.SMEM(query_len.shape, jnp.int32),
            pltpu.SMEM(positive.shape, jnp.int32),
            pltpu.VMEM((1, 128), f32),
            pltpu.VMEM((1, wrows), f32),
            pltpu.VMEM((1, 128), f32),
            pltpu.VMEM((rows, width), bf16),
            pltpu.VMEM((block_tok, proj_width), bf16),
            pltpu.VMEM((rows, width), bf16),
            pltpu.VMEM((group_axis, wrows, proj_width), bf16),
            pltpu.VMEM((chips, 2, block_tok, proj_width), bf16),
            pltpu.VMEM((chips, 2 * block_tok, lemmas_all), bf16),
            pltpu.VMEM((chips, lemmas_all, 2 * block_tok), bf16),
            pltpu.VMEM((chips, rows, 2 * block_tok), bf16),
            pltpu.VMEM((rows, width), bf16),
            pltpu.VMEM((chips, 2, group_axis, piece, rows), bf16),
            pltpu.VMEM((chips, group_axis, piece, proj_width), bf16),
            pltpu.VMEM((chips, group_axis, piece, proj_width), bf16),
            pltpu.VMEM((chips, group_axis, piece, proj_width), bf16),
            pltpu.VMEM((chips - 1, group_axis, piece, proj_width), bf16),
            pltpu.VMEM((group_axis, piece, proj_width), bf16),
            pltpu.VMEM((group_axis - 1, piece, proj_width), bf16),
            pltpu.VMEM((lemma_axis, piece, proj_width), bf16),
            pltpu.VMEM((group_axis * lemma_axis, 1, 128), f32),
            pltpu.VMEM((lemma_axis, piece, proj_width), f32),
            sem((3 + states_dev,)), sem((8,)),
            sem((group_axis,)), sem((group_axis,)), sem((group_axis,)), sem((group_axis,)),
            sem((chips,)), sem((chips,)), sem((chips,)), sem((chips,)),
            sem((chips,)), sem((chips,)),
            sem((chips - 1, group_axis)), sem((chips - 1, group_axis)),
            sem((group_axis,)), sem((group_axis,)),
            sem((lemma_axis,)), sem((lemma_axis,)),
            sem, sem,
        ],
        compiler_params=pltpu.CompilerParams(
            collective_id=0, has_side_effects=True, vmem_limit_bytes=62 * 1024 * 1024
        ),
        cost_estimate=pl.CostEstimate(
            flops=2 * rows * proj_width * (3 * width + 4 * block_tok * lemma_axis),
            bytes_accessed=4 * rows * width * 2,
            transcendentals=rows * block_tok * lemma_axis,
        ),
    )(
        hidden.reshape(rows, width), gain, weight,
        lemma_emb.reshape(block_tok, proj_width), lemma_len,
        query_len, positive,
    )
    loss, hidden_grad, weight_grad, gain_grad = pl.pallas_call(
        place_kernel,
        out_shape=(
            jax.ShapeDtypeStruct((states_dev,), f32),
            jax.ShapeDtypeStruct((rows, width), bf16),
            jax.ShapeDtypeStruct((wrows, proj_width), f32),
            jax.ShapeDtypeStruct((wrows,), f32),
        ),
        in_specs=[hbm] * 5,
        out_specs=(hbm,) * 4,
        scratch_shapes=[
            pltpu.VMEM((1, 128), f32),
            pltpu.VMEM((rows, width), bf16),
            pltpu.VMEM((lemma_axis, piece, proj_width), bf16),
            pltpu.VMEM((1, wrows), f32),
            pltpu.VMEM((1, 128), f32),
            pltpu.VMEM((states_dev,), f32),
            pltpu.VMEM((wrows, proj_width), f32),
            pltpu.VMEM((wrows,), f32),
            sem((9,)),
        ],
        compiler_params=pltpu.CompilerParams(vmem_limit_bytes=62 * 1024 * 1024),
    )(*outs)
    return (loss, hidden_grad.reshape(hidden.shape), weight_grad, gain_grad)


def solution(mesh):
    in_specs = (
        P(("lemma", "grp"), None, None),
        P(),
        P("grp", None),
        P("lemma", None, None),
        P(),
        P(),
        P(),
    )
    out_specs = (P(("lemma", "grp")), P(("lemma", "grp"), None, None), P("grp", None), P("grp"))

    def run(hidden, gain, weight, *rest):
        rows = weight.shape[0] // mesh.shape["grp"]
        tiled = rows % (16 * mesh.shape["lemma"]) == 0 and rows % 128 == 0
        chosen = fused_body if tiled else body
        return jax.shard_map(
            chosen, mesh=mesh, in_specs=in_specs, out_specs=out_specs, check_vma=False
        )(hidden, gain, weight, *rest)

    return run
```

```python
import functools
import math

import jax
import jax.numpy as jnp
from jax import lax
from jax.experimental import pallas as pl
from jax.experimental.pallas import tpu as pltpu
from jax.sharding import PartitionSpec as P

token_temp = 0.05
state_temp = 0.05
loss_scale = 1024.0
grad_limit = 400.0
norm_eps = 1e-06


def contract_last(left, right):
    return lax.dot_general(
        left, right, (((1,), (1,)), ((), ())), preferred_element_type=jnp.float32
    )


def unit_rows(values):
    scale_rows = lax.rsqrt(jnp.mean(values * values, axis=-1, keepdims=True) + norm_eps)
    return values * scale_rows / math.sqrt(values.shape[-1])


def lemma_terms(queries, keys, key_live, lemma_count, lemma_tok):
    scores = contract_last(queries, keys)
    exp_terms = jnp.exp(scores / token_temp) * key_live[None, :]
    per_lemma = jnp.sum(exp_terms.reshape(queries.shape[0], lemma_count, lemma_tok), axis=2)
    return (exp_terms, per_lemma)


def token_grads(queries, grads, keys, key_live, lemma_count, lemma_tok):
    exp_terms, per_lemma = lemma_terms(queries, keys, key_live, lemma_count, lemma_tok)
    rows = queries.shape[0]
    weights = exp_terms.reshape(rows, lemma_count, lemma_tok) / per_lemma[:, :, None]
    coef = (weights * grads[:, :, None]).reshape(rows, lemma_count * lemma_tok).astype(jnp.bfloat16)
    return jnp.dot(coef, keys, preferred_element_type=jnp.float32)


def state_loss(tok_lse, live_rows, lengths_f, targets, lemma_ids):
    states = live_rows.shape[0]
    similarity = (
        jnp.sum(tok_lse.reshape(states, live_rows.shape[1], -1) * live_rows[:, :, None], axis=1)
        / lengths_f[:, None]
    )
    powers = jnp.exp(similarity / state_temp)
    is_positive = (lemma_ids[None, :] == targets[:, None]).astype(jnp.float32)
    return (similarity, powers, is_positive)


def body(hidden, gain, weight, lemma_emb, lemma_len, query_len, positive):
    states_dev, query_tok, width = hidden.shape
    proj_width = weight.shape[1]
    lemma_dev, lemma_tok = (lemma_emb.shape[0], lemma_emb.shape[1])
    lemma_axis = lax.axis_size("lemma")
    group_axis = lax.axis_size("grp")
    lemma_idx = lax.axis_index("lemma")
    group_idx = lax.axis_index("grp")
    own_rows = states_dev * query_tok
    lemmas_all = lemma_dev * lemma_axis
    in_float = hidden.reshape(own_rows, width).astype(jnp.float32)
    inv_rms = lax.rsqrt(jnp.mean(in_float * in_float, axis=1, keepdims=True) + norm_eps)
    normed = in_float * inv_rms
    scaled = (normed * gain[None, :]).astype(jnp.bfloat16)
    projected = jnp.dot(
        scaled,
        lax.all_gather(weight, "grp", axis=0, tiled=True),
        preferred_element_type=jnp.float32,
    )
    proj_scale = lax.rsqrt(
        jnp.mean(projected * projected, axis=1, keepdims=True) + norm_eps
    ) / math.sqrt(proj_width)
    query_unit = (projected * proj_scale).astype(jnp.bfloat16)
    lemma_unit = unit_rows(lemma_emb.astype(jnp.float32).reshape(-1, proj_width)).astype(
        jnp.bfloat16
    )
    all_live = (jnp.arange(lemma_tok)[None, :] < lemma_len[:, None]).astype(jnp.float32)
    block_start = (lemma_idx * group_axis + group_idx) * states_dev
    all_keys = lax.all_gather(lemma_unit, "lemma", axis=0, tiled=True)
    block_count = 8
    block_lemmas = lemmas_all // block_count
    key_blocks = all_keys.reshape(block_count, block_lemmas * lemma_tok, proj_width)
    live_blocks = all_live.reshape(block_count, block_lemmas * lemma_tok)
    own_len = lax.dynamic_slice_in_dim(query_len, block_start, states_dev)
    own_pos = lax.dynamic_slice_in_dim(positive, block_start, states_dev)
    live_rows = (jnp.arange(query_tok)[None, :] < own_len[:, None]).astype(jnp.float32)
    lengths_f = own_len.astype(jnp.float32)

    def block_lse(items):
        keys, key_live = items
        exp_terms, per_lemma = lemma_terms(query_unit, keys, key_live, block_lemmas, lemma_tok)
        return token_temp * jnp.log(per_lemma)

    tok_lse = lax.map(block_lse, (key_blocks, live_blocks))
    tok_lse = jnp.moveaxis(tok_lse, 0, 1).reshape(own_rows, lemmas_all)
    similarity, powers, is_positive = state_loss(
        tok_lse, live_rows, lengths_f, own_pos, jnp.arange(lemmas_all)
    )
    partition = jnp.sum(powers, axis=1)
    pos_score = jnp.sum(similarity * is_positive, axis=1)
    loss = jnp.log(partition) - pos_score / state_temp
    grad_sim = loss_scale * (powers / partition[:, None] - is_positive) / state_temp
    tok_grad = (grad_sim[:, None, :] * live_rows[:, :, None] / lengths_f[:, None, None]).reshape(
        own_rows, block_count, block_lemmas
    )
    grad_blocks = jnp.moveaxis(tok_grad, 1, 0)

    def add_block(acc, items):
        keys, key_live, grads = items
        return (acc + token_grads(query_unit, grads, keys, key_live, block_lemmas, lemma_tok), None)

    unit_grad, unused = lax.scan(
        add_block,
        jnp.zeros((own_rows, proj_width), jnp.float32),
        (key_blocks, live_blocks, grad_blocks),
    )
    proj_grad = proj_scale * unit_grad - projected * proj_scale**3 * jnp.sum(
        projected * unit_grad, axis=1, keepdims=True
    )
    proj_grad_b = proj_grad.astype(jnp.bfloat16)
    scaled_grad = contract_last(proj_grad_b, lax.all_gather(weight, "grp", axis=0, tiled=True))
    normed_grad = scaled_grad * gain[None, :]
    input_grad = (
        inv_rms * normed_grad
        - in_float * inv_rms**3 * jnp.sum(in_float * normed_grad, axis=1, keepdims=True) / width
    )
    hidden_grad = input_grad.astype(jnp.bfloat16).reshape(states_dev, query_tok, width)
    weight_part = lax.dot_general(
        scaled, proj_grad_b, (((0,), (0,)), ((), ())), preferred_element_type=jnp.float32
    )
    gain_part = jnp.sum(scaled_grad * normed, axis=0)
    weight_sum, gain_sum = (
        lax.psum(weight_part.astype(jnp.bfloat16), "lemma").astype(jnp.float32),
        lax.psum(gain_part.astype(jnp.bfloat16), "lemma").astype(jnp.float32),
    )
    weight_sum, gain_sum = (
        lax.psum_scatter(
            weight_sum.astype(jnp.bfloat16), "grp", scatter_dimension=0, tiled=True
        ).astype(jnp.float32),
        lax.psum_scatter(
            gain_sum.astype(jnp.bfloat16), "grp", scatter_dimension=0, tiled=True
        ).astype(jnp.float32),
    )
    squares = jnp.sum(weight_sum * weight_sum) + jnp.sum(gain_sum * gain_sum)
    total_squares = lax.psum(squares, "grp")
    factor = jnp.minimum(1.0, grad_limit / jnp.sqrt(total_squares + norm_eps))
    return (loss, hidden_grad, weight_sum * factor, gain_sum * factor)


NT = (((1,), (1,)), ((), ()))
MESH = pl.DeviceIdType.MESH


def fused_kernel(
    lemma_axis, group_axis, lemma_dev, lemma_tok, states_dev, query_tok,
    hidden_ref, gain_hbm, weight_ref, emb_ref, len_hbm, qlen_hbm, pos_hbm,
    loss_ref, hgrad_ref, raw_ref, ggrad_ref, factor_ref,
    gain_ref, len_ref, qlen_ref, pos_ref, loss_row, gain_out, factor_row,
    hid, emb, hout, w_all, keys, live, live_t, powers_b, scaled_b, scaled_t,
    part, pair_in, half, chip_in, quarter, grp_in, raw, sq, over_gain,
    local_sem, table_sem, w_send, w_recv, wf_send, wf_recv, k_send, k_recv, kf_send, kf_recv,
    p_send, p_recv, c_send, c_recv, g_send, g_recv, a_send, a_recv, s_send, s_recv,
):
    chips = lemma_axis // 2
    me, grp = lax.axis_index("lemma"), lax.axis_index("grp")
    chip, core = me // 2, lax.rem(me, 2)
    pair = chip * 2 + (1 - core)
    rows, width = hid.shape
    proj_width = weight_ref.shape[1]
    wrows = weight_ref.shape[0]
    hrows = wrows // 2
    block_tok = lemma_dev * lemma_tok
    lemmas_all = lemma_dev * lemma_axis

    across = 2 - chips % 2
    along = chips // across
    chip_y, chip_x = chip // across, lax.rem(chip, across)

    def chip_to(step):
        step_y, step_x = step // across, step % across
        return lax.rem(chip_y + step_y, along) * across + lax.rem(chip_x + step_x, across)

    def chip_source(step):
        step_y, step_x = step // across, step % across
        return lax.rem(chip_y + along - step_y, along) * across + lax.rem(
            chip_x + across - step_x, across
        )

    def chip_peer(step):
        return chip_to(step) * 2 + core

    def chip_from(step):
        return chip_source(step) * 2 + core

    def grp_peer(step):
        return lax.rem(grp + step, group_axis)

    def grp_from(step):
        return lax.rem(grp + group_axis - step, group_axis)

    def remote(src, dst, send_sem, recv_sem, to_lemma, to_grp):
        return pltpu.make_async_remote_copy(
            src_ref=src, dst_ref=dst, send_sem=send_sem, recv_sem=recv_sem,
            device_id=(to_lemma, to_grp), device_id_type=MESH,
        )

    emb_copy = pltpu.make_async_copy(emb_ref, emb, local_sem.at[0])
    hid_copy = pltpu.make_async_copy(hidden_ref, hid, local_sem.at[1])
    w_copy = pltpu.make_async_copy(weight_ref, w_all.at[grp], local_sem.at[2])
    emb_copy.start()
    w_copy.start()

    barrier = pltpu.get_barrier_semaphore()
    others = [
        (lemma_step, grp_step)
        for lemma_step in range(lemma_axis)
        for grp_step in range(group_axis)
        if lemma_step or grp_step
    ]
    for lemma_step, grp_step in others:
        pl.semaphore_signal(
            barrier, inc=1, device_id_type=MESH,
            device_id=(lax.rem(me + lemma_step, lemma_axis), grp_peer(grp_step)),
        )

    tables = [
        pltpu.make_async_copy(src, dst, table_sem.at[index])
        for index, (src, dst) in enumerate(
            [(len_hbm, len_ref), (gain_hbm, gain_ref), (qlen_hbm, qlen_ref), (pos_hbm, pos_ref)]
        )
    ]
    hid_copy.start()
    for copy in tables:
        copy.start()

    emb_copy.wait()
    tokens = emb[...].astype(jnp.float32)
    token_scale = lax.rsqrt(
        jnp.mean(tokens * tokens, axis=1, keepdims=True) + norm_eps
    ) / math.sqrt(proj_width)
    keys[chip, core] = (tokens * token_scale).astype(jnp.bfloat16)
    w_copy.wait()
    pl.semaphore_wait(barrier, len(others))

    my_half = pl.ds(pl.multiple_of(core * hrows, hrows), hrows)
    w_out = []
    for step in range(1, group_axis):
        src = w_all.at[grp, my_half]
        copy = remote(src, src, w_send.at[step], w_recv.at[step], me, grp_peer(step))
        copy.start()
        w_out.append(copy)
    k_out = []
    for step in reversed(range(1, chips)):
        copy = remote(
            keys.at[chip, core], keys.at[chip, core], k_send.at[step], k_recv.at[step], chip_peer(step), grp
        )
        copy.start()
        k_out.append(copy)
    kf_out = [remote(keys.at[chip, core], keys.at[chip, core], kf_send.at[0], kf_recv.at[0], pair, grp)]
    kf_out[0].start()

    for copy in tables:
        copy.wait()
    gain_row = gain_ref[...].reshape(1, width)
    chip_tok = 2 * block_tok
    token_of = lax.broadcasted_iota(
        jnp.int32, (chip_tok, lemmas_all), 0
    ) - lemma_tok * lax.broadcasted_iota(jnp.int32, (chip_tok, lemmas_all), 1)
    token_of_t = lax.broadcasted_iota(
        jnp.int32, (lemmas_all, chip_tok), 1
    ) - lemma_tok * lax.broadcasted_iota(jnp.int32, (lemmas_all, chip_tok), 0)
    lengths = jnp.minimum(len_ref[...].reshape(1, lemmas_all), lemma_tok)
    lengths_t = jnp.broadcast_to(
        lengths.astype(jnp.float32), (lemmas_all, lemmas_all)
    ).T[:, :1].astype(jnp.int32)
    for block in range(chips):
        first = -block * chip_tok
        member = (token_of >= first) & (token_of < lengths + first)
        live[block] = jnp.where(member, 1.0, 0.0).astype(jnp.bfloat16)
        member = (token_of_t >= first) & (token_of_t < lengths_t + first)
        live_t[block] = jnp.where(member, 1.0, 0.0).astype(jnp.bfloat16)

    hid_copy.wait()
    in_float = hid[...].astype(jnp.float32)
    inv_rms = lax.rsqrt(jnp.mean(in_float * in_float, axis=1, keepdims=True) + norm_eps)
    scaled = (in_float * inv_rms * gain_row).astype(jnp.bfloat16)
    scaled_b[...] = scaled
    scaled_rows = scaled.T
    piece = wrows // lemma_axis
    for group in range(group_axis):
        for owner in range(lemma_axis):
            start = group * wrows + owner * piece
            scaled_t[owner // 2, owner % 2, group] = scaled_rows[start : start + piece]

    own_gain = gain_ref[pl.ds(pl.multiple_of(grp * wrows, 128), wrows)].reshape(1, wrows)
    gain_col = jnp.broadcast_to(own_gain, (proj_width, wrows)).T
    over_gain[...] = (w_all[grp].astype(jnp.float32) / gain_col).reshape(over_gain.shape)

    wf_out = []
    for step in range(1, group_axis):
        dst = w_all.at[grp_from(step), my_half]
        remote(dst, dst, w_send.at[step], w_recv.at[step], me, grp_peer(step)).wait_recv()
        copy = remote(dst, dst, wf_send.at[step], wf_recv.at[step], pair, grp)
        copy.start()
        wf_out.append(copy)
    def forward(step):
        dst = keys.at[chip_source(step), core]
        remote(dst, dst, k_send.at[step], k_recv.at[step], chip_peer(step), grp).wait_recv()
        copy = remote(dst, dst, kf_send.at[step], kf_recv.at[step], pair, grp)
        copy.start()
        kf_out.append(copy)

    for step in range(1, chips):
        forward(step)
    other_half = pl.ds(pl.multiple_of((1 - core) * hrows, hrows), hrows)
    for step in range(1, group_axis):
        dst = w_all.at[grp_from(step), other_half]
        remote(dst, dst, wf_send.at[step], wf_recv.at[step], pair, grp).wait_recv()

    weight = w_all[...].reshape(width, proj_width)
    projected = jnp.dot(scaled_b[...], weight, preferred_element_type=jnp.float32)
    proj_scale = lax.rsqrt(
        jnp.mean(projected * projected, axis=1, keepdims=True) + norm_eps
    ) / math.sqrt(proj_width)
    query_unit = (projected * proj_scale).astype(jnp.bfloat16)

    def first_pass(block, total):
        scores = lax.dot_general(
            query_unit, keys[block].reshape(chip_tok, proj_width), NT, preferred_element_type=jnp.float32
        )
        exp_terms = jnp.exp(scores * (1.0 / token_temp)).astype(jnp.bfloat16)
        powers_b[block] = exp_terms
        return total + jnp.dot(exp_terms, live[block], preferred_element_type=jnp.float32)

    def chip_pass(step, total):
        source = chip_source(step)
        dst = keys.at[source, 1 - core]
        remote(dst, dst, kf_send.at[step], kf_recv.at[step], pair, grp).wait_recv()
        return first_pass(source, total)

    total = jnp.zeros((rows, lemmas_all), jnp.float32)
    for step in range(chips):
        total = chip_pass(step, total)

    tok_lse = token_temp * jnp.log(total)
    first_state = (me * group_axis + grp) * states_dev
    ratios = []
    losses = jnp.zeros((1, 128), jnp.float32)
    lane = lax.broadcasted_iota(jnp.int32, (1, 128), 1)
    for state in range(states_dev):
        length = qlen_ref[first_state + state]
        target = pos_ref[first_state + state]
        length_f = jnp.full((1, lemmas_all), length, jnp.int32).astype(jnp.float32)
        span = slice(state * query_tok, (state + 1) * query_tok)
        row_ids = lax.broadcasted_iota(jnp.int32, (query_tok, lemmas_all), 0)
        live_rows = jnp.where(row_ids < length, 1.0, 0.0)
        similarity = jnp.sum(tok_lse[span] * live_rows, axis=0, keepdims=True) / length_f
        powers = jnp.exp(similarity / state_temp)
        lemma_ids = lax.broadcasted_iota(jnp.int32, (1, lemmas_all), 1)
        is_positive = jnp.where(lemma_ids == target, 1.0, 0.0)
        partition = jnp.sum(powers, axis=1, keepdims=True)
        pos_score = jnp.sum(similarity * is_positive, axis=1, keepdims=True)
        loss = jnp.log(partition) - pos_score / state_temp
        losses = jnp.where(lane == state, loss, losses)
        grad_sim = loss_scale * (powers / partition - is_positive) / state_temp
        ratios.append(live_rows * (grad_sim / length_f) / total[span])
    loss_row[...] = losses
    loss_copy = pltpu.make_async_copy(loss_row, loss_ref, table_sem.at[4])
    loss_copy.start()
    ratio = jnp.concatenate(ratios, axis=0).astype(jnp.bfloat16)

    unit_grad = jnp.zeros((rows, proj_width), jnp.float32)
    for block in range(chips):
        spread = jnp.dot(ratio, live_t[block], preferred_element_type=jnp.float32)
        coef = (powers_b[block].astype(jnp.float32) * spread).astype(jnp.bfloat16)
        unit_grad += jnp.dot(
            coef, keys[block].reshape(chip_tok, proj_width), preferred_element_type=jnp.float32
        )
    proj_grad = proj_scale * unit_grad - projected * (
        proj_scale * proj_scale * proj_scale
    ) * jnp.sum(projected * unit_grad, axis=1, keepdims=True)
    proj_grad_b = proj_grad.astype(jnp.bfloat16)

    def weight_part(target, side):
        left = scaled_t[target, side].reshape(group_axis * piece, rows)
        return jnp.dot(left, proj_grad_b, preferred_element_type=jnp.float32).reshape(
            group_axis, piece, proj_width
        )

    order = list(reversed(range(chips)))
    p_out = []
    for step in order:
        part[step] = weight_part(chip_to(step), 1 - core).astype(jnp.bfloat16)
        copy = remote(part.at[step], pair_in.at[step], p_send.at[step], p_recv.at[step], pair, grp)
        copy.start()
        p_out.append(copy)
    grp_order = list(reversed(range(group_axis)))
    c_out = {}
    for step, pair_copy in zip(order, p_out):
        mine = weight_part(chip_to(step), core)
        pair_copy.wait_recv()
        half[step] = (mine + pair_in[step].astype(jnp.float32)).astype(jnp.bfloat16)
        if step:
            for grp_step in grp_order:
                copy = remote(
                    half.at[step, grp_peer(grp_step)], chip_in.at[step - 1, grp_step],
                    c_send.at[step - 1, grp_step], c_recv.at[step - 1, grp_step],
                    chip_peer(step), grp,
                )
                copy.start()
                c_out[step, grp_step] = copy

    row_dot = jnp.sum(projected * proj_grad_b.astype(jnp.float32), axis=1, keepdims=True)
    row_scale = inv_rms * inv_rms * row_dot / width

    def hidden_part(state):
        span = slice(state * query_tok, (state + 1) * query_tok)
        scaled_grad = lax.dot_general(
            proj_grad_b[span], w_all[...].reshape(width, proj_width), NT,
            preferred_element_type=jnp.float32,
        )
        hout[span] = (
            inv_rms[span] * (scaled_grad * gain_row)
            - hid[span].astype(jnp.float32) * row_scale[span]
        ).astype(jnp.bfloat16)
        copy = pltpu.make_async_copy(hout.at[span], hgrad_ref.at[span], local_sem.at[3 + state])
        copy.start()
        return copy

    hout_copies = [hidden_part(0)]

    g_out = []
    for grp_step in grp_order:
        chip_sum = half[0, grp_peer(grp_step)].astype(jnp.float32)
        for step in range(1, chips):
            c_out[step, grp_step].wait_recv()
            chip_sum += chip_in[step - 1, grp_step].astype(jnp.float32)
        if grp_step:
            quarter[grp_step] = chip_sum.astype(jnp.bfloat16)
            copy = remote(
                quarter.at[grp_step], grp_in.at[grp_step - 1],
                g_send.at[grp_step], g_recv.at[grp_step], me, grp_peer(grp_step),
            )
            copy.start()
            g_out.append(copy)
        else:
            grp_sum = chip_sum
    hout_copies += [hidden_part(state) for state in range(1, states_dev)]
    for copy in g_out:
        copy.wait_recv()
    for step in range(1, group_axis):
        grp_sum += grp_in[step - 1].astype(jnp.float32)
    own_raw = grp_sum.astype(jnp.bfloat16)
    raw[me] = own_raw
    own_raw = own_raw.astype(jnp.float32)
    own_gain_raw = jnp.sum(own_raw * over_gain[me], axis=1, keepdims=True)
    squares = jnp.sum(own_raw * own_raw) + jnp.sum(own_gain_raw * own_gain_raw)
    my_sq = sq.at[grp * lemma_axis + me]
    my_sq[...] = jnp.full((1, 128), squares, jnp.float32)
    for lemma_step, grp_step in reversed(others):
        copy = remote(
            my_sq, my_sq, s_send, s_recv,
            lax.rem(me + lemma_step, lemma_axis), grp_peer(grp_step),
        )
        copy.start()
    a_out = []
    for step in range(1, lemma_axis):
        copy = remote(
            raw.at[me], raw.at[me], a_send.at[step], a_recv.at[step],
            lax.rem(me + step, lemma_axis), grp,
        )
        copy.start()
        a_out.append(copy)
    for step in range(1, lemma_axis):
        dst = raw.at[lax.rem(me + lemma_axis - step, lemma_axis)]
        remote(dst, dst, a_send.at[step], a_recv.at[step], pair, grp).wait_recv()

    raw_copy = pltpu.make_async_copy(raw, raw_ref, table_sem.at[5])
    raw_copy.start()
    weight_raw = raw[...].reshape(wrows, proj_width).astype(jnp.float32)
    ones = jnp.ones((8, proj_width), jnp.float32)
    gain_raw = lax.dot_general(
        ones, over_gain[...].reshape(wrows, proj_width) * weight_raw, NT,
        preferred_element_type=jnp.float32, precision=lax.Precision.HIGHEST,
    )[:1]
    gain_out[...] = gain_raw
    gain_copy = pltpu.make_async_copy(gain_out, ggrad_ref, table_sem.at[6])
    gain_copy.start()
    all_but_one = sq.at[pl.ds(0, len(others))]
    remote(all_but_one, all_but_one, s_send, s_recv, pair, grp).wait()
    squares_all = jnp.sum(sq[...], axis=0)
    factor = jnp.minimum(1.0, grad_limit / jnp.sqrt(squares_all + norm_eps))
    factor_row[...] = factor
    factor_copy = pltpu.make_async_copy(factor_row, factor_ref, table_sem.at[7])
    factor_copy.start()

    for copy in w_out + k_out + wf_out + kf_out + p_out + list(c_out.values()) + g_out + a_out:
        copy.wait_send()
    for copy in hout_copies + [loss_copy, raw_copy, gain_copy, factor_copy]:
        copy.wait()


def place_kernel(
    loss, hgrad, raw, gain_raw, factor, loss_out, hgrad_out, wgrad_out, ggrad_out,
    loss_in, hbuf, raw_in, gain_in, factor_in, loss_row, wbuf, ggrad_row, sems,
):
    pairs = [(factor, factor_in), (raw, raw_in), (gain_raw, gain_in), (loss, loss_in), (hgrad, hbuf)]
    copies = [pltpu.make_async_copy(a, b, sems.at[i]) for i, (a, b) in enumerate(pairs)]
    for copy in copies:
        copy.start()
    pairs = [(wbuf, wgrad_out), (ggrad_row, ggrad_out), (loss_row, loss_out), (hbuf, hgrad_out)]
    backs = [pltpu.make_async_copy(a, b, sems.at[5 + i]) for i, (a, b) in enumerate(pairs)]
    copies[4].wait()
    backs[3].start()
    copies[0].wait()
    copies[1].wait()
    wbuf[...] = raw_in[...].reshape(wbuf.shape).astype(jnp.float32) * factor_in[...]
    backs[0].start()
    copies[2].wait()
    ggrad_row[...] = (gain_in[...] * factor_in[:, :1]).reshape(ggrad_row.shape)
    backs[1].start()
    copies[3].wait()
    loss_row[...] = loss_in[0, : loss_row.shape[0]]
    backs[2].start()
    for copy in backs:
        copy.wait()


def fused_body(hidden, gain, weight, lemma_emb, lemma_len, query_len, positive):
    states_dev, query_tok, width = hidden.shape
    wrows, proj_width = weight.shape
    lemma_dev, lemma_tok = lemma_emb.shape[:2]
    lemma_axis, group_axis = lax.axis_size("lemma"), lax.axis_size("grp")
    chips = lemma_axis // 2
    rows, block_tok = states_dev * query_tok, lemma_dev * lemma_tok
    piece = wrows // lemma_axis
    lemmas_all = lemma_dev * lemma_axis
    hbm = pl.BlockSpec(memory_space=pltpu.HBM)
    sem = pltpu.SemaphoreType.DMA
    bf16, f32 = jnp.bfloat16, jnp.float32
    outs = pl.pallas_call(
        functools.partial(
            fused_kernel, lemma_axis, group_axis, lemma_dev, lemma_tok, states_dev, query_tok
        ),
        out_shape=(
            jax.ShapeDtypeStruct((1, 128), f32),
            jax.ShapeDtypeStruct((rows, width), bf16),
            jax.ShapeDtypeStruct((lemma_axis, piece, proj_width), bf16),
            jax.ShapeDtypeStruct((1, wrows), f32),
            jax.ShapeDtypeStruct((1, 128), f32),
        ),
        in_specs=[hbm] * 7,
        out_specs=(hbm,) * 5,
        scratch_shapes=[
            pltpu.VMEM((width,), f32),
            pltpu.VMEM((lemmas_all,), jnp.int32),
            pltpu.SMEM(query_len.shape, jnp.int32),
            pltpu.SMEM(positive.shape, jnp.int32),
            pltpu.VMEM((1, 128), f32),
            pltpu.VMEM((1, wrows), f32),
            pltpu.VMEM((1, 128), f32),
            pltpu.VMEM((rows, width), bf16),
            pltpu.VMEM((block_tok, proj_width), bf16),
            pltpu.VMEM((rows, width), bf16),
            pltpu.VMEM((group_axis, wrows, proj_width), bf16),
            pltpu.VMEM((chips, 2, block_tok, proj_width), bf16),
            pltpu.VMEM((chips, 2 * block_tok, lemmas_all), bf16),
            pltpu.VMEM((chips, lemmas_all, 2 * block_tok), bf16),
            pltpu.VMEM((chips, rows, 2 * block_tok), bf16),
            pltpu.VMEM((rows, width), bf16),
            pltpu.VMEM((chips, 2, group_axis, piece, rows), bf16),
            pltpu.VMEM((chips, group_axis, piece, proj_width), bf16),
            pltpu.VMEM((chips, group_axis, piece, proj_width), bf16),
            pltpu.VMEM((chips, group_axis, piece, proj_width), bf16),
            pltpu.VMEM((chips - 1, group_axis, piece, proj_width), bf16),
            pltpu.VMEM((group_axis, piece, proj_width), bf16),
            pltpu.VMEM((group_axis - 1, piece, proj_width), bf16),
            pltpu.VMEM((lemma_axis, piece, proj_width), bf16),
            pltpu.VMEM((group_axis * lemma_axis, 1, 128), f32),
            pltpu.VMEM((lemma_axis, piece, proj_width), f32),
            sem((3 + states_dev,)), sem((8,)),
            sem((group_axis,)), sem((group_axis,)), sem((group_axis,)), sem((group_axis,)),
            sem((chips,)), sem((chips,)), sem((chips,)), sem((chips,)),
            sem((chips,)), sem((chips,)),
            sem((chips - 1, group_axis)), sem((chips - 1, group_axis)),
            sem((group_axis,)), sem((group_axis,)),
            sem((lemma_axis,)), sem((lemma_axis,)),
            sem, sem,
        ],
        compiler_params=pltpu.CompilerParams(
            collective_id=0, has_side_effects=True, vmem_limit_bytes=62 * 1024 * 1024
        ),
        cost_estimate=pl.CostEstimate(
            flops=2 * rows * proj_width * (3 * width + 4 * block_tok * lemma_axis),
            bytes_accessed=4 * rows * width * 2,
            transcendentals=rows * block_tok * lemma_axis,
        ),
    )(
        hidden.reshape(rows, width), gain, weight,
        lemma_emb.reshape(block_tok, proj_width), lemma_len,
        query_len, positive,
    )
    loss, hidden_grad, weight_grad, gain_grad = pl.pallas_call(
        place_kernel,
        out_shape=(
            jax.ShapeDtypeStruct((states_dev,), f32),
            jax.ShapeDtypeStruct((rows, width), bf16),
            jax.ShapeDtypeStruct((wrows, proj_width), f32),
            jax.ShapeDtypeStruct((wrows,), f32),
        ),
        in_specs=[hbm] * 5,
        out_specs=(hbm,) * 4,
        scratch_shapes=[
            pltpu.VMEM((1, 128), f32),
            pltpu.VMEM((rows, width), bf16),
            pltpu.VMEM((lemma_axis, piece, proj_width), bf16),
            pltpu.VMEM((1, wrows), f32),
            pltpu.VMEM((1, 128), f32),
            pltpu.VMEM((states_dev,), f32),
            pltpu.VMEM((wrows, proj_width), f32),
            pltpu.VMEM((wrows,), f32),
            sem((9,)),
        ],
        compiler_params=pltpu.CompilerParams(vmem_limit_bytes=62 * 1024 * 1024),
    )(*outs)
    return (loss, hidden_grad.reshape(hidden.shape), weight_grad, gain_grad)


def solution(mesh):
    in_specs = (
        P(("lemma", "grp"), None, None),
        P(),
        P("grp", None),
        P("lemma", None, None),
        P(),
        P(),
        P(),
    )
    out_specs = (P(("lemma", "grp")), P(("lemma", "grp"), None, None), P("grp", None), P("grp"))

    def run(hidden, gain, weight, *rest):
        rows = weight.shape[0] // mesh.shape["grp"]
        tiled = rows % (16 * mesh.shape["lemma"]) == 0 and rows % 128 == 0
        chosen = fused_body if tiled else body
        return jax.shard_map(
            chosen, mesh=mesh, in_specs=in_specs, out_specs=out_specs, check_vma=False
        )(hidden, gain, weight, *rest)

    return run
```
